256 devices in a mesh: patch: 64 (over x, z_lo, y, core), dp: 4 (over z_hi).
Axes of the slice: x: 4, y: 4, z: 8 (z_hi: 4, z_lo: 2; z = z_hi * 2 + z_lo), core: 2. Of those that a mesh axis runs over, the one named last changes fastest.
Arguments:
- coarse_state: float32 [4, 5, 3072, 256], P('dp', None, 'patch'), may hold values from -6 to 6
- fine_state: float32 [4, 5, 1024, 1024], P('dp', None, 'patch'), may hold values from -6 to 6
- coarse_cot: float32 [4, 5, 3072, 256], P('dp', None, 'patch'), may hold values from -6 to 6
- fine_cot: float32 [4, 5, 1024, 1024], P('dp', None, 'patch'), may hold values from -6 to 6
- coarse_diffusion: float32 [5], replicated, may hold values from 0.02 to 0.07
- w_in: bfloat16 [128, 135], replicated, may hold values from -0.5 to 0.5
- b_in: float32 [128], replicated, may hold values from -3 to 3
- w_mid: bfloat16 [128, 128], replicated, may hold values from -0.5 to 0.5
- b_mid: float32 [128], replicated, may hold values from -3 to 3
- w_out: bfloat16 [5, 128], replicated, may hold values from -0.5 to 0.5
- b_out: float32 [5], replicated, may hold values from -2 to 2
- coarse_counts: int32 [64], replicated, may hold values from 1 to 3, 128 in all
- fine_counts: int32 [64], replicated, may hold values from 1 to 2, 96 in all
- fine_anchor: int32 [1], replicated, may hold values from 0 to 2047
Outputs:
- coarse_out: float32 [4, 5, 3072, 256], P('dp', None, 'patch')
- fine_out: float32 [4, 5, 1024, 1024], P('dp', None, 'patch')
- coarse_adj: float32 [4, 5, 3072, 256], P('dp', None, 'patch')
- fine_adj: float32 [4, 5, 1024, 1024], P('dp', None, 'patch')
- grad_w_in: float32 [128, 135], replicated
- grad_b_in: float32 [128], replicated
- grad_w_mid: float32 [128, 128], replicated
- grad_b_mid: float32 [128], replicated
- grad_w_out: float32 [5, 128], replicated
- grad_b_out: float32 [5], replicated
The draws below stay inside these ranges and needn't reach their ends.
Inputs may be any that keep to these rules, and one draw needn't show every extreme that they name: Device d of patch holds the coarse patches that follow those of devices 0 to d - 1 along the chain, in its first coarse_counts[d] slots; the counts sum to 128. Device d of patch holds the fine patches that follow those of devices 0 to d - 1 along the fine chain, in its first fine_counts[d] slots; the counts sum to 96. `fine_anchor`: the fine level covers 384 consecutive coarse rows from here, wrapping around the periodic chain.
All inputs are finite; a program needn't handle non-finite values.
Results may differ from the reference program's by a relative error of at most 0.0058.
Values sent between devices are 32-bit elements; how exact they have to be, the bound alone decides.
A program may use at most 128 MiB of HBM per device.

```python
import math
import jax
import jax.numpy as jnp
import numpy as np
from jax import lax

S = 16
C = 16
F = 5
HID = 128
CCAP = 3
FCAP = 2
SUB = 2
FEAT = 135
SF = 8
ZB = 4
CROWS = 48
FROWS = 16
SAMPLES = 4
NCOARSE = 128
NFINE = 96
NZC = 2048
NZF = 768
REGION = 384
FINE_CELLS = 786432
N_PATCH = 64


def level_of(own_key, extent, shards, least, top_value):
    def one(dim, blocks):
        steps = jax.random.uniform(jax.random.fold_in(jax.random.fold_in(own_key, 6), dim), (blocks,), jnp.float32, least / len(shards), top_value / len(shards))
        return jnp.repeat(jnp.exp(steps), extent[dim] // blocks).reshape((-1,) + (1,) * (len(extent) - dim - 1))

    loudness = one(*shards[0])
    for cut in shards[1:]:
        loudness = loudness * one(*cut)
    return loudness


def split_up(count, total, bound, lean):
    weights = [(1 << 20) // math.isqrt(grade ** lean) + 1 for grade in range(2, count + 1)]
    surplus, holding = total - bound - (count - 1), [1] * (count - 1)
    while surplus > 0:
        candidates = [i for i in range(count - 1) if holding[i] < bound]
        whole, left = sum([weights[i] for i in candidates]), surplus
        for i in candidates:
            addition = min(bound - holding[i], max(1, left * weights[i] // whole), surplus)
            holding[i] = holding[i] + addition
            surplus = surplus - addition
    return np.array([bound] + holding)


def uneven_parts(stream_key, number_of, total, reach, slope):
    if number_of == 2:
        one = jax.random.randint(stream_key, (), max(1, total - reach), min(reach, total - 1) + 1)
        return jnp.stack([one, total - one])
    lengths = jnp.asarray(split_up(number_of, total, reach, slope), jnp.int32)
    pairs = (number_of - 1) // 2
    giver, taker = lengths[1:1 + 2 * pairs:2], lengths[2:2 + 2 * pairs:2]
    slack = jnp.minimum(giver - 1, reach - taker)
    passed = jax.random.randint(jax.random.fold_in(stream_key, 1), (pairs,), 0, 1 << 20) % (slack + 1)
    lengths = lengths.at[1:1 + 2 * pairs:2].set(giver - passed).at[2:2 + 2 * pairs:2].set(taker + passed)
    return lengths[jax.random.permutation(jax.random.fold_in(stream_key, 2), number_of)]


def noise(stream_key, shape, deviation, limit, split=(), kind=jnp.bfloat16):
    loudness = level_of(stream_key, shape, split, -0.22, 0.18) if split else 1.0
    drawn = jax.random.normal(stream_key, shape, jnp.float32) * deviation * loudness
    return jnp.minimum(jnp.maximum(drawn, -limit), limit).astype(kind)


def setup_inputs(seed: int = 0) -> dict:
    key_of = jax.random.split(jax.random.key(seed), 15)
    coarse_state = noise(key_of[0], (SAMPLES, F, N_PATCH * CROWS, C * C), 1.0, 6.0, ((0, 4), (2, 64)), jnp.float32)
    fine_state = noise(key_of[1], (SAMPLES, F, N_PATCH * FROWS, 4 * C * C), 1.0, 6.0, ((0, 4), (2, 64)), jnp.float32)
    coarse_cot = noise(key_of[2], (SAMPLES, F, N_PATCH * CROWS, C * C), 1.0, 6.0, ((0, 4), (2, 64)), jnp.float32)
    fine_cot = noise(key_of[3], (SAMPLES, F, N_PATCH * FROWS, 4 * C * C), 1.0, 6.0, ((0, 4), (2, 64)), jnp.float32)
    coarse_diffusion = jnp.clip(jnp.exp(jax.random.uniform(key_of[4], (F,), jnp.float32, math.log(0.02), math.log(0.07))), 0.02, 0.07)
    w_in = noise(key_of[5], (HID, FEAT), FEAT ** -0.5, 0.5)
    b_in = noise(key_of[6], (HID,), 0.5, 3.0, (), jnp.float32)
    w_mid = noise(key_of[7], (HID, HID), HID ** -0.5, 0.5)
    b_mid = noise(key_of[8], (HID,), 0.5, 3.0, (), jnp.float32)
    w_out = noise(key_of[9], (F, HID), HID ** -0.5, 0.5)
    b_out = noise(key_of[10], (F,), 0.3, 2.0, (), jnp.float32)
    coarse_counts = uneven_parts(key_of[11], N_PATCH, NCOARSE, CCAP, 2).astype(jnp.int32)
    fine_counts = uneven_parts(key_of[12], N_PATCH, NFINE, FCAP, 2).astype(jnp.int32)
    fine_anchor = jax.random.randint(key_of[13], (1,), 0, NZC).astype(jnp.int32)
    return {"coarse_state": coarse_state, "fine_state": fine_state, "coarse_cot": coarse_cot, "fine_cot": fine_cot, "coarse_diffusion": coarse_diffusion, "w_in": w_in, "b_in": b_in, "w_mid": w_mid, "b_mid": b_mid, "w_out": w_out, "b_out": b_out, "coarse_counts": coarse_counts, "fine_counts": fine_counts, "fine_anchor": fine_anchor}


HIGH_PRECISION = lax.Precision.HIGHEST
DT_SOURCE = 0.5

def shift_rows(values, plane_width, offset_y):
    if offset_y == 0:
        return values
    return jnp.roll(values, -offset_y * plane_width, axis=-1)

def shift_columns(values, plane_width, offset_x):
    if offset_x == 0:
        return values
    column = jnp.arange(values.shape[-1], dtype=jnp.int32) % plane_width
    if offset_x == 1:
        return jnp.where(column == plane_width - 1, jnp.roll(values, plane_width - 1, axis=-1), jnp.roll(values, -1, axis=-1))
    return jnp.where(column == 0, jnp.roll(values, 1 - plane_width, axis=-1), jnp.roll(values, 1, axis=-1))

def plane_neighbours(values, plane_width):
    return shift_rows(values, plane_width, -1) + shift_rows(values, plane_width, 1) + shift_columns(values, plane_width, -1) + shift_columns(values, plane_width, 1)

def pooling_table(coarse_width):
    fine_index = jnp.arange(4 * coarse_width * coarse_width, dtype=jnp.int32)
    fine_row = fine_index // (2 * coarse_width)
    fine_column = fine_index % (2 * coarse_width)
    target = fine_row // 2 * coarse_width + fine_column // 2
    return (target[:, None] == jnp.arange(coarse_width * coarse_width, dtype=jnp.int32)[None, :]).astype(jnp.float32)

def block_features(row_slab, plane_width):
    inner_rows = row_slab.shape[1] - 2
    pieces = []
    for step_z in range(3):
        layer_rows = row_slab[:, step_z:step_z + inner_rows]
        for step_y in (-1, 0, 1):
            moved_rows = shift_rows(layer_rows, plane_width, step_y)
            for step_x in (-1, 0, 1):
                pieces.append(shift_columns(moved_rows, plane_width, step_x))
    stacked = jnp.concatenate(pieces, axis=0)
    return stacked.reshape(stacked.shape[0], inner_rows * row_slab.shape[2])

def spread_features(grad_features, fields, inner_rows, plane_width):
    grad_parts = grad_features.reshape(27, fields, inner_rows, grad_features.shape[1] // inner_rows)
    layers_out = []
    position = 0
    for step_z in range(3):
        layer_total = None
        for step_y in (-1, 0, 1):
            row_total = None
            for step_x in (-1, 0, 1):
                term_x = shift_columns(grad_parts[position], plane_width, -step_x)
                position += 1
                row_total = term_x if row_total is None else row_total + term_x
            term_y = shift_rows(row_total, plane_width, -step_y)
            layer_total = term_y if layer_total is None else layer_total + term_y
        layers_out.append(layer_total)
    return jnp.pad(layers_out[0], ((0, 0), (0, 2), (0, 0))) + jnp.pad(layers_out[1], ((0, 0), (1, 1), (0, 0))) + jnp.pad(layers_out[2], ((0, 0), (2, 0), (0, 0)))

def closure_forward(features, params):
    w_in, b_in, w_mid, b_mid, w_out, b_out = params
    pre_one = jnp.dot(w_in, features, preferred_element_type=jnp.float32) + b_in[:, None]
    act_one = jax.nn.silu(pre_one).astype(jnp.bfloat16)
    pre_two = jnp.dot(w_mid, act_one, preferred_element_type=jnp.float32) + b_mid[:, None]
    act_two = jax.nn.silu(pre_two).astype(jnp.bfloat16)
    source = jnp.dot(w_out, act_two, preferred_element_type=jnp.float32) + b_out[:, None]
    return (source, (pre_one, act_one, pre_two, act_two))

def silu_slope(values):
    logistic = jax.nn.sigmoid(values)
    return logistic * (1.0 + values * (1.0 - logistic))

def closure_backward(features, saved, source_grad, params):
    w_in, b_in, w_mid, b_mid, w_out, b_out = params
    pre_one, act_one, pre_two, act_two = saved
    by_cells = (((1,), (1,)), ((), ()))
    by_units = (((0,), (0,)), ((), ()))
    source_bf = source_grad.astype(jnp.bfloat16)
    grad_w_out = lax.dot_general(source_bf, act_two, by_cells, preferred_element_type=jnp.float32)
    grad_b_out = lax.optimization_barrier(jnp.sum(source_grad, axis=1))
    delta_two = lax.dot_general(w_out, source_bf, by_units, preferred_element_type=jnp.float32) * silu_slope(pre_two)
    delta_two_bf = delta_two.astype(jnp.bfloat16)
    grad_w_mid = lax.dot_general(delta_two_bf, act_one, by_cells, preferred_element_type=jnp.float32)
    grad_b_mid = lax.optimization_barrier(jnp.sum(delta_two, axis=1))
    delta_one = lax.dot_general(w_mid, delta_two_bf, by_units, preferred_element_type=jnp.float32) * silu_slope(pre_one)
    delta_one_bf = delta_one.astype(jnp.bfloat16)
    grad_w_in = lax.dot_general(delta_one_bf, features, by_cells, preferred_element_type=jnp.float32)
    grad_b_in = lax.optimization_barrier(jnp.sum(delta_one, axis=1))
    grad_features = lax.dot_general(w_in, delta_one_bf, by_units, preferred_element_type=jnp.float32)
    return ((grad_w_in, grad_b_in, grad_w_mid, grad_b_mid, grad_w_out, grad_b_out), grad_features)

def closure_sources(padded_bf, block_rows, params, plane_width):
    fields = padded_bf.shape[0]
    inner_rows = padded_bf.shape[1] - 2
    blocks = inner_rows // block_rows

    def one_block(carried, block_index):
        row_slab = lax.dynamic_slice_in_dim(padded_bf, block_index * block_rows, block_rows + 2, axis=1)
        source, unused_saved = closure_forward(block_features(row_slab, plane_width), params)
        return (carried, source)
    unused_carry, sources = lax.scan(one_block, jnp.zeros((), jnp.float32), jnp.arange(blocks, dtype=jnp.int32))
    sources = sources.reshape(blocks, fields, block_rows, padded_bf.shape[2])
    return jnp.moveaxis(sources, 0, 1).reshape(fields, inner_rows, padded_bf.shape[2])

def closure_adjoint(padded_bf, grad_field, totals, params, plane_width, block_rows):
    fields = grad_field.shape[0]
    inner_rows = grad_field.shape[1]
    blocks = inner_rows // block_rows

    def one_block(carried, block_index):
        grad_sums, spread = carried
        first_row = block_index * block_rows
        row_slab = lax.dynamic_slice_in_dim(padded_bf, first_row, block_rows + 2, axis=1)
        grad_rows = lax.dynamic_slice_in_dim(grad_field, first_row, block_rows, axis=1)
        features = block_features(row_slab, plane_width)
        unused_source, saved = closure_forward(features, params)
        grads, grad_features = closure_backward(features, saved, DT_SOURCE * grad_rows.reshape(fields, -1), params)
        grad_sums = tuple((before + added for before, added in zip(grad_sums, grads)))
        window = lax.dynamic_slice_in_dim(spread, first_row, block_rows + 2, axis=1)
        window = window + spread_features(grad_features, fields, block_rows, plane_width)
        spread = lax.dynamic_update_slice_in_dim(spread, window, first_row, axis=1)
        return ((grad_sums, spread), None)
    initial = (totals, jnp.zeros((fields, inner_rows + 2, grad_field.shape[2]), jnp.float32))
    (totals, spread), unused_out = lax.scan(one_block, initial, jnp.arange(blocks, dtype=jnp.int32))
    return (totals, spread)

def diffusion_adjoint(spread, grad_field, kappa_fine, plane_width):
    side_term = kappa_fine * grad_field
    centre = grad_field + kappa_fine * (plane_neighbours(grad_field, plane_width) - 6.0 * grad_field)
    return spread + jnp.pad(side_term, ((0, 0), (0, 2), (0, 0))) + jnp.pad(centre, ((0, 0), (1, 1), (0, 0))) + jnp.pad(side_term, ((0, 0), (2, 0), (0, 0)))

def periodic_update(values, kappa_coarse, plane_width):
    wrapped = jnp.concatenate([values[:, -1:], values, values[:, :1]], axis=1)
    return values + kappa_coarse * (wrapped[:, :-2] + wrapped[:, 2:] + plane_neighbours(values, plane_width) - 6.0 * values)

def chain_slots(counts, patch_rows, slot_rows, length):
    starts = jnp.cumsum(counts) - counts
    chain_index = jnp.arange(length, dtype=jnp.int32)
    patch_number = chain_index // patch_rows
    owner_device = lax.optimization_barrier(jnp.sum((starts[None, :] <= patch_number[:, None]).astype(jnp.int32), axis=1)) - 1
    return (owner_device * slot_rows + (patch_number - starts[owner_device]) * patch_rows + chain_index % patch_rows).astype(jnp.int32)

def reference(coarse_state, fine_state, coarse_cot, fine_cot, coarse_diffusion, w_in, b_in, w_mid, b_mid, w_out, b_out, coarse_counts, fine_counts, fine_anchor):
    params = (w_in, b_in, w_mid, b_mid, w_out, b_out)
    coarse_slots = chain_slots(coarse_counts, S, CROWS, NZC)
    fine_slots = chain_slots(fine_counts, SF, FROWS, NZF)
    pool = pooling_table(C)
    kappa_coarse = coarse_diffusion[:, None, None]
    kappa_fine = 2.0 * kappa_coarse
    anchor = fine_anchor[0]
    region_rows = ((anchor + jnp.arange(REGION, dtype=jnp.int32)) % NZC).astype(jnp.int32)
    low_row = (anchor + NZC - 1) % NZC
    high_row = (anchor + REGION) % NZC
    totals = (jnp.zeros((HID, FEAT), jnp.float32), jnp.zeros((HID,), jnp.float32), jnp.zeros((HID, HID), jnp.float32), jnp.zeros((HID,), jnp.float32), jnp.zeros((F, HID), jnp.float32), jnp.zeros((F,), jnp.float32))
    coarse_results, fine_results, coarse_grads, fine_grads = ([], [], [], [])
    for sample in range(SAMPLES):
        coarse_chain = jnp.take(coarse_state[sample], coarse_slots, axis=1)
        fine_chain = jnp.take(fine_state[sample], fine_slots, axis=1)
        lower_rim = jnp.dot(jnp.take(coarse_chain, low_row, axis=1), pool.T, precision=HIGH_PRECISION)
        upper_rim = jnp.dot(jnp.take(coarse_chain, high_row, axis=1), pool.T, precision=HIGH_PRECISION)
        updated = periodic_update(coarse_chain, kappa_coarse, C)
        segments = []
        for cycle in range(SUB):
            padded = jnp.concatenate([lower_rim[:, None], fine_chain, upper_rim[:, None]], axis=1)
            padded_bf = padded.astype(jnp.bfloat16)
            segments.append(padded_bf)
            laplace = padded[:, :-2] + padded[:, 2:] + plane_neighbours(fine_chain, 2 * C) - 6.0 * fine_chain
            fine_chain = fine_chain + kappa_fine * laplace + DT_SOURCE * closure_sources(padded_bf, ZB, params, 2 * C)
        pairs = fine_chain.reshape(F, REGION, 2, 4 * C * C).sum(axis=2)
        restricted = jnp.dot(pairs, pool, precision=HIGH_PRECISION) * 0.125
        coarse_new = updated.at[:, region_rows].set(restricted)
        coarse_grad = jnp.take(coarse_cot[sample], coarse_slots, axis=1)
        fine_grad = jnp.take(fine_cot[sample], fine_slots, axis=1)
        region_grad = jnp.take(coarse_grad, region_rows, axis=1)
        kept = coarse_grad.at[:, region_rows].set(0.0)
        coarse_back = periodic_update(kept, kappa_coarse, C)
        fine_back = fine_grad + jnp.repeat(jnp.dot(region_grad, pool.T, precision=HIGH_PRECISION), 2, axis=1) * 0.125
        rim_low = jnp.zeros((F, C * C), jnp.float32)
        rim_high = jnp.zeros((F, C * C), jnp.float32)
        for cycle in reversed(range(SUB)):
            totals, spread = closure_adjoint(segments[cycle], fine_back, totals, params, 2 * C, ZB)
            spread = diffusion_adjoint(spread, fine_back, kappa_fine, 2 * C)
            rim_low = rim_low + jnp.dot(spread[:, 0], pool, precision=HIGH_PRECISION)
            rim_high = rim_high + jnp.dot(spread[:, -1], pool, precision=HIGH_PRECISION)
            fine_back = spread[:, 1:-1]
        coarse_back = coarse_back.at[:, low_row].add(rim_low)
        coarse_back = coarse_back.at[:, high_row].add(rim_high)
        coarse_empty = jnp.zeros((F, N_PATCH * CROWS, C * C), jnp.float32)
        fine_empty = jnp.zeros((F, N_PATCH * FROWS, 4 * C * C), jnp.float32)
        coarse_results.append(coarse_empty.at[:, coarse_slots].set(coarse_new))
        fine_results.append(fine_empty.at[:, fine_slots].set(fine_chain))
        coarse_grads.append(coarse_empty.at[:, coarse_slots].set(coarse_back))
        fine_grads.append(fine_empty.at[:, fine_slots].set(fine_back))
    scale = 1.0 / math.sqrt(SAMPLES * FINE_CELLS)
    grad_w_in, grad_b_in, grad_w_mid, grad_b_mid, grad_w_out, grad_b_out = tuple((total * scale for total in totals))
    return (jnp.stack(coarse_results), jnp.stack(fine_results), jnp.stack(coarse_grads), jnp.stack(fine_grads), grad_w_in, grad_b_in, grad_w_mid, grad_b_mid, grad_w_out, grad_b_out)
```

```python
import math

import jax
import jax.numpy as jnp
from jax import lax
from jax.experimental import pallas as pl
from jax.experimental.pallas import tpu as pltpu
from jax.sharding import PartitionSpec as P

MESH = pl.DeviceIdType.MESH
F32 = jnp.float32
BF16 = jnp.bfloat16

DEV = 64
CHIPS = 32
CW = 16
FW = 32
CL = CW * CW
FL = FW * FW
CR = 48
FR = 16
NF = 5
CHAIN = 2048
REGION = 384
HALO = 4
EXT = FR + 2 * HALO
FB_ROWS = 80
HID = 128
HB = 144
GROUP = 16
PL = 640
GA_ROWS = 56
CHUNK = 256


def dot(a, b):
    return jnp.dot(a, b, preferred_element_type=F32)


def dot_nt(a, b):
    return lax.dot_general(a, b, (((1,), (1,)), ((), ())), preferred_element_type=F32)


def split(x):
    hi = x.astype(BF16)
    return hi, (x - hi.astype(F32)).astype(BF16)


def shift_x(v, step, width):
    lanes = v.shape[1]
    col = lax.broadcasted_iota(jnp.int32, (v.shape[0], 128), 1) % width
    parts = []
    for i in range(lanes // 128):
        s = v[:, 128 * i : 128 * (i + 1)]
        if step == 1:
            parts.append(
                jnp.where(
                    col == width - 1, pltpu.roll(s, width - 1, 1), pltpu.roll(s, 127, 1)
                )
            )
        else:
            parts.append(
                jnp.where(col == 0, pltpu.roll(s, 129 - width, 1), pltpu.roll(s, 1, 1))
            )
    return jnp.concatenate(parts, axis=1)


def shift_y(v, step, width):
    lanes = v.shape[1]
    return pltpu.roll(v, lanes - width if step == 1 else width, 1)


def neighbours(v, width):
    return (
        shift_y(v, -1, width)
        + shift_y(v, 1, width)
        + shift_x(v, -1, width)
        + shift_x(v, 1, width)
    )


def kernel(
    fc_smem,
    cc_smem,
    anchor_smem,
    fcv,
    cst,
    fst,
    cct,
    fct,
    kf_ref,
    kc_ref,
    w1,
    w2,
    w3,
    w1t,
    w2t,
    w3t,
    pool,
    pool_t,
    coarse_out,
    fine_out,
    coarse_adj,
    fine_adj,
    p_out,
    base_s,
    v0,
    v1,
    v2,
    nb0,
    nb1,
    s0,
    s1,
    a1,
    a2,
    sl1,
    d1,
    d2,
    sbv,
    g2,
    g1,
    araw,
    gout,
    rim,
    p1,
    p2,
    p3,
    gsum,
    sendb,
    pairb,
    recvb,
    gab,
    hs_dn,
    hs_up,
    hr_lo,
    hr_hi,
    cs_dn,
    cs_up,
    cr_lo,
    cr_hi,
    upd,
    back,
    rim_src,
    rim_got,
    rim_row_ref,
    rs,
    gath,
    rgs,
    rg,
    pk,
    r1,
    r1sum,
    r2,
    pall,
    sem_pair,
    sem_ga,
    sem_halo,
    sem_rim_s,
    sem_rim_r,
    sem_rs,
    sem_gp,
    sem_rg_s,
    sem_rg_r,
    sem_r1s,
    sem_r1r,
    sem_r2s,
    sem_r2r,
    sem_r3s,
    sem_r3r,
):
    me = lax.axis_index("patch")
    dp = lax.axis_index("dp")
    core = lax.rem(me, 2)
    chip = me // 2
    partner = chip * 2 + (1 - core)
    nxt = lax.rem(me + 1, DEV)
    prv = lax.rem(me + DEV - 1, DEV)
    xg = me // GROUP
    w = lax.rem(me, GROUP)
    slot2 = xg * 4 + dp

    barrier = pltpu.get_barrier_semaphore()

    def greet(t, c):
        pl.semaphore_signal(
            barrier, inc=1, device_id={"patch": lax.rem(me + t, DEV)}, device_id_type=MESH
        )
        return c

    lax.fori_loop(1, DEV, greet, 0)

    def greet_dp(t, c):
        pl.semaphore_signal(
            barrier,
            inc=1,
            device_id={
                "patch": (t // 3) * GROUP + w,
                "dp": lax.rem(dp + 1 + lax.rem(t, 3), 4),
            },
            device_id_type=MESH,
        )
        return c

    lax.fori_loop(0, 12, greet_dp, 0)

    anchor = anchor_smem[0]

    def count(d, carry):
        fs, cs = carry
        base_s[d] = fs
        fs = fs + fc_smem[d]
        cs = cs + jnp.where(d < me, cc_smem[d], 0)
        return (fs, cs)

    _, cpatch = lax.fori_loop(0, DEV, count, (jnp.int32(0), jnp.int32(0)))
    cstart = cpatch * CW
    nc = cc_smem[me] * CW
    n = fc_smem[me] * 8
    wide = n == FR
    first = me == 0
    last = me == DEV - 1

    def wrap(x):
        return lax.rem(x + 2 * CHAIN + CHAIN // 2, CHAIN) - CHAIN // 2

    def live_or_none(local):
        return jnp.where((local >= 0) & (local < nc), local, -10000)

    low_local = live_or_none(wrap(anchor - 1 - cstart))
    high_local = live_or_none(wrap(anchor + REGION - cstart))

    row48 = lax.broadcasted_iota(jnp.int32, (CR, CL), 0)
    live48 = row48 < nc
    off48 = lax.rem(row48 + (cstart - anchor + 2 * CHAIN), CHAIN)
    in_region = (off48 < REGION) & live48

    for f in range(NF):
        hs_dn[f, 0:4, :] = fst[f, 0:4, :]
        hs_dn[f, 4:8, :] = fct[f, 0:4, :]
        hs_up[f, 0:4, :] = jnp.where(wide, fst[f, 12:16, :], fst[f, 4:8, :])
        hs_up[f, 4:8, :] = jnp.where(wide, fct[f, 12:16, :], fct[f, 4:8, :])
    cs_dn[...] = jnp.zeros_like(cs_dn)
    cs_up[...] = jnp.zeros_like(cs_up)
    for f in range(NF):
        kept = jnp.where(in_region, 0.0, cct[f])
        cs_dn[f : f + 1, :] = cst[f, 0:1, :]
        cs_dn[8 + f : 9 + f, :] = kept[0:1]
        cs_up[f : f + 1, :] = jnp.where(
            nc == 48,
            cst[f, 47:48, :],
            jnp.where(nc == 32, cst[f, 31:32, :], cst[f, 15:16, :]),
        )
        cs_up[8 + f : 9 + f, :] = jnp.where(
            nc == 48, kept[47:48], jnp.where(nc == 32, kept[31:32], kept[15:16])
        )

    def neighbour_copies():
        def one(src, dst, k, dev):
            return pltpu.make_async_remote_copy(
                src_ref=src,
                dst_ref=dst,
                send_sem=sem_halo.at[0, k],
                recv_sem=sem_halo.at[1, k],
                device_id={"patch": dev},
                device_id_type=MESH,
            )

        return (
            one(hs_up, hr_lo, 0, nxt),
            one(hs_dn, hr_hi, 1, prv),
            one(cs_up, cr_lo, 2, nxt),
            one(cs_dn, cr_hi, 3, prv),
        )

    cot = jnp.concatenate([jnp.where(live48, cct[f], 0.0) for f in range(NF)], axis=0)
    cot_hi, cot_lo = split(cot)
    cot2 = jnp.concatenate([cot_hi, cot_lo], axis=1)
    srow = lax.broadcasted_iota(jnp.int32, (GA_ROWS, NF * CR), 0)
    scol = lax.broadcasted_iota(jnp.int32, (GA_ROWS, NF * CR), 1)
    pick = jnp.where(
        (scol // CR == srow % NF) & (srow < 50), scol % CR - srow // NF, 99999
    )

    def rows_for(c2):
        def one(k, c):
            base = wrap(anchor + 4 * base_s[2 * k + c2] - 1 - cstart)
            onehot = (pick == base).astype(F32).astype(BF16)
            both = dot(onehot, cot2)
            sendb[c2, k] = both[:, :CL] + both[:, CL:]
            return c

        lax.fori_loop(0, CHIPS, one, 0)

    rows_for(1 - core)
    rows_for(core)
    ust = jnp.concatenate([cst[f] for f in range(NF)], axis=0)
    ust_hi, ust_lo = split(ust)
    ust2 = jnp.concatenate([ust_hi, ust_lo], axis=1)
    frow = lax.broadcasted_iota(jnp.int32, (16, NF * CR), 0)
    fcol = lax.broadcasted_iota(jnp.int32, (16, NF * CR), 1)
    fpick = jnp.where(fcol // CR == frow, fcol % CR, 99999)
    for e, local in ((0, low_local), (1, high_local)):
        both = dot((fpick == local).astype(F32).astype(BF16), ust2)
        rim_src[e] = (both[:, :CL] + both[:, CL:])[0:8]

    pl.semaphore_wait(barrier, DEV - 1 + 12)

    halo_copies = neighbour_copies()
    for copy in halo_copies:
        copy.start()
    pair_copy = pltpu.make_async_remote_copy(
        src_ref=sendb.at[1 - core],
        dst_ref=pairb,
        send_sem=sem_pair.at[0],
        recv_sem=sem_pair.at[1],
        device_id={"patch": partner},
        device_id_type=MESH,
    )
    pair_copy.start()

    def rim_copy(e, sender):
        return pltpu.make_async_remote_copy(
            src_ref=rim_src.at[e],
            dst_ref=rim_got.at[sender],
            send_sem=sem_rim_s.at[e],
            recv_sem=sem_rim_r.at[sender],
            device_id={"patch": (DEV - 1) * e},
            device_id_type=MESH,
        )

    ends = ((0, 0), (1, DEV - 1))
    for e, who in ends:

        @pl.when(me != who)
        def _(e=e):
            rim_copy(e, me).start()

    ones8 = jnp.ones((8, FL), F32)

    def build_features(s_ref, nb_ref, z, v):
        xm = shift_x(v, -1, FW)
        xp = shift_x(v, 1, FW)
        xs = jnp.concatenate([xm, v, xp], axis=0)
        ym = shift_y(xs, -1, FW)
        yp = shift_y(xs, 1, FW)
        s_ref[z] = jnp.concatenate([ym, xs, yp, ones8], axis=0).astype(BF16)
        nb_ref[z] = ym[8:16] + yp[8:16] + xm + xp - 6.0 * v

    a1[HID:HB, :] = jnp.ones((HB - HID, FL), BF16)
    a2[HID:HB, :] = jnp.ones((HB - HID, FL), BF16)
    p1[...] = jnp.zeros_like(p1)
    p2[...] = jnp.zeros_like(p2)
    p3[...] = jnp.zeros_like(p3)
    gsum[...] = jnp.zeros_like(gsum)
    v0[...] = jnp.zeros_like(v0)
    g2[...] = jnp.zeros_like(g2)
    g1[...] = jnp.zeros_like(g1)
    gout[...] = jnp.zeros_like(gout)
    d1[...] = jnp.zeros_like(d1)
    sbv[...] = jnp.zeros_like(sbv)
    v1[...] = jnp.zeros_like(v1)
    s1[...] = jnp.zeros_like(s1)

    halo_copies[0].wait()
    halo_copies[1].wait()
    for src, at, dst in ((fst, 0, v0), (fct, 4, g2)):
        for f in range(NF):
            lo = hr_lo[f, at : at + 4, :]
            hi = hr_hi[f, at : at + 4, :]
            own = src[f]
            rows = jnp.concatenate(
                [
                    lo,
                    own[0:8],
                    jnp.where(wide, own[8:12], hi),
                    jnp.where(wide, own[12:16], 0.0),
                    jnp.where(wide, hi, 0.0),
                ],
                axis=0,
            )
            for i in range(EXT):
                dst[i, f : f + 1, :] = rows[i : i + 1]

    rim_row_ref[...] = jnp.zeros_like(rim_row_ref)
    for e, who in ends:

        @pl.when(me != who)
        def _(e=e):
            rim_copy(e, me).wait_send()

        @pl.when(me == who)
        def _(e=e, who=who):
            rim_row_ref[...] = rim_src[e]

            def one(t, c):
                s = lax.rem(who + t, DEV)
                rim_copy(e, s).wait_recv()
                rim_row_ref[...] = rim_row_ref[...] + rim_got[s]
                return c

            lax.fori_loop(1, DEV, one, 0)

    rim_hi, rim_lo = split(rim_row_ref[...])
    beside = dot(rim_hi, pool_t[...]) + dot(rim_lo, pool_t[...])
    v0[3] = jnp.where(first, beside, v0[3])
    v0[HALO + 8] = jnp.where(last & ~wide, beside, v0[HALO + 8])
    v0[HALO + 16] = jnp.where(last & wide, beside, v0[HALO + 16])

    pair_copy.wait()

    def add_pair(k, c):
        sendb[core, k] = sendb[core, k] + pairb[k]
        return c

    lax.fori_loop(0, CHIPS, add_pair, 0)

    def ga_copy(t):
        k = lax.rem(chip + t, CHIPS)
        return pltpu.make_async_remote_copy(
            src_ref=sendb.at[core, k],
            dst_ref=recvb.at[chip],
            send_sem=sem_ga.at[0, t],
            recv_sem=sem_ga.at[1, t],
            device_id={"patch": 2 * k + core},
            device_id_type=MESH,
        )

    def start_ga(t, c):
        ga_copy(t).start()
        return c

    lax.fori_loop(1, CHIPS, start_ga, 0)

    halo_copies[2].wait()
    halo_copies[3].wait()
    for f in range(NF):
        kappa = kc_ref[f : f + 1, :]
        for src, lo, hi, dst in (
            (jnp.where(live48, cst[f], 0.0), cr_lo[f : f + 1], cr_hi[f : f + 1], upd),
            (
                jnp.where(in_region | ~live48, 0.0, cct[f]),
                cr_lo[8 + f : 9 + f],
                cr_hi[8 + f : 9 + f],
                back,
            ),
        ):
            below = jnp.where(row48 == 0, lo, pltpu.roll(src, 1, 0))
            above = jnp.where(row48 == nc - 1, hi, pltpu.roll(src, CR - 1, 0))
            new = src + kappa * (below + above + neighbours(src, CW) - 6.0 * src)
            dst[f] = jnp.where(live48, new, 0.0)

    kf = kf_ref[...]

    def features_first(z, c):
        build_features(s0, nb0, z, v0[z])
        return c

    lax.fori_loop(0, EXT, features_first, 0)

    def rim_row(z):
        return (first & (z < HALO)) | (last & (z >= HALO + n))

    def advance(z, v, nb, source):
        lap = v[z - 1] + v[z + 1] + nb[z]
        return v[z] + kf * lap + 0.5 * source[0:8]

    def forward_row(z, c):
        for i in range(FL // CHUNK):
            ln = slice(CHUNK * i, CHUNK * (i + 1))
            feat = s0[pl.ds(z - 1, 3), :, ln].reshape(3 * FB_ROWS, CHUNK)
            h = dot(w1[...], feat)
            a1[0:HID, ln] = (h + h * jnp.tanh(h)).astype(BF16)
            h = dot(w2[...], a1[:, ln])
            a2[0:HID, ln] = (h + h * jnp.tanh(h)).astype(BF16)
        new = advance(z, v0, nb0, dot(w3[...], a2[...]))
        new = jnp.where(rim_row(z), v0[z], new)
        v1[z] = new
        build_features(s1, nb1, z, new)
        return c

    lax.fori_loop(1, EXT - 1, forward_row, 0)

    def wait_ga(t, c):
        ga_copy(t).wait()
        return c

    lax.fori_loop(1, CHIPS, wait_ga, 0)
    recvb[chip] = sendb[core, chip]
    gab[...] = jnp.zeros_like(gab)

    def add_ga(k, c):
        gab[...] = gab[...] + recvb[k]
        return c

    lax.fori_loop(0, CHIPS, add_ga, 0)
    gab_hi, gab_lo = split(gab[...])
    lifted = dot(gab_hi, pool_t[...]) + dot(gab_lo, pool_t[...])
    for r in range(10):
        lift = lifted[5 * r : 5 * r + 5] * 0.125
        for i in (2 + 2 * r, 3 + 2 * r):
            g2[i, 0:5, :] = g2[i, 0:5, :] + lift

    def level_row(z):
        return ~(rim_row(z)) & (z < HALO + n + 2)

    def mask_g2(z, c):
        g2[z] = jnp.where(level_row(z) & (z >= 2), g2[z], 0.0)
        return c

    lax.fori_loop(0, EXT, mask_g2, 0)

    def backward_row(z, s_ref, g_ref, v_ref, nb_ref, with_source):
        own = (z >= HALO) & (z < HALO + n)
        g = g_ref[z]
        half = 0.5 * g
        gsum[...] = gsum[...] + jnp.where(own, half, 0.0)
        sbv[...] = jnp.concatenate([half, jnp.zeros_like(half)], axis=0).astype(BF16)
        for i in range(FL // CHUNK):
            ln = slice(CHUNK * i, CHUNK * (i + 1))
            feat = s_ref[pl.ds(z - 1, 3), :, ln].reshape(3 * FB_ROWS, CHUNK)
            h = dot(w1[...], feat)
            t = jnp.tanh(h)
            u = h * t
            a1[0:HID, ln] = (h + u).astype(BF16)
            sl1[:, ln] = (1.0 + t) * (1.0 + h - u)
            h = dot(w2[...], a1[:, ln])
            t = jnp.tanh(h)
            u = h * t
            a2[0:HID, ln] = (h + u).astype(BF16)
            slope = (1.0 + t) * (1.0 + h - u)
            d2[:, ln] = (dot(w3t[...], sbv[:, ln]) * slope).astype(BF16)
            d1[z + 2, :, ln] = (dot(w2t[...], d2[:, ln]) * sl1[:, ln]).astype(BF16)
        feat = s_ref[pl.ds(z - 1, 3)].reshape(3 * FB_ROWS, FL)
        p1[...] = p1[...] + jnp.where(own, dot_nt(d1[z + 2], feat), 0.0)
        p2[...] = p2[...] + jnp.where(own, dot_nt(d2[...], a1[...]), 0.0)
        p3[...] = p3[...] + jnp.where(own, dot_nt(a2[0:HID, :], sbv[...]), 0.0)
        if with_source:
            v2[z] = advance(z, v_ref, nb_ref, dot(w3[...], a2[...]))

    def spread_row(r, g_ref, out_ref):
        wide_rows = d1[pl.ds(r + 1, 3)].reshape(3 * HID, FL)
        acc = dot(w1t[...], wide_rows)
        xs = shift_y(acc[0:24], 1, FW) + acc[24:48] + shift_y(acc[48:72], -1, FW)
        field = shift_x(xs[0:8], 1, FW) + xs[8:16] + shift_x(xs[16:24], -1, FW)
        g = g_ref[r]
        below = g_ref[jnp.maximum(r - 1, 0)]
        above = g_ref[r + 1]
        a = g + kf * (neighbours(g, FW) - 6.0 * g + below + above) + field
        araw[r] = a
        inside = level_row(r) & (r >= 3) & (r < HALO + n + 1)
        out_ref[r] = jnp.where(inside, a, 0.0)

    def second_backward(z, c):
        backward_row(z, s1, g2, v1, nb1, True)
        spread_row(z - 2, g2, g1)
        return c

    lax.fori_loop(2, EXT - 2, second_backward, 0)
    spread_row(EXT - 4, g2, g1)
    rim[0] = araw[3]
    rim[1] = jnp.where(wide, araw[HALO + 16], araw[HALO + 8])

    pairs = jnp.concatenate(
        [v2[HALO + 2 * k] + v2[HALO + 2 * k + 1] for k in range(8)], axis=0
    )
    pairs_hi, pairs_lo = split(pairs)
    rest = (dot(pairs_hi, pool[...]) + dot(pairs_lo, pool[...])) * 0.125
    for k in range(8):
        for f in range(NF):
            rs[8 * f + k : 8 * f + k + 1, :] = rest[8 * k + f : 8 * k + f + 1]

    def rs_copy(t):
        return pltpu.make_async_remote_copy(
            src_ref=rs,
            dst_ref=gath.at[core, chip],
            send_sem=sem_rs.at[0, t],
            recv_sem=sem_rs.at[1, t],
            device_id={"patch": 2 * lax.rem(chip + t, CHIPS) + core},
            device_id_type=MESH,
        )

    def start_rs(t, c):
        rs_copy(t).start()
        return c

    lax.fori_loop(1, CHIPS, start_rs, 0)
    gath[core, chip] = rs[...]

    def first_backward(z, c):
        backward_row(z, s0, g1, v0, nb0, False)
        spread_row(z - 2, g1, gout)
        return c

    lax.fori_loop(3, EXT - 3, first_backward, 0)
    spread_row(EXT - 5, g1, gout)
    spread_row(EXT - 4, g1, gout)

    lane = lax.broadcasted_iota(jnp.int32, (8, 128), 1)
    pk[...] = jnp.zeros_like(pk)
    for k in range(GROUP):
        rows = slice(8 * k, 8 * k + 8)
        pk[k, :, 0:240] = p1[rows]
        pk[k, :, 256 : 256 + HB] = p2[rows]
        pk[k, :, 512:528] = p3[rows]
    total = jnp.sum(gsum[...], axis=1, keepdims=True)
    pk[0, :, 512:640] = jnp.where(lane == 16, total, pk[0, :, 512:640])

    def r1_copy(t):
        k = lax.rem(w + t, GROUP)
        return pltpu.make_async_remote_copy(
            src_ref=pk.at[k],
            dst_ref=r1.at[w],
            send_sem=sem_r1s.at[t],
            recv_sem=sem_r1r.at[t],
            device_id={"patch": xg * GROUP + k},
            device_id_type=MESH,
        )

    def r2_copy(t):
        k = lax.rem(slot2 + t, 16)
        return pltpu.make_async_remote_copy(
            src_ref=r1sum,
            dst_ref=r2.at[slot2],
            send_sem=sem_r2s.at[t],
            recv_sem=sem_r2r.at[t],
            device_id={"patch": (k // 4) * GROUP + w, "dp": lax.rem(k, 4)},
            device_id_type=MESH,
        )

    def r3_copy(t):
        k = lax.rem(w + t, GROUP)
        return pltpu.make_async_remote_copy(
            src_ref=pall.at[w],
            dst_ref=pall.at[w],
            send_sem=sem_r3s.at[t],
            recv_sem=sem_r3r.at[t],
            device_id={"patch": xg * GROUP + k},
            device_id_type=MESH,
        )

    def run(make, what):
        def one(t, c):
            what(make(t))
            return c

        lax.fori_loop(1, 16, one, 0)

    run(r1_copy, lambda x: x.start())

    rim[0] = rim[0] + araw[3]
    rim[1] = rim[1] + jnp.where(wide, araw[HALO + 16], araw[HALO + 8])
    rims = jnp.concatenate([rim[0], rim[1]], axis=0)
    rims_hi, rims_lo = split(rims)
    rims = dot(rims_hi, pool[...]) + dot(rims_lo, pool[...])
    rgs[...] = rims

    def rg_copy(e, dev, t):
        return pltpu.make_async_remote_copy(
            src_ref=rgs.at[pl.ds(8 * e, 8)],
            dst_ref=rg.at[e],
            send_sem=sem_rg_s.at[e, t],
            recv_sem=sem_rg_r.at[e],
            device_id={"patch": dev},
            device_id_type=MESH,
        )

    for e, who in ends:

        @pl.when(me == who)
        def _(e=e, who=who):
            def one(t, c):
                rg_copy(e, lax.rem(who + t, DEV), t).start()
                return c

            lax.fori_loop(1, DEV, one, 0)
            rg[e] = rgs[8 * e : 8 * e + 8, :]

    r1[w] = pk[w]
    run(r1_copy, lambda x: x.wait())

    def add_up(ref):
        out = ref[0]
        for k in range(1, 16):
            out = out + ref[k]
        return out

    r1sum[...] = add_up(r1)
    run(r2_copy, lambda x: x.start())

    def wait_rs(t, c):
        rs_copy(t).wait()
        return c

    lax.fori_loop(1, CHIPS, wait_rs, 0)
    gp_copy = pltpu.make_async_remote_copy(
        src_ref=gath.at[core],
        dst_ref=gath.at[core],
        send_sem=sem_gp.at[0],
        recv_sem=sem_gp.at[1],
        device_id={"patch": partner},
        device_id_type=MESH,
    )
    gp_copy.start()

    for i in range(FR):
        keep = (i < n)
        a = jnp.where(keep, v2[HALO + i], 0.0)
        b = jnp.where(keep, gout[HALO + i], 0.0)
        for f in range(NF):
            fine_out[f, i : i + 1, :] = a[f : f + 1]
            fine_adj[f, i : i + 1, :] = b[f : f + 1]

    r2[slot2] = r1sum[...]
    run(r2_copy, lambda x: x.wait())
    pall[w] = add_up(r2)
    run(r3_copy, lambda x: x.start())

    qi = lax.broadcasted_iota(jnp.int32, (DEV, 512), 0)
    qc = lax.broadcasted_iota(jnp.int32, (DEV, 512), 1)
    qd = 2 * ((qc % 256) // 8) + qc // 256
    counts = fcv[...]
    starts = dot(counts, (qi < qd).astype(F32).astype(BF16))
    sizes = dot(counts, (qi == qd).astype(F32).astype(BF16))
    qr = (lax.broadcasted_iota(jnp.int32, (16, 512), 1) % 8).astype(F32)
    place = jnp.where(qr < 4.0 * sizes, 4.0 * starts + qr, -1.0)[0:1]
    off = off48[:, 0:1].astype(F32)
    onehot = (off == place).astype(F32).astype(BF16)

    gp_copy.wait()
    for f in range(NF):
        rows = gath[:, :, 8 * f : 8 * f + 8, :].reshape(512, CL)
        rows_hi, rows_lo = split(rows)
        pulled = dot(onehot, rows_hi) + dot(onehot, rows_lo)
        coarse_out[f] = jnp.where(in_region, pulled, upd[f])

    for e, who in ends:

        @pl.when(me != who)
        def _(e=e):
            rg_copy(e, partner, 0).wait_recv()

        @pl.when(me == who)
        def _(e=e, who=who):
            def one(t, c):
                rg_copy(e, lax.rem(who + t, DEV), t).wait_send()
                return c

            lax.fori_loop(1, DEV, one, 0)

    for f in range(NF):
        coarse_adj[f] = (
            back[f]
            + jnp.where(row48 == low_local, rg[0, f : f + 1, :], 0.0)
            + jnp.where(row48 == high_local, rg[1, f : f + 1, :], 0.0)
        )

    run(r3_copy, lambda x: x.wait())
    for k in range(GROUP):
        p_out[8 * k : 8 * k + 8, :] = pall[k]


def pieces(b):
    hi = lax.reduce_precision(b, 8, 7)
    mid = lax.reduce_precision(b - hi, 8, 7)
    return jnp.stack([hi, mid, b - hi - mid], axis=1).astype(BF16)


def on_device(
    coarse_state,
    fine_state,
    coarse_cot,
    fine_cot,
    coarse_diffusion,
    w_in,
    b_in,
    w_mid,
    b_mid,
    w_out,
    b_out,
    coarse_counts,
    fine_counts,
    fine_anchor,
):
    win = jnp.pad(w_in.reshape(HID, 3, 9, NF), ((0, 0), (0, 0), (0, 0), (0, 3)))
    win = jnp.pad(win.reshape(HID, 3, 72), ((0, 0), (0, 0), (0, 8)))
    bias1 = jnp.pad(pieces(b_in)[:, None], ((0, 0), (1, 1), (72, 5)))
    w1 = ((win + bias1) * 0.5).reshape(HID, 3 * FB_ROWS).astype(BF16)
    w1t = jnp.concatenate([win[:, 2].T, win[:, 1].T, win[:, 0].T], axis=1)
    w2 = (jnp.concatenate([w_mid, jnp.pad(pieces(b_mid), ((0, 0), (0, 13)))], axis=1) * 0.5).astype(
        BF16
    )
    w2t = (w_mid.T * 0.5).astype(BF16)
    w3 = jnp.concatenate([w_out, jnp.pad(pieces(b_out), ((0, 0), (0, 13)))], axis=1)
    w3 = jnp.pad(w3, ((0, 11), (0, 0)))
    w3t = (jnp.pad(w_out.T, ((0, 0), (0, 11))) * 0.5).astype(BF16)
    fine_index = jnp.arange(FL, dtype=jnp.int32)
    target = fine_index // FW // 2 * CW + fine_index % FW // 2
    pool = (target[:, None] == jnp.arange(CL, dtype=jnp.int32)[None, :]).astype(BF16)
    kc = jnp.broadcast_to(jnp.pad(coarse_diffusion, (0, 3))[:, None], (8, CL))
    kf = jnp.broadcast_to(jnp.pad(2.0 * coarse_diffusion, (0, 3))[:, None], (8, FL))
    fcv = jnp.broadcast_to(fine_counts[None, :].astype(BF16), (16, DEV))

    vm = pltpu.VMEM
    slab = vm((EXT, 8, FL), F32)
    dma = pltpu.SemaphoreType.DMA
    in_vmem = pl.BlockSpec(memory_space=pltpu.VMEM)
    in_smem = pl.BlockSpec(memory_space=pltpu.SMEM)
    coarse_shape = jax.ShapeDtypeStruct((NF, CR, CL), F32)
    fine_shape = jax.ShapeDtypeStruct((NF, FR, FL), F32)
    coarse_new, fine_new, coarse_back, fine_back, packed = pl.pallas_call(
        kernel,
        out_shape=(
            coarse_shape,
            fine_shape,
            coarse_shape,
            fine_shape,
            jax.ShapeDtypeStruct((HID, PL), F32),
        ),
        in_specs=[in_smem] * 3 + [in_vmem] * 15,
        out_specs=(in_vmem,) * 5,
        scratch_shapes=[
            pltpu.SMEM((DEV,), jnp.int32),
            slab,
            slab,
            slab,
            slab,
            slab,
            vm((EXT, FB_ROWS, FL), BF16),
            vm((EXT, FB_ROWS, FL), BF16),
            vm((HB, FL), BF16),
            vm((HB, FL), BF16),
            vm((HID, FL), F32),
            vm((EXT + 2, HID, FL), BF16),
            vm((HID, FL), BF16),
            vm((16, FL), BF16),
            slab,
            slab,
            slab,
            slab,
            vm((2, 8, FL), F32),
            vm((HID, 3 * FB_ROWS), F32),
            vm((HID, HB), F32),
            vm((HID, 16), F32),
            vm((8, FL), F32),
            vm((2, CHIPS, GA_ROWS, CL), F32),
            vm((CHIPS, GA_ROWS, CL), F32),
            vm((CHIPS, GA_ROWS, CL), F32),
            vm((GA_ROWS, CL), F32),
            vm((NF, 8, FL), F32),
            vm((NF, 8, FL), F32),
            vm((NF, 8, FL), F32),
            vm((NF, 8, FL), F32),
            vm((16, CL), F32),
            vm((16, CL), F32),
            vm((16, CL), F32),
            vm((16, CL), F32),
            vm((NF, CR, CL), F32),
            vm((NF, CR, CL), F32),
            vm((2, 8, CL), F32),
            vm((DEV, 8, CL), F32),
            vm((8, CL), F32),
            vm((40, CL), F32),
            vm((2, CHIPS, 40, CL), F32),
            vm((16, CL), F32),
            vm((2, 8, CL), F32),
            vm((GROUP, 8, PL), F32),
            vm((GROUP, 8, PL), F32),
            vm((8, PL), F32),
            vm((16, 8, PL), F32),
            vm((GROUP, 8, PL), F32),
            dma((2,)),
            dma((2, CHIPS)),
            dma((2, 4)),
            dma((2,)),
            dma((DEV,)),
            dma((2, CHIPS)),
            dma((2,)),
            dma((2, DEV)),
            dma((2,)),
            dma((16,)),
            dma((16,)),
            dma((16,)),
            dma((16,)),
            dma((16,)),
            dma((16,)),
        ],
        compiler_params=pltpu.CompilerParams(
            collective_id=0, has_side_effects=True, vmem_limit_bytes=56 * 1024 * 1024
        ),
    )(
        fine_counts,
        coarse_counts,
        fine_anchor,
        fcv,
        coarse_state[0],
        fine_state[0],
        coarse_cot[0],
        fine_cot[0],
        kf,
        kc,
        w1,
        w2,
        w3,
        w1t,
        w2t,
        w3t,
        pool,
        pool.T,
    )
    scale = 1.0 / math.sqrt(4 * 96 * 8 * FL)
    packed = packed * scale
    grad_w_in = packed[:, : 3 * FB_ROWS].reshape(HID, 3, FB_ROWS)[:, :, :72]
    grad_w_in = grad_w_in.reshape(HID, 27, 8)[:, :, :NF].reshape(HID, 27 * NF)
    return (
        coarse_new[None],
        fine_new[None],
        coarse_back[None],
        fine_back[None],
        grad_w_in,
        packed[:, FB_ROWS + 72],
        packed[:, 256 : 256 + HID],
        packed[:, 256 + HID],
        packed[:, 512 : 512 + NF].T,
        packed[:NF, 528],
    )


def solution(mesh):
    state = P("dp", None, "patch", None)
    return jax.shard_map(
        on_device,
        mesh=mesh,
        in_specs=(state,) * 4 + (P(),) * 10,
        out_specs=(state,) * 4 + (P(),) * 6,
        check_vma=False,
    )
```

```python
import math

import jax
import jax.numpy as jnp
from jax import lax
from jax.experimental import pallas as pl
from jax.experimental.pallas import tpu as pltpu
from jax.sharding import PartitionSpec as P

MESH = pl.DeviceIdType.MESH
F32 = jnp.float32
BF16 = jnp.bfloat16

DEV = 64
CHIPS = 32
CW = 16
FW = 32
CL = CW * CW
FL = FW * FW
CR = 48
FR = 16
NF = 5
CHAIN = 2048
REGION = 384
TAKEN = 4
HALO = TAKEN + 1
EXT = FR + 2 * HALO
UNROLL = 4
FB_ROWS = 80
HID = 128
HB = 144
GROUP = 16
PART = 24
PACKED = GROUP * PART
GA_ROWS = 40


def dot(a, b):
    return jnp.dot(a, b, preferred_element_type=F32)


def dot_nt(a, b):
    return lax.dot_general(a, b, (((1,), (1,)), ((), ())), preferred_element_type=F32)


def dot_tn(a, b):
    return lax.dot_general(a, b, (((0,), (0,)), ((), ())), preferred_element_type=F32)


def grid(shape, dim):
    return lax.broadcasted_iota(jnp.int32, shape, dim)


def bits(mask):
    return mask.astype(F32).astype(BF16)


def pieces(b):
    hi = b.astype(BF16).astype(F32)
    mid = (b - hi).astype(BF16).astype(F32)
    zeros = jnp.zeros((13, b.shape[1]), F32)
    return jnp.concatenate([hi, mid, b - hi - mid, zeros], axis=0).astype(BF16)


def split(x):
    hi = x.astype(BF16)
    return hi, (x - hi.astype(F32)).astype(BF16)


def shift_x(v, step, width):
    lanes = v.shape[1]
    col = grid((v.shape[0], 128), 1) % width
    parts = []
    for i in range(lanes // 128):
        s = v[:, 128 * i : 128 * (i + 1)]
        if step == 1:
            parts.append(
                jnp.where(
                    col == width - 1, pltpu.roll(s, width - 1, 1), pltpu.roll(s, 127, 1)
                )
            )
        else:
            parts.append(
                jnp.where(col == 0, pltpu.roll(s, 129 - width, 1), pltpu.roll(s, 1, 1))
            )
    return jnp.concatenate(parts, axis=1)


def shift_y(v, step, width):
    lanes = v.shape[1]
    return pltpu.roll(v, lanes - width if step == 1 else width, 1)


def neighbours(v, width):
    return (
        shift_y(v, -1, width)
        + shift_y(v, 1, width)
        + shift_x(v, -1, width)
        + shift_x(v, 1, width)
    )


def kernel(
    fc_smem,
    cc_smem,
    anchor_smem,
    cd_smem,
    bo_smem,
    fcv,
    win_ref,
    bin_ref,
    wmid_ref,
    bmid_ref,
    wout_ref,
    cst_hbm,
    fst_hbm,
    cct_hbm,
    fct_hbm,
    coarse_out_hbm,
    fine_out_hbm,
    coarse_adj_hbm,
    fine_adj_hbm,
    p_out,
    cst,
    fst,
    cct,
    fct,
    coarse_out,
    fine_out,
    coarse_adj,
    fine_adj,
    w1,
    w2,
    w3,
    wp,
    w2t,
    w3t,
    pool,
    pool_t,
    sem_in,
    sem_out,
    base_s,
    v0,
    v1,
    v2,
    nb0,
    nb1,
    s0,
    s1,
    a1,
    a2,
    sl1,
    d1,
    d2,
    sbv,
    g2,
    g1,
    araw,
    gout,
    rim,
    p1,
    p2,
    p3,
    gsum,
    sendb,
    pairb,
    ga_a,
    ga_b,
    sum_a,
    sum_b,
    ga_a2,
    ga_b2,
    gh,
    gr,
    hs_dn,
    hs_up,
    hr_lo,
    hr_hi,
    cs_dn,
    cs_up,
    cr_lo,
    cr_hi,
    upd,
    back,
    rim_src,
    rim_got,
    rim_row_ref,
    rs,
    gath,
    rgs,
    rg,
    pk,
    r1,
    r1sum,
    r2,
    pall,
    sem_pair,
    sem_a1,
    sem_b1,
    sem_a2,
    sem_b2,
    sem_edge,
    sem_halo,
    sem_rim_s,
    sem_rim_r,
    sem_rs,
    sem_gp,
    sem_rg_s,
    sem_rg_r,
    sem_r1s,
    sem_r1r,
    sem_r2s,
    sem_r2r,
    sem_r3s,
    sem_r3r,
):
    me = lax.axis_index("patch")
    dp = lax.axis_index("dp")
    core = lax.rem(me, 2)
    chip = me // 2
    partner = chip * 2 + (1 - core)
    nxt = lax.rem(me + 1, DEV)
    prv = lax.rem(me + DEV - 1, DEV)

    xg = me // GROUP
    w = lax.rem(me, GROUP)
    slot2 = xg * 4 + dp
    cx, czy = chip // 8, lax.rem(chip, 8)
    cy, cxz = lax.rem(chip, 4), chip // 4
    arrivals = [
        pltpu.make_async_copy(src, dst, sem_in.at[i])
        for i, (src, dst) in enumerate(
            ((cst_hbm, cst), (fst_hbm, fst), (cct_hbm, cct), (fct_hbm, fct))
        )
    ]
    for copy in arrivals:
        copy.start()

    barrier = pltpu.get_barrier_semaphore()

    def greet(t, c):
        pl.semaphore_signal(
            barrier, inc=1, device_id={"patch": lax.rem(me + t, DEV)}, device_id_type=MESH
        )
        return c

    lax.fori_loop(1, DEV, greet, 0)

    def greet_dp(t, c):
        pl.semaphore_signal(
            barrier,
            inc=1,
            device_id={
                "patch": (t // 3) * GROUP + w,
                "dp": lax.rem(dp + 1 + lax.rem(t, 3), 4),
            },
            device_id_type=MESH,
        )
        return c

    lax.fori_loop(0, 12, greet_dp, 0)

    col = grid((27 * NF, 3 * FB_ROWS), 1)
    row = grid((27 * NF, 3 * FB_ROWS), 0)
    part, field = col % FB_ROWS // 8, col % 8
    place = (col // FB_ROWS * 9 + part) * NF + field
    laid = dot_tn(win_ref[...], bits((row == place) & (part < 9) & (field < NF)))
    brow, bcol = grid((16, 3 * FB_ROWS), 0), grid((16, 3 * FB_ROWS), 1)
    bias = dot_tn(pieces(bin_ref[...]), bits((bcol == FB_ROWS + 72 + brow) & (brow < 3)))
    w1[...] = ((laid + bias) * 0.5).astype(BF16)
    qrow, qcol = grid((FB_ROWS, 27 * NF), 0), grid((FB_ROWS, 27 * NF), 1)
    wp[...] = jnp.zeros_like(wp)
    for a in range(3):
        take = (qcol == (a * 9 + qrow // 8) * NF + qrow % 8) & (qrow < 72) & (qrow % 8 < NF)
        turned = dot(bits(take), win_ref[...]).astype(BF16)
        for j in range(2):
            m = j + 2 - a
            wp[FB_ROWS * j : FB_ROWS * (j + 1), HID * m : HID * (m + 1)] = turned
    eye = bits(grid((HID, HID), 0) == grid((HID, HID), 1))
    eye16 = bits(grid((16, 16), 0) == grid((16, 16), 1))
    w2[:, 0:HID] = (wmid_ref[...].astype(F32) * 0.5).astype(BF16)
    w2[:, HID:HB] = (dot_tn(pieces(bmid_ref[...]), eye16) * 0.5).astype(BF16)
    w2t[...] = (dot_nt(eye, wmid_ref[...]) * 0.5).astype(BF16)
    w3[...] = dot(bits(grid((16, NF), 0) == grid((16, NF), 1)), wout_ref[...]).astype(BF16)
    w3t[...] = (dot_nt(eye, w3[...]) * 0.5).astype(BF16)
    fine_cell, coarse_cell = grid((FL, CL), 0), grid((FL, CL), 1)
    pool[...] = bits(fine_cell // (2 * FW) * CW + fine_cell % FW // 2 == coarse_cell)
    coarse_cell, fine_cell = grid((CL, FL), 0), grid((CL, FL), 1)
    pool_t[...] = bits(fine_cell // (2 * FW) * CW + fine_cell % FW // 2 == coarse_cell)
    field_row = grid((8, FL), 0)
    kf = jnp.zeros((8, FL), F32)
    half_bias = jnp.zeros((8, FL), F32)
    for f in range(NF):
        kf = jnp.where(field_row == f, 2.0 * cd_smem[f], kf)
        half_bias = jnp.where(field_row == f, 0.5 * bo_smem[f], half_bias)
    for copy in arrivals:
        copy.wait()

    anchor = anchor_smem[0]

    def count(d, carry):
        fs, cs = carry
        base_s[d] = fs
        fs = fs + fc_smem[d]
        cs = cs + jnp.where(d < me, cc_smem[d], 0)
        return (fs, cs)

    _, cpatch = lax.fori_loop(0, DEV, count, (jnp.int32(0), jnp.int32(0)))
    cstart = cpatch * CW
    nc = cc_smem[me] * CW
    n = fc_smem[me] * 8
    wide = n == FR
    first = me == 0
    last = me == DEV - 1

    def wrap(x):
        return lax.rem(x + 2 * CHAIN + CHAIN // 2, CHAIN) - CHAIN // 2

    def live_or_none(local):
        return jnp.where((local >= 0) & (local < nc), local, -10000)

    low_local = live_or_none(wrap(anchor - 1 - cstart))
    high_local = live_or_none(wrap(anchor + REGION - cstart))

    row48 = grid((CR, CL), 0)
    live48 = row48 < nc
    off48 = lax.rem(row48 + (cstart - anchor + 2 * CHAIN), CHAIN)
    in_region = (off48 < REGION) & live48

    for f in range(NF):
        hs_dn[f, 0:4, :] = fst[f, 0:4, :]
        hs_dn[f, 4:8, :] = fct[f, 0:4, :]
        hs_up[f, 0:4, :] = jnp.where(wide, fst[f, 12:16, :], fst[f, 4:8, :])
        hs_up[f, 4:8, :] = jnp.where(wide, fct[f, 12:16, :], fct[f, 4:8, :])
    cs_dn[...] = jnp.zeros_like(cs_dn)
    cs_up[...] = jnp.zeros_like(cs_up)
    for f in range(NF):
        kept = jnp.where(in_region, 0.0, cct[f])
        cs_dn[f : f + 1, :] = cst[f, 0:1, :]
        cs_dn[8 + f : 9 + f, :] = kept[0:1]
        cs_up[f : f + 1, :] = jnp.where(
            nc == 48,
            cst[f, 47:48, :],
            jnp.where(nc == 32, cst[f, 31:32, :], cst[f, 15:16, :]),
        )
        cs_up[8 + f : 9 + f, :] = jnp.where(
            nc == 48, kept[47:48], jnp.where(nc == 32, kept[31:32], kept[15:16])
        )

    def neighbour_copies():
        def one(src, dst, k, dev):
            return pltpu.make_async_remote_copy(
                src_ref=src,
                dst_ref=dst,
                send_sem=sem_halo.at[0, k],
                recv_sem=sem_halo.at[1, k],
                device_id={"patch": dev},
                device_id_type=MESH,
            )

        return (
            one(hs_up, hr_lo, 0, nxt),
            one(hs_dn, hr_hi, 1, prv),
            one(cs_up, cr_lo, 2, nxt),
            one(cs_dn, cr_hi, 3, prv),
        )

    cot = jnp.concatenate([jnp.where(live48, cct[f], 0.0) for f in range(NF)], axis=0)
    cot_hi, cot_lo = split(cot)
    cot2 = jnp.concatenate([cot_hi, cot_lo], axis=1)
    srow = grid((GA_ROWS, NF * CR), 0)
    scol = grid((GA_ROWS, NF * CR), 1)
    pick = jnp.where(
        scol // CR == srow % NF, scol % CR - srow // NF, 99999
    )

    def rows_for(c2):
        def one(i, c):
            hot = []
            for k in range(8):
                base = wrap(anchor + 4 * base_s[2 * (8 * i + k) + c2] - cstart)
                hot.append((pick == base).astype(F32))
            both = dot(jnp.concatenate(hot, axis=0).astype(BF16), cot2)
            both = both[:, :CL] + both[:, CL:]
            sendb[c2, i] = both.reshape(2, 4, GA_ROWS, CL)
            return c

        lax.fori_loop(0, CHIPS // 8, one, 0)

    ust = jnp.concatenate([cst[f] for f in range(NF)], axis=0)
    ust_hi, ust_lo = split(ust)
    ust2 = jnp.concatenate([ust_hi, ust_lo], axis=1)
    frow = grid((16, NF * CR), 0)
    fcol = grid((16, NF * CR), 1)
    fpick = jnp.where(fcol // CR == frow, fcol % CR, 99999)
    for e, local in ((0, low_local), (1, high_local)):
        both = dot(bits(fpick == local), ust2)
        rim_src[e] = (both[:, :CL] + both[:, CL:])[0:8]

    rows_for(1 - core)

    pl.semaphore_wait(barrier, DEV - 1 + 12)

    halo_copies = neighbour_copies()
    for copy in halo_copies:
        copy.start()

    def rim_copy(e, sender):
        return pltpu.make_async_remote_copy(
            src_ref=rim_src.at[e],
            dst_ref=rim_got.at[sender],
            send_sem=sem_rim_s.at[e],
            recv_sem=sem_rim_r.at[sender],
            device_id={"patch": (DEV - 1) * e},
            device_id_type=MESH,
        )

    ends = ((0, 0), (1, DEV - 1))
    for e, who in ends:

        @pl.when(me != who)
        def _(e=e):
            rim_copy(e, me).start()

    pair_copy = pltpu.make_async_remote_copy(
        src_ref=sendb.at[1 - core],
        dst_ref=pairb,
        send_sem=sem_pair.at[0],
        recv_sem=sem_pair.at[1],
        device_id={"patch": partner},
        device_id_type=MESH,
    )
    pair_copy.start()
    rows_for(core)

    ones8 = jnp.ones((8, FL), F32)

    def build_features(s_ref, nb_ref, z, v):
        xm = shift_x(v, -1, FW)
        xp = shift_x(v, 1, FW)
        xs = jnp.concatenate([xm, v, xp], axis=0)
        ym = shift_y(xs, -1, FW)
        yp = shift_y(xs, 1, FW)
        s_ref[z] = jnp.concatenate([ym, xs, yp, ones8], axis=0).astype(BF16)
        nb_ref[z] = ym[8:16] + yp[8:16] + xm + xp - 6.0 * v

    for j in range(UNROLL):
        a1[j, HID:HB, :] = jnp.ones((HB - HID, FL), BF16)
    p1[...] = jnp.zeros_like(p1)
    p2[...] = jnp.zeros_like(p2)
    p3[...] = jnp.zeros_like(p3)
    gsum[...] = jnp.zeros_like(gsum)
    v0[...] = jnp.zeros_like(v0)
    g2[...] = jnp.zeros_like(g2)
    for z in (0, EXT - 1):
        s0[z] = jnp.zeros((FB_ROWS, FL), BF16)
        v1[z] = jnp.zeros((8, FL), F32)
    for z in range(EXT - 4, EXT):
        g1[z] = jnp.zeros((8, FL), F32)

    pair_copy.wait()

    def add_pair(k, c):
        sendb[core, k] = sendb[core, k] + pairb[k]
        return c

    lax.fori_loop(0, 4, add_pair, 0)

    def chip_copy(src, dst, sems, t, to):
        return pltpu.make_async_remote_copy(
            src_ref=src,
            dst_ref=dst,
            send_sem=sems.at[0, t],
            recv_sem=sems.at[1, t],
            device_id={"patch": 2 * to + core},
            device_id_type=MESH,
        )

    def a1_copy(t):
        k = lax.rem(cy + t, 4)
        src = sendb.at[core, :, :, k, :, 0:128]
        return chip_copy(src, ga_a.at[cy], sem_a1, t, cxz * 4 + k)

    def b1_copy(t):
        k = lax.rem(cx + t, 4)
        src = sendb.at[core, k, :, :, :, 128:256]
        return chip_copy(src, ga_b.at[cx], sem_b1, t, k * 8 + czy)

    def a2_copy(t):
        k = lax.rem(cxz + t, 8)
        src = sum_a.at[k // 2, lax.rem(k, 2)]
        return chip_copy(src, ga_a2.at[cxz], sem_a2, t, k * 4 + cy)

    def b2_copy(t):
        k = lax.rem(czy + t, 8)
        src = sum_b.at[k // 4, lax.rem(k, 4)]
        return chip_copy(src, ga_b2.at[czy], sem_b2, t, cx * 8 + k)

    def run(make, what, count=16):
        def one(t, c):
            what(make(t))
            return c

        lax.fori_loop(1, count, one, 0)

    def begin(copy):
        copy.start()

    def end(copy):
        copy.wait()

    run(a1_copy, begin, 4)
    run(b1_copy, begin, 4)

    halo_copies[0].wait()
    halo_copies[1].wait()
    for src, at, dst in ((fst, 0, v0), (fct, 4, g2)):
        for f in range(NF):
            lo = hr_lo[f, at : at + TAKEN, :]
            hi = hr_hi[f, at : at + TAKEN, :]
            own = src[f]
            rows = jnp.concatenate(
                [
                    lo,
                    own[0:8],
                    jnp.where(wide, own[8:12], hi),
                    jnp.where(wide, own[12:16], 0.0),
                    jnp.where(wide, hi, 0.0),
                ],
                axis=0,
            )
            for i in range(FR + 2 * TAKEN):
                dst[i + 1, f : f + 1, :] = rows[i : i + 1]

    rim_row_ref[...] = jnp.zeros_like(rim_row_ref)
    for e, who in ends:

        @pl.when(me != who)
        def _(e=e):
            rim_copy(e, me).wait_send()

        @pl.when(me == who)
        def _(e=e, who=who):
            rim_row_ref[...] = rim_src[e]

            def one(t, c):
                s = lax.rem(who + t, DEV)
                rim_copy(e, s).wait_recv()
                rim_row_ref[...] = rim_row_ref[...] + rim_got[s]
                return c

            lax.fori_loop(1, DEV, one, 0)

    rim_hi, rim_lo = split(rim_row_ref[...])
    beside = dot(rim_hi, pool_t[...]) + dot(rim_lo, pool_t[...])
    v0[HALO - 1] = jnp.where(first, beside, v0[HALO - 1])
    v0[HALO + 8] = jnp.where(last & ~wide, beside, v0[HALO + 8])
    v0[HALO + 16] = jnp.where(last & wide, beside, v0[HALO + 16])

    halo_copies[2].wait()
    halo_copies[3].wait()
    for f in range(NF):
        kappa = cd_smem[f]
        for src, lo, hi, dst in (
            (jnp.where(live48, cst[f], 0.0), cr_lo[f : f + 1], cr_hi[f : f + 1], upd),
            (
                jnp.where(in_region | ~live48, 0.0, cct[f]),
                cr_lo[8 + f : 9 + f],
                cr_hi[8 + f : 9 + f],
                back,
            ),
        ):
            below = jnp.where(row48 == 0, lo, pltpu.roll(src, 1, 0))
            above = jnp.where(row48 == nc - 1, hi, pltpu.roll(src, CR - 1, 0))
            new = src + kappa * (below + above + neighbours(src, CW) - 6.0 * src)
            dst[f] = jnp.where(live48, new, 0.0)

    def features_first(k, c):
        for j in range(UNROLL):
            z = 1 + UNROLL * k + j
            build_features(s0, nb0, z, v0[z])
        return c

    steps_all = (EXT - 2) // UNROLL
    lax.fori_loop(0, steps_all, features_first, 0)

    def rim_row(z):
        return (first & (z < HALO)) | (last & (z >= HALO + n))

    def advance(z, v, nb, source):
        lap = v[z - 1] + v[z + 1] + nb[z]
        return v[z] + kf * lap + (0.5 * source[0:8] + half_bias)

    def features_of(s_ref, z):
        return s_ref[pl.ds(z - 1, 3)].reshape(3 * FB_ROWS, FL)

    def forward_rows(k, c):
        rows = [(j, 1 + UNROLL * k + j) for j in range(UNROLL)]
        for _, z in rows:
            before = jnp.maximum(z - UNROLL, 0)
            build_features(s1, nb1, before, v1[before])
        for j, z in rows:
            h = dot(w1[...], features_of(s0, z))
            a1[j, 0:HID, :] = (h + h * jnp.tanh(h)).astype(BF16)
        for j, z in rows:
            h = dot(w2[...], a1[j])
            a2[j] = (h + h * jnp.tanh(h)).astype(BF16)
        for j, z in rows:
            new = advance(z, v0, nb0, dot(w3[...], a2[j]))
            v1[z] = jnp.where(rim_row(z), v0[z], new)
        return c

    lax.fori_loop(0, 4, forward_rows, 0)

    ga_a[cy] = sendb[core, :, :, cy, :, 0:128]
    ga_b[cx] = sendb[core, cx, :, :, :, 128:256]
    run(a1_copy, end, 4)
    run(b1_copy, end, 4)
    sum_a[...] = ga_a[0] + ga_a[1] + ga_a[2] + ga_a[3]
    sum_b[...] = ga_b[0] + ga_b[1] + ga_b[2] + ga_b[3]
    run(a2_copy, begin, 8)
    run(b2_copy, begin, 8)

    lax.fori_loop(4, steps_all, forward_rows, 0)
    for z in range(EXT - 1 - UNROLL, EXT - 1):
        build_features(s1, nb1, z, v1[z])

    ga_a2[cxz] = sum_a[cxz // 2, lax.rem(cxz, 2)]
    ga_b2[czy] = sum_b[czy // 4, lax.rem(czy, 4)]
    run(a2_copy, end, 8)
    run(b2_copy, end, 8)
    parts = []
    for ref in (ga_a2, ga_b2):
        part = ref[0]
        for k in range(1, 8):
            part = part + ref[k]
        parts.append(part)
    region = jnp.concatenate(parts, axis=1)
    blank = jnp.zeros((3, CL), F32)
    gh[0] = jnp.concatenate([region[0:5], blank], axis=0)
    gh[1] = jnp.concatenate([jnp.where(wide, region[35:40], region[15:20]), blank], axis=0)

    def edge_copy(k, to):
        return pltpu.make_async_remote_copy(
            src_ref=gh.at[k],
            dst_ref=gr.at[k],
            send_sem=sem_edge.at[0, k],
            recv_sem=sem_edge.at[1, k],
            device_id={"patch": to},
            device_id_type=MESH,
        )

    edges = (edge_copy(0, prv), edge_copy(1, nxt))
    for copy in edges:
        copy.start()

    def lift(x):
        hi, lo = split(x)
        return (dot(hi, pool_t[...]) + dot(lo, pool_t[...])) * 0.125

    lifted = lift(region)
    for r in range(8):
        for i in (HALO + 2 * r, HALO + 2 * r + 1):
            g2[i, 0:5, :] = g2[i, 0:5, :] + jnp.where(2 * r < n, lifted[5 * r : 5 * r + 5], 0.0)
    for copy in edges:
        copy.wait()
    lifted = lift(jnp.concatenate([gr[0], gr[1]], axis=0))
    for i in (HALO - 2, HALO - 1):
        g2[i] = g2[i] + lifted[8:16]
    for i in (HALO + 8, HALO + 9):
        g2[i] = g2[i] + jnp.where(wide, 0.0, lifted[0:8])
    for i in (HALO + 16, HALO + 17):
        g2[i] = g2[i] + jnp.where(wide, lifted[0:8], 0.0)

    def level_row(z):
        return ~(rim_row(z)) & (z < HALO + n + 2)

    def mask_g2(z, c):
        g2[z] = jnp.where(level_row(z) & (z >= HALO - 2), g2[z], 0.0)
        return c

    lax.fori_loop(0, EXT, mask_g2, 0)

    def backward_rows(zs, s_ref, g_ref, v_ref, nb_ref, with_source):
        rows = list(enumerate(zs))
        own = [(z >= HALO) & (z < HALO + n) for z in zs]
        for j, z in rows:
            half = 0.5 * g_ref[z]
            gsum[...] = gsum[...] + jnp.where(own[j], half, 0.0)
            sbv[j] = jnp.concatenate([half, jnp.zeros_like(half)], axis=0).astype(BF16)
        for j, z in rows:
            h = dot(w1[...], features_of(s_ref, z))
            t = jnp.tanh(h)
            u = h * t
            a1[j, 0:HID, :] = (h + u).astype(BF16)
            sl1[j] = (1.0 + t) * (1.0 + h - u)
        for j, z in rows:
            h = dot(w2[...], a1[j])
            t = jnp.tanh(h)
            u = h * t
            a2[j] = (h + u).astype(BF16)
            d2[j] = (dot(w3t[...], sbv[j]) * ((1.0 + t) * (1.0 + h - u))).astype(BF16)
        for j, z in rows:
            d1[z] = (dot(w2t[...], d2[j]) * sl1[j]).astype(BF16)
        for j, z in rows:
            p1[...] = p1[...] + jnp.where(own[j], dot_nt(features_of(s_ref, z), d1[z]), 0.0)
            p2[...] = p2[...] + jnp.where(own[j], dot_nt(a1[j], d2[j]), 0.0)
            p3[...] = p3[...] + jnp.where(own[j], dot_nt(sbv[j], a2[j]), 0.0)
            if with_source:
                v2[z] = advance(z, v_ref, nb_ref, dot(w3[...], a2[j]))

    def spread_rows(r0, g_ref, out_ref):
        both = dot(wp[...], d1[pl.ds(r0 - 1, 4)].reshape(4 * HID, FL))
        for j in range(2):
            r = r0 + j
            acc = both[FB_ROWS * j : FB_ROWS * (j + 1)]
            g = g_ref[r]
            kg = kf * g
            lo = jnp.concatenate([acc[0:8], acc[8:16] + kg, acc[16:24]], axis=0)
            mid = jnp.concatenate([acc[24:32] + kg, acc[32:40], acc[40:48] + kg], axis=0)
            hi = jnp.concatenate([acc[48:56], acc[56:64] + kg, acc[64:72]], axis=0)
            xs = shift_y(lo, 1, FW) + mid + shift_y(hi, -1, FW)
            moved = shift_x(xs[0:8], 1, FW) + xs[8:16] + shift_x(xs[16:24], -1, FW)
            a = g + kf * (g_ref[r - 1] + g_ref[r + 1] - 6.0 * g) + moved
            araw[r] = a
            inside = level_row(r) & (r >= HALO - 1) & (r < HALO + n + 1)
            out_ref[r] = jnp.where(inside, a, 0.0)

    def reverse(s_ref, g_ref, out_ref, v_ref, nb_ref, with_source, after=lambda: None):
        start = HALO - 2

        def step(k, c):
            z0 = start + UNROLL * k
            for j in range(0, UNROLL, 2):
                spread_rows(jnp.maximum(z0 - UNROLL - 1 + j, 1), g_ref, out_ref)
            zs = [z0 + j for j in range(UNROLL)]
            backward_rows(zs, s_ref, g_ref, v_ref, nb_ref, with_source)
            return c

        steps = (FR + 4) // UNROLL
        lax.fori_loop(0, steps, step, 0)
        after()
        for j in range(0, UNROLL, 2):
            spread_rows(start + UNROLL * steps - UNROLL - 1 + j, g_ref, out_ref)

    reverse(s1, g2, g1, v1, nb1, True)
    rim[0] = araw[HALO - 1]
    rim[1] = jnp.where(wide, araw[HALO + 16], araw[HALO + 8])

    pairs = jnp.concatenate(
        [v2[HALO + 2 * k] + v2[HALO + 2 * k + 1] for k in range(8)], axis=0
    )
    pairs_hi, pairs_lo = split(pairs)
    rest = (dot(pairs_hi, pool[...]) + dot(pairs_lo, pool[...])) * 0.125
    for k in range(8):
        for f in range(NF):
            rs[8 * f + k : 8 * f + k + 1, :] = rest[8 * k + f : 8 * k + f + 1]

    def rs_copy(t):
        return pltpu.make_async_remote_copy(
            src_ref=rs,
            dst_ref=gath.at[core, chip],
            send_sem=sem_rs.at[0, t],
            recv_sem=sem_rs.at[1, t],
            device_id={"patch": 2 * lax.rem(chip + t, CHIPS) + core},
            device_id_type=MESH,
        )

    def start_rs(t, c):
        rs_copy(t).start()
        return c

    lax.fori_loop(1, CHIPS, start_rs, 0)
    gath[core, chip] = rs[...]

    def r1_copy(t):
        k = lax.rem(w + t, GROUP)
        return pltpu.make_async_remote_copy(
            src_ref=pk.at[k],
            dst_ref=r1.at[w],
            send_sem=sem_r1s.at[t],
            recv_sem=sem_r1r.at[t],
            device_id={"patch": xg * GROUP + k},
            device_id_type=MESH,
        )

    def r2_copy(t):
        k = lax.rem(slot2 + t, 16)
        return pltpu.make_async_remote_copy(
            src_ref=r1sum,
            dst_ref=r2.at[slot2],
            send_sem=sem_r2s.at[t],
            recv_sem=sem_r2r.at[t],
            device_id={"patch": (k // 4) * GROUP + w, "dp": lax.rem(k, 4)},
            device_id_type=MESH,
        )

    def r3_copy(t):
        k = lax.rem(w + t, GROUP)
        return pltpu.make_async_remote_copy(
            src_ref=pall.at[w],
            dst_ref=pall.at[w],
            send_sem=sem_r3s.at[t],
            recv_sem=sem_r3r.at[t],
            device_id={"patch": xg * GROUP + k},
            device_id_type=MESH,
        )

    def send_parts():
        total = jnp.sum(gsum[...], axis=1, keepdims=True)
        tiles = [(p1, 8 * i) for i in range(9)]
        tiles += [(p1, FB_ROWS + 8 * i) for i in range(10)]
        tiles += [(p1, 2 * FB_ROWS + 8 * i) for i in range(9)]
        tiles += [(p2, 8 * i) for i in range(17)]
        tiles += [(p3, 0)]
        for i, (ref, at) in enumerate(tiles):
            pk[i // 3, 8 * (i % 3) : 8 * (i % 3) + 8, :] = ref[at : at + 8, :]
        pk[15, 8:16, :] = jnp.broadcast_to(total, (8, HID))
        pk[15, 16:24, :] = jnp.zeros((8, HID), F32)
        run(r1_copy, begin)

    reverse(s0, g1, gout, v0, nb0, False, send_parts)

    rim[0] = rim[0] + araw[HALO - 1]
    rim[1] = rim[1] + jnp.where(wide, araw[HALO + 16], araw[HALO + 8])
    rims = jnp.concatenate([rim[0], rim[1]], axis=0)
    rims_hi, rims_lo = split(rims)
    rims = dot(rims_hi, pool[...]) + dot(rims_lo, pool[...])
    rgs[...] = rims

    def rg_copy(e, dev, t):
        return pltpu.make_async_remote_copy(
            src_ref=rgs.at[pl.ds(8 * e, 8)],
            dst_ref=rg.at[e],
            send_sem=sem_rg_s.at[e, t],
            recv_sem=sem_rg_r.at[e],
            device_id={"patch": dev},
            device_id_type=MESH,
        )

    for e, who in ends:

        @pl.when(me == who)
        def _(e=e, who=who):
            def one(t, c):
                rg_copy(e, lax.rem(who + t, DEV), t).start()
                return c

            lax.fori_loop(1, DEV, one, 0)
            rg[e] = rgs[8 * e : 8 * e + 8, :]

    r1[w] = pk[w]
    run(r1_copy, end)

    def add_up(ref):
        out = ref[0]
        for k in range(1, 16):
            out = out + ref[k]
        return out

    r1sum[...] = add_up(r1)
    run(r2_copy, begin)

    def wait_rs(t, c):
        rs_copy(t).wait()
        return c

    lax.fori_loop(1, CHIPS, wait_rs, 0)
    gp_copy = pltpu.make_async_remote_copy(
        src_ref=gath.at[core],
        dst_ref=gath.at[core],
        send_sem=sem_gp.at[0],
        recv_sem=sem_gp.at[1],
        device_id={"patch": partner},
        device_id_type=MESH,
    )
    gp_copy.start()

    for i in range(FR):
        keep = (i < n)
        a = jnp.where(keep, v2[HALO + i], 0.0)
        b = jnp.where(keep, gout[HALO + i], 0.0)
        for f in range(NF):
            fine_out[f, i : i + 1, :] = a[f : f + 1]
            fine_adj[f, i : i + 1, :] = b[f : f + 1]
    departures = [
        pltpu.make_async_copy(src, dst, sem_out.at[i])
        for i, (src, dst) in enumerate(
            (
                (fine_out, fine_out_hbm),
                (fine_adj, fine_adj_hbm),
                (coarse_out, coarse_out_hbm),
                (coarse_adj, coarse_adj_hbm),
            )
        )
    ]
    departures[0].start()
    departures[1].start()

    r2[slot2] = r1sum[...]
    run(r2_copy, end)
    pall[w] = add_up(r2)
    run(r3_copy, begin)

    qi = grid((DEV, 512), 0)
    qc = grid((DEV, 512), 1)
    qd = 2 * ((qc % 256) // 8) + qc // 256
    counts = jnp.broadcast_to(fcv[...].astype(F32), (16, DEV)).astype(BF16)
    starts = dot(counts, (qi < qd).astype(F32).astype(BF16))
    sizes = dot(counts, (qi == qd).astype(F32).astype(BF16))
    qr = (grid((16, 512), 1) % 8).astype(F32)
    place = jnp.where(qr < 4.0 * sizes, 4.0 * starts + qr, -1.0)[0:1]
    off = off48[:, 0:1].astype(F32)
    onehot = (off == place).astype(F32).astype(BF16)

    gp_copy.wait()
    for f in range(NF):
        rows = gath[:, :, 8 * f : 8 * f + 8, :].reshape(512, CL)
        rows_hi, rows_lo = split(rows)
        pulled = dot(onehot, rows_hi) + dot(onehot, rows_lo)
        coarse_out[f] = jnp.where(in_region, pulled, upd[f])
    departures[2].start()

    for e, who in ends:

        @pl.when(me != who)
        def _(e=e):
            rg_copy(e, partner, 0).wait_recv()

        @pl.when(me == who)
        def _(e=e, who=who):
            def one(t, c):
                rg_copy(e, lax.rem(who + t, DEV), t).wait_send()
                return c

            lax.fori_loop(1, DEV, one, 0)

    for f in range(NF):
        coarse_adj[f] = (
            back[f]
            + jnp.where(row48 == low_local, rg[0, f : f + 1, :], 0.0)
            + jnp.where(row48 == high_local, rg[1, f : f + 1, :], 0.0)
        )

    departures[3].start()

    run(r3_copy, end)
    p_out[...] = pall[...]
    for copy in departures:
        copy.wait()


def finish(packed, ins, outs, w_in, b_in, w_mid, b_mid, w_out, b_out, sems):
    copies = [
        pltpu.make_async_copy(src, dst, sems.at[i])
        for i, (src, dst) in enumerate(zip(ins, outs))
    ]
    for copy in copies:
        copy.start()
    x = packed[...].reshape(PACKED, HID) * (1.0 / math.sqrt(4 * 96 * 8 * FL))
    hi = x.astype(BF16)
    rest = x - hi.astype(F32)
    mid = rest.astype(BF16)
    lo = (rest - mid.astype(F32)).astype(BF16)
    j = grid((27 * NF, 224), 0)
    at = j // NF * 8 + j % NF + jnp.where(j >= 18 * NF, 8, 0)
    take = bits(grid((27 * NF, 224), 1) == at)
    eye = bits(grid((HID, HID), 0) == grid((HID, HID), 1))

    def pull(product, a, b):
        return product(hi[a:b]) + product(mid[a:b]) + product(lo[a:b])

    w_in[...] = pull(lambda y: dot(take, y), 0, 224)
    w_mid[...] = pull(lambda y: dot_tn(y, eye), 224, 224 + HID)
    b_in[...] = x[144:145]
    b_mid[...] = x[352:353]
    w_out[...] = x[360:365]
    on = grid((8, HID), 0) == grid((8, HID), 1)
    b_out[...] = jnp.sum(jnp.where(on, x[368:376], 0.0), axis=0, keepdims=True)[:, 0:NF]
    for copy in copies:
        copy.wait()


def on_device(
    coarse_state,
    fine_state,
    coarse_cot,
    fine_cot,
    coarse_diffusion,
    w_in,
    b_in,
    w_mid,
    b_mid,
    w_out,
    b_out,
    coarse_counts,
    fine_counts,
    fine_anchor,
):
    vm = pltpu.VMEM
    slab = vm((EXT, 8, FL), F32)
    dma = pltpu.SemaphoreType.DMA
    in_vmem = pl.BlockSpec(memory_space=pltpu.VMEM)
    in_smem = pl.BlockSpec(memory_space=pltpu.SMEM)
    in_any = pl.BlockSpec(memory_space=pl.ANY)
    coarse_shape = jax.ShapeDtypeStruct((NF, CR, CL), F32)
    fine_shape = jax.ShapeDtypeStruct((NF, FR, FL), F32)
    whole = (coarse_shape, fine_shape, coarse_shape, fine_shape)
    big = [vm(x.shape, F32) for x in whole]
    *states, packed = pl.pallas_call(
        kernel,
        out_shape=whole + (jax.ShapeDtypeStruct((GROUP, PART, HID), F32),),
        in_specs=[in_smem] * 5 + [in_vmem] * 6 + [in_any] * 4,
        out_specs=(in_any,) * 4 + (in_vmem,),
        scratch_shapes=[
            *big,
            *big,
            vm((HID, 3 * FB_ROWS), BF16),
            vm((HID, HB), BF16),
            vm((16, HID), BF16),
            vm((2 * FB_ROWS, 4 * HID), BF16),
            vm((HID, HID), BF16),
            vm((HID, 16), BF16),
            vm((FL, CL), BF16),
            vm((CL, FL), BF16),
            dma((4,)),
            dma((4,)),
            pltpu.SMEM((DEV,), jnp.int32),
            slab,
            slab,
            slab,
            slab,
            slab,
            vm((EXT, FB_ROWS, FL), BF16),
            vm((EXT, FB_ROWS, FL), BF16),
            vm((UNROLL, HB, FL), BF16),
            vm((UNROLL, HID, FL), BF16),
            vm((UNROLL, HID, FL), F32),
            vm((EXT, HID, FL), BF16),
            vm((UNROLL, HID, FL), BF16),
            vm((UNROLL, 16, FL), BF16),
            slab,
            slab,
            slab,
            slab,
            vm((2, 8, FL), F32),
            vm((3 * FB_ROWS, HID), F32),
            vm((HB, HID), F32),
            vm((16, HID), F32),
            vm((8, FL), F32),
            vm((2, 4, 2, 4, GA_ROWS, CL), F32),
            vm((4, 2, 4, GA_ROWS, CL), F32),
            vm((4, 4, 2, GA_ROWS, 128), F32),
            vm((4, 2, 4, GA_ROWS, 128), F32),
            vm((4, 2, GA_ROWS, 128), F32),
            vm((2, 4, GA_ROWS, 128), F32),
            vm((8, GA_ROWS, 128), F32),
            vm((8, GA_ROWS, 128), F32),
            vm((2, 8, CL), F32),
            vm((2, 8, CL), F32),
            vm((NF, 8, FL), F32),
            vm((NF, 8, FL), F32),
            vm((NF, 8, FL), F32),
            vm((NF, 8, FL), F32),
            vm((16, CL), F32),
            vm((16, CL), F32),
            vm((16, CL), F32),
            vm((16, CL), F32),
            vm((NF, CR, CL), F32),
            vm((NF, CR, CL), F32),
            vm((2, 8, CL), F32),
            vm((DEV, 8, CL), F32),
            vm((8, CL), F32),
            vm((40, CL), F32),
            vm((2, CHIPS, 40, CL), F32),
            vm((16, CL), F32),
            vm((2, 8, CL), F32),
            vm((GROUP, PART, HID), F32),
            vm((GROUP, PART, HID), F32),
            vm((PART, HID), F32),
            vm((16, PART, HID), F32),
            vm((GROUP, PART, HID), F32),
            dma((2,)),
            dma((2, 4)),
            dma((2, 4)),
            dma((2, 8)),
            dma((2, 8)),
            dma((2, 2)),
            dma((2, 4)),
            dma((2,)),
            dma((DEV,)),
            dma((2, CHIPS)),
            dma((2,)),
            dma((2, DEV)),
            dma((2,)),
            dma((16,)),
            dma((16,)),
            dma((16,)),
            dma((16,)),
            dma((16,)),
            dma((16,)),
        ],
        compiler_params=pltpu.CompilerParams(
            collective_id=0, has_side_effects=True, vmem_limit_bytes=56 * 1024 * 1024
        ),
    )(
        fine_counts,
        coarse_counts,
        fine_anchor,
        coarse_diffusion,
        b_out,
        fine_counts.reshape(1, DEV),
        w_in.T,
        b_in.reshape(1, HID),
        w_mid,
        b_mid.reshape(1, HID),
        w_out,
        coarse_state[0],
        fine_state[0],
        coarse_cot[0],
        fine_cot[0],
    )
    *states, g_w_in, g_b_in, g_w_mid, g_b_mid, g_w_out, g_b_out = pl.pallas_call(
        lambda p, i0, i1, i2, i3, o0, o1, o2, o3, *rest: finish(
            p, (i0, i1, i2, i3), (o0, o1, o2, o3), *rest
        ),
        out_shape=whole
        + tuple(
            jax.ShapeDtypeStruct(shape, F32)
            for shape in (
                (27 * NF, HID),
                (1, HID),
                (HID, HID),
                (1, HID),
                (NF, HID),
                (1, NF),
            )
        ),
        in_specs=[in_vmem] * 5,
        out_specs=(in_any,) * 4 + (in_vmem,) * 6,
        scratch_shapes=[dma((4,))],
    )(packed, *states)
    return (
        *(x[None] for x in states),
        g_w_in.T,
        g_b_in[0],
        g_w_mid,
        g_b_mid[0],
        g_w_out,
        g_b_out[0],
    )


def solution(mesh):
    state = P("dp", None, "patch", None)
    return jax.shard_map(
        on_device,
        mesh=mesh,
        in_specs=(state,) * 4 + (P(),) * 10,
        out_specs=(state,) * 4 + (P(),) * 6,
        check_vma=False,
    )
```

```python
import math

import jax
import jax.numpy as jnp
from jax import lax
from jax.experimental import pallas as pl
from jax.experimental.pallas import tpu as pltpu
from jax.sharding import PartitionSpec as P

MESH = pl.DeviceIdType.MESH
F32 = jnp.float32
BF16 = jnp.bfloat16

DEV = 64
CHIPS = 32
CW = 16
FW = 32
CL = CW * CW
FL = FW * FW
CR = 48
FR = 16
NF = 5
CHAIN = 2048
REGION = 384
TAKEN = 4
HALO = TAKEN + 1
EXT = FR + 2 * HALO
UNROLL = 4
FB_ROWS = 80
HID = 128
HB = 144
GROUP = 16
PART = 24
PACKED = GROUP * PART
GA_ROWS = 40


def dot(a, b):
    return jnp.dot(a, b, preferred_element_type=F32)


def dot_nt(a, b):
    return lax.dot_general(a, b, (((1,), (1,)), ((), ())), preferred_element_type=F32)


def dot_tn(a, b):
    return lax.dot_general(a, b, (((0,), (0,)), ((), ())), preferred_element_type=F32)


def grid(shape, dim):
    return lax.broadcasted_iota(jnp.int32, shape, dim)


def bits(mask):
    return mask.astype(F32).astype(BF16)


def pieces(b):
    hi = b.astype(BF16).astype(F32)
    mid = (b - hi).astype(BF16).astype(F32)
    zeros = jnp.zeros((13, b.shape[1]), F32)
    return jnp.concatenate([hi, mid, b - hi - mid, zeros], axis=0).astype(BF16)


def split(x):
    hi = x.astype(BF16)
    return hi, (x - hi.astype(F32)).astype(BF16)


def shift_x(v, step, width):
    lanes = v.shape[1]
    col = grid((v.shape[0], 128), 1) % width
    parts = []
    for i in range(lanes // 128):
        s = v[:, 128 * i : 128 * (i + 1)]
        if step == 1:
            parts.append(
                jnp.where(
                    col == width - 1, pltpu.roll(s, width - 1, 1), pltpu.roll(s, 127, 1)
                )
            )
        else:
            parts.append(
                jnp.where(col == 0, pltpu.roll(s, 129 - width, 1), pltpu.roll(s, 1, 1))
            )
    return jnp.concatenate(parts, axis=1)


def shift_y(v, step, width):
    lanes = v.shape[1]
    return pltpu.roll(v, lanes - width if step == 1 else width, 1)


def neighbours(v, width):
    return (
        shift_y(v, -1, width)
        + shift_y(v, 1, width)
        + shift_x(v, -1, width)
        + shift_x(v, 1, width)
    )


def kernel(
    fc_smem,
    cc_smem,
    anchor_smem,
    cd_smem,
    bo_smem,
    fcv,
    win_ref,
    bin_ref,
    wmid_ref,
    bmid_ref,
    wout_ref,
    cst_hbm,
    fst_hbm,
    cct_hbm,
    fct_hbm,
    coarse_out_hbm,
    fine_out_hbm,
    coarse_adj_hbm,
    fine_adj_hbm,
    p_out,
    cst,
    fst,
    cct,
    fct,
    coarse_out,
    fine_out,
    coarse_adj,
    fine_adj,
    w1,
    w2,
    w3,
    wp,
    w2t,
    w3t,
    pool,
    pool_t,
    sem_in,
    sem_out,
    base_s,
    v0,
    v1,
    v2,
    nb0,
    nb1,
    s0,
    s1,
    a1,
    a2,
    sl1,
    d1,
    d2,
    sbv,
    g2,
    g1,
    araw,
    gout,
    rim,
    p1,
    p2,
    p3,
    gsum,
    sendb,
    pairb,
    ga_a,
    ga_b,
    sum_a,
    sum_b,
    ga_a2,
    ga_b2,
    gh,
    gr,
    hs_dn,
    hs_up,
    hr_lo,
    hr_hi,
    cs_dn,
    cs_up,
    cr_lo,
    cr_hi,
    upd,
    back,
    rim_src,
    rim_got,
    rim_row_ref,
    rs,
    gath,
    rgs,
    rg,
    pk,
    r1,
    r1sum,
    r2,
    r2sum,
    rd,
    pall,
    sem_pair,
    sem_a1,
    sem_b1,
    sem_a2,
    sem_b2,
    sem_edge,
    sem_halo,
    sem_rim_s,
    sem_rim_r,
    sem_rs,
    sem_gp,
    sem_rg_s,
    sem_rg_r,
    sem_r1s,
    sem_r1r,
    sem_r2s,
    sem_r2r,
    sem_rds,
    sem_rdr,
    sem_r3s,
    sem_r3r,
):
    me = lax.axis_index("patch")
    dp = lax.axis_index("dp")
    core = lax.rem(me, 2)
    chip = me // 2
    partner = chip * 2 + (1 - core)
    nxt = lax.rem(me + 1, DEV)
    prv = lax.rem(me + DEV - 1, DEV)

    xg = me // GROUP
    w = lax.rem(me, GROUP)
    cx, czy = chip // 8, lax.rem(chip, 8)
    cy, cxz = lax.rem(chip, 4), chip // 4
    arrivals = [
        pltpu.make_async_copy(src, dst, sem_in.at[i])
        for i, (src, dst) in enumerate(
            ((cst_hbm, cst), (fst_hbm, fst), (cct_hbm, cct), (fct_hbm, fct))
        )
    ]
    for copy in arrivals:
        copy.start()

    barrier = pltpu.get_barrier_semaphore()

    def greet(t, c):
        pl.semaphore_signal(
            barrier, inc=1, device_id={"patch": lax.rem(me + t, DEV)}, device_id_type=MESH
        )
        return c

    lax.fori_loop(1, DEV, greet, 0)

    def greet_dp(t, c):
        pl.semaphore_signal(
            barrier,
            inc=1,
            device_id={"patch": me, "dp": lax.rem(dp + t, 4)},
            device_id_type=MESH,
        )
        return c

    lax.fori_loop(1, 4, greet_dp, 0)

    col = grid((27 * NF, 3 * FB_ROWS), 1)
    row = grid((27 * NF, 3 * FB_ROWS), 0)
    part, field = col % FB_ROWS // 8, col % 8
    place = (col // FB_ROWS * 9 + part) * NF + field
    laid = dot_tn(win_ref[...], bits((row == place) & (part < 9) & (field < NF)))
    brow, bcol = grid((16, 3 * FB_ROWS), 0), grid((16, 3 * FB_ROWS), 1)
    bias = dot_tn(pieces(bin_ref[...]), bits((bcol == FB_ROWS + 72 + brow) & (brow < 3)))
    w1[...] = ((laid + bias) * 0.5).astype(BF16)
    qrow, qcol = grid((FB_ROWS, 27 * NF), 0), grid((FB_ROWS, 27 * NF), 1)
    wp[...] = jnp.zeros_like(wp)
    for a in range(3):
        take = (qcol == (a * 9 + qrow // 8) * NF + qrow % 8) & (qrow < 72) & (qrow % 8 < NF)
        turned = dot(bits(take), win_ref[...]).astype(BF16)
        for j in range(2):
            m = j + 2 - a
            wp[FB_ROWS * j : FB_ROWS * (j + 1), HID * m : HID * (m + 1)] = turned
    eye = bits(grid((HID, HID), 0) == grid((HID, HID), 1))
    eye16 = bits(grid((16, 16), 0) == grid((16, 16), 1))
    w2[:, 0:HID] = (wmid_ref[...].astype(F32) * 0.5).astype(BF16)
    w2[:, HID:HB] = (dot_tn(pieces(bmid_ref[...]), eye16) * 0.5).astype(BF16)
    w2t[...] = (dot_nt(eye, wmid_ref[...]) * 0.5).astype(BF16)
    w3[...] = dot(bits(grid((16, NF), 0) == grid((16, NF), 1)), wout_ref[...]).astype(BF16)
    w3t[...] = (dot_nt(eye, w3[...]) * 0.5).astype(BF16)
    fine_cell, coarse_cell = grid((FL, CL), 0), grid((FL, CL), 1)
    pool[...] = bits(fine_cell // (2 * FW) * CW + fine_cell % FW // 2 == coarse_cell)
    coarse_cell, fine_cell = grid((CL, FL), 0), grid((CL, FL), 1)
    pool_t[...] = bits(fine_cell // (2 * FW) * CW + fine_cell % FW // 2 == coarse_cell)
    field_row = grid((8, FL), 0)
    kf = jnp.zeros((8, FL), F32)
    half_bias = jnp.zeros((8, FL), F32)
    for f in range(NF):
        kf = jnp.where(field_row == f, 2.0 * cd_smem[f], kf)
        half_bias = jnp.where(field_row == f, 0.5 * bo_smem[f], half_bias)
    for copy in arrivals:
        copy.wait()

    anchor = anchor_smem[0]

    def count(d, carry):
        fs, cs = carry
        base_s[d] = fs
        fs = fs + fc_smem[d]
        cs = cs + jnp.where(d < me, cc_smem[d], 0)
        return (fs, cs)

    _, cpatch = lax.fori_loop(0, DEV, count, (jnp.int32(0), jnp.int32(0)))
    cstart = cpatch * CW
    nc = cc_smem[me] * CW
    n = fc_smem[me] * 8
    wide = n == FR
    first = me == 0
    last = me == DEV - 1

    def wrap(x):
        return lax.rem(x + 2 * CHAIN + CHAIN // 2, CHAIN) - CHAIN // 2

    def live_or_none(local):
        return jnp.where((local >= 0) & (local < nc), local, -10000)

    low_local = live_or_none(wrap(anchor - 1 - cstart))
    high_local = live_or_none(wrap(anchor + REGION - cstart))

    row48 = grid((CR, CL), 0)
    live48 = row48 < nc
    off48 = lax.rem(row48 + (cstart - anchor + 2 * CHAIN), CHAIN)
    in_region = (off48 < REGION) & live48

    for f in range(NF):
        hs_dn[f, 0:4, :] = fst[f, 0:4, :]
        hs_dn[f, 4:8, :] = fct[f, 0:4, :]
        hs_up[f, 0:4, :] = jnp.where(wide, fst[f, 12:16, :], fst[f, 4:8, :])
        hs_up[f, 4:8, :] = jnp.where(wide, fct[f, 12:16, :], fct[f, 4:8, :])
    cs_dn[...] = jnp.zeros_like(cs_dn)
    cs_up[...] = jnp.zeros_like(cs_up)
    for f in range(NF):
        kept = jnp.where(in_region, 0.0, cct[f])
        cs_dn[f : f + 1, :] = cst[f, 0:1, :]
        cs_dn[8 + f : 9 + f, :] = kept[0:1]
        cs_up[f : f + 1, :] = jnp.where(
            nc == 48,
            cst[f, 47:48, :],
            jnp.where(nc == 32, cst[f, 31:32, :], cst[f, 15:16, :]),
        )
        cs_up[8 + f : 9 + f, :] = jnp.where(
            nc == 48, kept[47:48], jnp.where(nc == 32, kept[31:32], kept[15:16])
        )

    def neighbour_copies():
        def one(src, dst, k, dev):
            return pltpu.make_async_remote_copy(
                src_ref=src,
                dst_ref=dst,
                send_sem=sem_halo.at[0, k],
                recv_sem=sem_halo.at[1, k],
                device_id={"patch": dev},
                device_id_type=MESH,
            )

        return (
            one(hs_up, hr_lo, 0, nxt),
            one(hs_dn, hr_hi, 1, prv),
            one(cs_up, cr_lo, 2, nxt),
            one(cs_dn, cr_hi, 3, prv),
        )

    cot = jnp.concatenate([jnp.where(live48, cct[f], 0.0) for f in range(NF)], axis=0)
    cot_hi, cot_lo = split(cot)
    cot2 = jnp.concatenate([cot_hi, cot_lo], axis=1)
    srow = grid((GA_ROWS, NF * CR), 0)
    scol = grid((GA_ROWS, NF * CR), 1)
    pick = jnp.where(
        scol // CR == srow % NF, scol % CR - srow // NF, 99999
    )

    def rows_for(c2):
        def one(i, c):
            hot = []
            for k in range(8):
                base = wrap(anchor + 4 * base_s[2 * (8 * i + k) + c2] - cstart)
                hot.append((pick == base).astype(F32))
            both = dot(jnp.concatenate(hot, axis=0).astype(BF16), cot2)
            both = both[:, :CL] + both[:, CL:]
            sendb[c2, i] = both.reshape(2, 4, GA_ROWS, CL)
            return c

        lax.fori_loop(0, CHIPS // 8, one, 0)

    ust = jnp.concatenate([cst[f] for f in range(NF)], axis=0)
    ust_hi, ust_lo = split(ust)
    ust2 = jnp.concatenate([ust_hi, ust_lo], axis=1)
    frow = grid((16, NF * CR), 0)
    fcol = grid((16, NF * CR), 1)
    fpick = jnp.where(fcol // CR == frow, fcol % CR, 99999)
    for e, local in ((0, low_local), (1, high_local)):
        both = dot(bits(fpick == local), ust2)
        rim_src[e] = (both[:, :CL] + both[:, CL:])[0:8]

    ones8 = jnp.ones((8, FL), F32)

    def build_features(s_ref, nb_ref, z, v):
        xm = shift_x(v, -1, FW)
        xp = shift_x(v, 1, FW)
        xs = jnp.concatenate([xm, v, xp], axis=0)
        ym = shift_y(xs, -1, FW)
        yp = shift_y(xs, 1, FW)
        s_ref[z] = jnp.concatenate([ym, xs, yp, ones8], axis=0).astype(BF16)
        nb_ref[z] = ym[8:16] + yp[8:16] + xm + xp - 6.0 * v

    for j in range(UNROLL):
        a1[j, HID:HB, :] = jnp.ones((HB - HID, FL), BF16)
    p1[...] = jnp.zeros_like(p1)
    p2[...] = jnp.zeros_like(p2)
    p3[...] = jnp.zeros_like(p3)
    gsum[...] = jnp.zeros_like(gsum)
    v0[...] = jnp.zeros_like(v0)
    g2[...] = jnp.zeros_like(g2)
    for z in (0, EXT - 1):
        s0[z] = jnp.zeros((FB_ROWS, FL), BF16)
        v1[z] = jnp.zeros((8, FL), F32)
    for z in range(EXT - 4, EXT):
        g1[z] = jnp.zeros((8, FL), F32)

    for src, dst in ((fst, v0), (fct, g2)):
        for f in range(NF):
            for i in range(FR):
                line = src[f, i : i + 1, :]
                dst[HALO + i, f : f + 1, :] = line if i < 8 else jnp.where(wide, line, 0.0)

    def features_first(k, c):
        for j in range(UNROLL):
            z = 1 + UNROLL * k + j
            build_features(s0, nb0, z, v0[z])
        return c

    rows_for(1 - core)

    pl.semaphore_wait(barrier, DEV - 1 + 3)

    halo_copies = neighbour_copies()
    for copy in halo_copies:
        copy.start()

    def rim_copy(e, sender):
        return pltpu.make_async_remote_copy(
            src_ref=rim_src.at[e],
            dst_ref=rim_got.at[sender],
            send_sem=sem_rim_s.at[e],
            recv_sem=sem_rim_r.at[sender],
            device_id={"patch": (DEV - 1) * e},
            device_id_type=MESH,
        )

    ends = ((0, 0), (1, DEV - 1))
    for e, who in ends:

        @pl.when(me != who)
        def _(e=e):
            rim_copy(e, me).start()

    pair_copy = pltpu.make_async_remote_copy(
        src_ref=sendb.at[1 - core],
        dst_ref=pairb,
        send_sem=sem_pair.at[0],
        recv_sem=sem_pair.at[1],
        device_id={"patch": partner},
        device_id_type=MESH,
    )
    pair_copy.start()
    rows_for(core)
    lax.fori_loop(1, 3, features_first, 0)

    pair_copy.wait()

    def add_pair(k, c):
        sendb[core, k] = sendb[core, k] + pairb[k]
        return c

    lax.fori_loop(0, 4, add_pair, 0)

    def chip_copy(src, dst, sems, t, to):
        return pltpu.make_async_remote_copy(
            src_ref=src,
            dst_ref=dst,
            send_sem=sems.at[0, t],
            recv_sem=sems.at[1, t],
            device_id={"patch": 2 * to + core},
            device_id_type=MESH,
        )

    def a1_copy(t):
        k = lax.rem(cy + t, 4)
        src = sendb.at[core, :, :, k, :, 0:128]
        return chip_copy(src, ga_a.at[cy], sem_a1, t, cxz * 4 + k)

    def b1_copy(t):
        k = lax.rem(cx + t, 4)
        src = sendb.at[core, k, :, :, :, 128:256]
        return chip_copy(src, ga_b.at[cx], sem_b1, t, k * 8 + czy)

    def a2_copy(t):
        k = lax.rem(cxz + t, 8)
        src = sum_a.at[k // 2, lax.rem(k, 2)]
        return chip_copy(src, ga_a2.at[cxz], sem_a2, t, k * 4 + cy)

    def b2_copy(t):
        k = lax.rem(czy + t, 8)
        src = sum_b.at[k // 4, lax.rem(k, 4)]
        return chip_copy(src, ga_b2.at[czy], sem_b2, t, cx * 8 + k)

    def run(make, what, count=16):
        def one(t, c):
            what(make(t))
            return c

        lax.fori_loop(1, count, one, 0)

    def begin(copy):
        copy.start()

    def end(copy):
        copy.wait()

    run(a1_copy, begin, 4)
    run(b1_copy, begin, 4)

    halo_copies[0].wait()
    halo_copies[1].wait()
    for at, dst in ((0, v0), (4, g2)):
        for f in range(NF):
            one = slice(f, f + 1)
            for i in range(TAKEN):
                hi = hr_hi[f, at + i : at + i + 1, :]
                dst[1 + i, one, :] = hr_lo[f, at + i : at + i + 1, :]
                dst[HALO + 8 + i, one, :] = jnp.where(wide, dst[HALO + 8 + i, one, :], hi)
                dst[HALO + 16 + i, one, :] = jnp.where(wide, hi, 0.0)

    rim_row_ref[...] = jnp.zeros_like(rim_row_ref)
    for e, who in ends:

        @pl.when(me != who)
        def _(e=e):
            rim_copy(e, me).wait_send()

        @pl.when(me == who)
        def _(e=e, who=who):
            rim_row_ref[...] = rim_src[e]

            def one(t, c):
                s = lax.rem(who + t, DEV)
                rim_copy(e, s).wait_recv()
                rim_row_ref[...] = rim_row_ref[...] + rim_got[s]
                return c

            lax.fori_loop(1, DEV, one, 0)

    rim_hi, rim_lo = split(rim_row_ref[...])
    beside = dot(rim_hi, pool_t[...]) + dot(rim_lo, pool_t[...])
    v0[HALO - 1] = jnp.where(first, beside, v0[HALO - 1])
    v0[HALO + 8] = jnp.where(last & ~wide, beside, v0[HALO + 8])
    v0[HALO + 16] = jnp.where(last & wide, beside, v0[HALO + 16])

    steps_all = (EXT - 2) // UNROLL
    lax.fori_loop(0, 1, features_first, 0)
    lax.fori_loop(3, steps_all, features_first, 0)

    def rim_row(z):
        return (first & (z < HALO)) | (last & (z >= HALO + n))

    def advance(z, v, nb, source):
        lap = v[z - 1] + v[z + 1] + nb[z]
        return v[z] + kf * lap + (0.5 * source[0:8] + half_bias)

    def features_of(s_ref, z):
        return s_ref[pl.ds(z - 1, 3)].reshape(3 * FB_ROWS, FL)

    def forward_rows(k, c):
        rows = [(j, 1 + UNROLL * k + j) for j in range(UNROLL)]
        for _, z in rows:
            before = jnp.maximum(z - UNROLL, 0)
            build_features(s1, nb1, before, v1[before])
        for j, z in rows:
            h = dot(w1[...], features_of(s0, z))
            a1[j, 0:HID, :] = (h + h * jnp.tanh(h)).astype(BF16)
        for j, z in rows:
            h = dot(w2[...], a1[j])
            a2[j] = (h + h * jnp.tanh(h)).astype(BF16)
        for j, z in rows:
            new = advance(z, v0, nb0, dot(w3[...], a2[j]))
            v1[z] = jnp.where(rim_row(z), v0[z], new)
        return c

    lax.fori_loop(0, 3, forward_rows, 0)

    ga_a[cy] = sendb[core, :, :, cy, :, 0:128]
    ga_b[cx] = sendb[core, cx, :, :, :, 128:256]
    run(a1_copy, end, 4)
    run(b1_copy, end, 4)
    sum_a[...] = ga_a[0] + ga_a[1] + ga_a[2] + ga_a[3]
    sum_b[...] = ga_b[0] + ga_b[1] + ga_b[2] + ga_b[3]
    run(a2_copy, begin, 8)
    run(b2_copy, begin, 8)

    lax.fori_loop(3, 5, forward_rows, 0)
    ga_a2[cxz] = sum_a[cxz // 2, lax.rem(cxz, 2)]
    ga_b2[czy] = sum_b[czy // 4, lax.rem(czy, 4)]
    run(a2_copy, end, 8)
    run(b2_copy, end, 8)
    parts = []
    for ref in (ga_a2, ga_b2):
        part = ref[0]
        for k in range(1, 8):
            part = part + ref[k]
        parts.append(part)
    region = jnp.concatenate(parts, axis=1)
    blank = jnp.zeros((3, CL), F32)
    gh[0] = jnp.concatenate([region[0:5], blank], axis=0)
    gh[1] = jnp.concatenate([jnp.where(wide, region[35:40], region[15:20]), blank], axis=0)

    def edge_copy(k, to):
        return pltpu.make_async_remote_copy(
            src_ref=gh.at[k],
            dst_ref=gr.at[k],
            send_sem=sem_edge.at[0, k],
            recv_sem=sem_edge.at[1, k],
            device_id={"patch": to},
            device_id_type=MESH,
        )

    edges = (edge_copy(0, prv), edge_copy(1, nxt))
    for copy in edges:
        copy.start()

    lax.fori_loop(5, steps_all, forward_rows, 0)
    for z in range(EXT - 1 - UNROLL, EXT - 1):
        build_features(s1, nb1, z, v1[z])

    def lift(x):
        hi, lo = split(x)
        return (dot(hi, pool_t[...]) + dot(lo, pool_t[...])) * 0.125

    lifted = lift(region)
    for r in range(8):
        for i in (HALO + 2 * r, HALO + 2 * r + 1):
            g2[i, 0:5, :] = g2[i, 0:5, :] + jnp.where(2 * r < n, lifted[5 * r : 5 * r + 5], 0.0)
    for copy in edges:
        copy.wait()
    lifted = lift(jnp.concatenate([gr[0], gr[1]], axis=0))
    for i in (HALO - 2, HALO - 1):
        g2[i] = g2[i] + lifted[8:16]
    for i in (HALO + 8, HALO + 9):
        g2[i] = g2[i] + jnp.where(wide, 0.0, lifted[0:8])
    for i in (HALO + 16, HALO + 17):
        g2[i] = g2[i] + jnp.where(wide, lifted[0:8], 0.0)

    def level_row(z):
        return ~(rim_row(z)) & (z < HALO + n + 2)

    def mask_g2(z, c):
        g2[z] = jnp.where(level_row(z) & (z >= HALO - 2), g2[z], 0.0)
        return c

    lax.fori_loop(0, EXT, mask_g2, 0)

    def backward_rows(zs, s_ref, g_ref, v_ref, nb_ref, with_source):
        rows = list(enumerate(zs))
        own = [(z >= HALO) & (z < HALO + n) for z in zs]
        for j, z in rows:
            half = 0.5 * g_ref[z]
            gsum[...] = gsum[...] + jnp.where(own[j], half, 0.0)
            sbv[j] = jnp.concatenate([half, jnp.zeros_like(half)], axis=0).astype(BF16)
        for j, z in rows:
            h = dot(w1[...], features_of(s_ref, z))
            t = jnp.tanh(h)
            u = h * t
            a1[j, 0:HID, :] = (h + u).astype(BF16)
            sl1[j] = (1.0 + t) * (1.0 + h - u)
        for j, z in rows:
            h = dot(w2[...], a1[j])
            t = jnp.tanh(h)
            u = h * t
            a2[j] = (h + u).astype(BF16)
            d2[j] = (dot(w3t[...], sbv[j]) * ((1.0 + t) * (1.0 + h - u))).astype(BF16)
        for j, z in rows:
            d1[z] = (dot(w2t[...], d2[j]) * sl1[j]).astype(BF16)
        for j, z in rows:
            p1[...] = p1[...] + jnp.where(own[j], dot_nt(features_of(s_ref, z), d1[z]), 0.0)
            p2[...] = p2[...] + jnp.where(own[j], dot_nt(a1[j], d2[j]), 0.0)
            p3[...] = p3[...] + jnp.where(own[j], dot_nt(sbv[j], a2[j]), 0.0)
            if with_source:
                v2[z] = advance(z, v_ref, nb_ref, dot(w3[...], a2[j]))

    def spread_rows(r0, g_ref, out_ref):
        both = dot(wp[...], d1[pl.ds(r0 - 1, 4)].reshape(4 * HID, FL))
        for j in range(2):
            r = r0 + j
            acc = both[FB_ROWS * j : FB_ROWS * (j + 1)]
            g = g_ref[r]
            kg = kf * g
            lo = jnp.concatenate([acc[0:8], acc[8:16] + kg, acc[16:24]], axis=0)
            mid = jnp.concatenate([acc[24:32] + kg, acc[32:40], acc[40:48] + kg], axis=0)
            hi = jnp.concatenate([acc[48:56], acc[56:64] + kg, acc[64:72]], axis=0)
            xs = shift_y(lo, 1, FW) + mid + shift_y(hi, -1, FW)
            moved = shift_x(xs[0:8], 1, FW) + xs[8:16] + shift_x(xs[16:24], -1, FW)
            a = g + kf * (g_ref[r - 1] + g_ref[r + 1] - 6.0 * g) + moved
            araw[r] = a
            inside = level_row(r) & (r >= HALO - 1) & (r < HALO + n + 1)
            out_ref[r] = jnp.where(inside, a, 0.0)

    start = HALO - 2
    steps = (FR + 4) // UNROLL

    def reverse(first_spread, s_ref, g_ref, out_ref, v_ref, nb_ref, with_source):
        def rows_at(z0):
            zs = [z0 + j for j in range(UNROLL)]
            backward_rows(zs, s_ref, g_ref, v_ref, nb_ref, with_source)

        def step(k, c):
            z0 = start + UNROLL * k
            for j in range(0, UNROLL, 2):
                spread_rows(z0 - UNROLL - 1 + j, g_ref, out_ref)
            rows_at(z0)
            return c

        first_spread()
        rows_at(start)
        lax.fori_loop(1, steps, step, 0)

    def last_spread(g_ref, out_ref):
        for j in range(0, UNROLL, 2):
            spread_rows(start + UNROLL * steps - UNROLL - 1 + j, g_ref, out_ref)

    def second_rest():
        last_spread(g2, g1)
        rim[0] = araw[HALO - 1]
        rim[1] = jnp.where(wide, araw[HALO + 16], araw[HALO + 8])

    reverse(lambda: None, s1, g2, g1, v1, nb1, True)

    pairs = jnp.concatenate(
        [v2[HALO + 2 * k] + v2[HALO + 2 * k + 1] for k in range(8)], axis=0
    )
    pairs_hi, pairs_lo = split(pairs)
    rest = (dot(pairs_hi, pool[...]) + dot(pairs_lo, pool[...])) * 0.125
    for k in range(8):
        for f in range(NF):
            rs[8 * f + k : 8 * f + k + 1, :] = rest[8 * k + f : 8 * k + f + 1]

    def rs_copy(t):
        return pltpu.make_async_remote_copy(
            src_ref=rs,
            dst_ref=gath.at[core, chip],
            send_sem=sem_rs.at[0, t],
            recv_sem=sem_rs.at[1, t],
            device_id={"patch": 2 * lax.rem(chip + t, CHIPS) + core},
            device_id_type=MESH,
        )

    def start_rs(t, c):
        rs_copy(t).start()
        return c

    lax.fori_loop(1, CHIPS, start_rs, 0)
    gath[core, chip] = rs[...]

    def r1_copy(t):
        k = lax.rem(w + t, GROUP)
        return pltpu.make_async_remote_copy(
            src_ref=pk.at[k],
            dst_ref=r1.at[w],
            send_sem=sem_r1s.at[t],
            recv_sem=sem_r1r.at[t],
            device_id={"patch": xg * GROUP + k},
            device_id_type=MESH,
        )

    def r2_copy(t):
        return pltpu.make_async_remote_copy(
            src_ref=r1sum,
            dst_ref=r2.at[xg],
            send_sem=sem_r2s.at[t],
            recv_sem=sem_r2r.at[t],
            device_id={"patch": lax.rem(xg + t, 4) * GROUP + w},
            device_id_type=MESH,
        )

    def rd_copy(t):
        return pltpu.make_async_remote_copy(
            src_ref=r2sum,
            dst_ref=rd.at[dp],
            send_sem=sem_rds.at[t],
            recv_sem=sem_rdr.at[t],
            device_id={"patch": me, "dp": lax.rem(dp + t, 4)},
            device_id_type=MESH,
        )

    def r3_copy(t):
        k = lax.rem(w + t, GROUP)
        return pltpu.make_async_remote_copy(
            src_ref=pall.at[w],
            dst_ref=pall.at[w],
            send_sem=sem_r3s.at[t],
            recv_sem=sem_r3r.at[t],
            device_id={"patch": xg * GROUP + k},
            device_id_type=MESH,
        )

    def send_parts():
        total = jnp.sum(gsum[...], axis=1, keepdims=True)
        tiles = [(p1, 8 * i) for i in range(9)]
        tiles += [(p1, FB_ROWS + 8 * i) for i in range(10)]
        tiles += [(p1, 2 * FB_ROWS + 8 * i) for i in range(9)]
        tiles += [(p2, 8 * i) for i in range(17)]
        tiles += [(p3, 0)]
        for i, (ref, at) in enumerate(tiles):
            pk[i // 3, 8 * (i % 3) : 8 * (i % 3) + 8, :] = ref[at : at + 8, :]
        pk[15, 8:16, :] = jnp.broadcast_to(total, (8, HID))
        pk[15, 16:24, :] = jnp.zeros((8, HID), F32)
        run(r1_copy, begin)

    reverse(second_rest, s0, g1, gout, v0, nb0, False)
    send_parts()
    last_spread(g1, gout)

    rim[0] = rim[0] + araw[HALO - 1]
    rim[1] = rim[1] + jnp.where(wide, araw[HALO + 16], araw[HALO + 8])
    rims = jnp.concatenate([rim[0], rim[1]], axis=0)
    rims_hi, rims_lo = split(rims)
    rims = dot(rims_hi, pool[...]) + dot(rims_lo, pool[...])
    rgs[...] = rims

    def rg_copy(e, dev, t):
        return pltpu.make_async_remote_copy(
            src_ref=rgs.at[pl.ds(8 * e, 8)],
            dst_ref=rg.at[e],
            send_sem=sem_rg_s.at[e, t],
            recv_sem=sem_rg_r.at[e],
            device_id={"patch": dev},
            device_id_type=MESH,
        )

    for e, who in ends:

        @pl.when(me == who)
        def _(e=e, who=who):
            def one(t, c):
                rg_copy(e, lax.rem(who + t, DEV), t).start()
                return c

            lax.fori_loop(1, DEV, one, 0)
            rg[e] = rgs[8 * e : 8 * e + 8, :]

    halo_copies[2].wait()
    halo_copies[3].wait()
    for f in range(NF):
        kappa = cd_smem[f]
        for src, lo, hi, dst in (
            (jnp.where(live48, cst[f], 0.0), cr_lo[f : f + 1], cr_hi[f : f + 1], upd),
            (
                jnp.where(in_region | ~live48, 0.0, cct[f]),
                cr_lo[8 + f : 9 + f],
                cr_hi[8 + f : 9 + f],
                back,
            ),
        ):
            below = jnp.where(row48 == 0, lo, pltpu.roll(src, 1, 0))
            above = jnp.where(row48 == nc - 1, hi, pltpu.roll(src, CR - 1, 0))
            new = src + kappa * (below + above + neighbours(src, CW) - 6.0 * src)
            dst[f] = jnp.where(live48, new, 0.0)

    r1[w] = pk[w]
    run(r1_copy, end)

    def add_up(ref, count):
        out = ref[0]
        for k in range(1, count):
            out = out + ref[k]
        return out

    r1sum[...] = add_up(r1, GROUP)
    run(r2_copy, begin, 4)

    def wait_rs(t, c):
        rs_copy(t).wait()
        return c

    lax.fori_loop(1, CHIPS, wait_rs, 0)
    gp_copy = pltpu.make_async_remote_copy(
        src_ref=gath.at[core],
        dst_ref=gath.at[core],
        send_sem=sem_gp.at[0],
        recv_sem=sem_gp.at[1],
        device_id={"patch": partner},
        device_id_type=MESH,
    )
    gp_copy.start()

    r2[xg] = r1sum[...]
    run(r2_copy, end, 4)
    r2sum[...] = add_up(r2, 4)
    run(rd_copy, begin, 4)

    for i in range(FR):
        keep = (i < n)
        a = jnp.where(keep, v2[HALO + i], 0.0)
        b = jnp.where(keep, gout[HALO + i], 0.0)
        for f in range(NF):
            fine_out[f, i : i + 1, :] = a[f : f + 1]
            fine_adj[f, i : i + 1, :] = b[f : f + 1]
    departures = [
        pltpu.make_async_copy(src, dst, sem_out.at[i])
        for i, (src, dst) in enumerate(
            (
                (fine_out, fine_out_hbm),
                (fine_adj, fine_adj_hbm),
                (coarse_out, coarse_out_hbm),
                (coarse_adj, coarse_adj_hbm),
            )
        )
    ]
    departures[0].start()
    departures[1].start()

    rd[dp] = r2sum[...]
    run(rd_copy, end, 4)
    pall[w] = add_up(rd, 4)
    run(r3_copy, begin)

    qi = grid((DEV, 512), 0)
    qc = grid((DEV, 512), 1)
    qd = 2 * ((qc % 256) // 8) + qc // 256
    counts = jnp.broadcast_to(fcv[...].astype(F32), (16, DEV)).astype(BF16)
    starts = dot(counts, (qi < qd).astype(F32).astype(BF16))
    sizes = dot(counts, (qi == qd).astype(F32).astype(BF16))
    qr = (grid((16, 512), 1) % 8).astype(F32)
    place = jnp.where(qr < 4.0 * sizes, 4.0 * starts + qr, -1.0)[0:1]
    off = off48[:, 0:1].astype(F32)
    onehot = (off == place).astype(F32).astype(BF16)

    gp_copy.wait()
    for f in range(NF):
        rows = gath[:, :, 8 * f : 8 * f + 8, :].reshape(512, CL)
        rows_hi, rows_lo = split(rows)
        pulled = dot(onehot, rows_hi) + dot(onehot, rows_lo)
        coarse_out[f] = jnp.where(in_region, pulled, upd[f])
    departures[2].start()

    for e, who in ends:

        @pl.when(me != who)
        def _(e=e):
            rg_copy(e, partner, 0).wait_recv()

        @pl.when(me == who)
        def _(e=e, who=who):
            def one(t, c):
                rg_copy(e, lax.rem(who + t, DEV), t).wait_send()
                return c

            lax.fori_loop(1, DEV, one, 0)

    for f in range(NF):
        coarse_adj[f] = (
            back[f]
            + jnp.where(row48 == low_local, rg[0, f : f + 1, :], 0.0)
            + jnp.where(row48 == high_local, rg[1, f : f + 1, :], 0.0)
        )

    departures[3].start()

    run(r3_copy, end)
    p_out[...] = pall[...]
    for copy in departures:
        copy.wait()


def finish(packed, ins, outs, w_in, b_in, w_mid, b_mid, w_out, b_out, sems):
    copies = [
        pltpu.make_async_copy(src, dst, sems.at[i])
        for i, (src, dst) in enumerate(zip(ins, outs))
    ]
    for copy in copies:
        copy.start()
    x = packed[...].reshape(PACKED, HID) * (1.0 / math.sqrt(4 * 96 * 8 * FL))
    hi = x.astype(BF16)
    rest = x - hi.astype(F32)
    mid = rest.astype(BF16)
    lo = (rest - mid.astype(F32)).astype(BF16)
    j = grid((27 * NF, 224), 0)
    at = j // NF * 8 + j % NF + jnp.where(j >= 18 * NF, 8, 0)
    take = bits(grid((27 * NF, 224), 1) == at)
    eye = bits(grid((HID, HID), 0) == grid((HID, HID), 1))

    def pull(product, a, b):
        return product(hi[a:b]) + product(mid[a:b]) + product(lo[a:b])

    w_in[...] = pull(lambda y: dot(take, y), 0, 224)
    w_mid[...] = pull(lambda y: dot_tn(y, eye), 224, 224 + HID)
    b_in[...] = x[144:145]
    b_mid[...] = x[352:353]
    w_out[...] = x[360:365]
    on = grid((8, HID), 0) == grid((8, HID), 1)
    b_out[...] = jnp.sum(jnp.where(on, x[368:376], 0.0), axis=0, keepdims=True)[:, 0:NF]
    for copy in copies:
        copy.wait()


def on_device(
    coarse_state,
    fine_state,
    coarse_cot,
    fine_cot,
    coarse_diffusion,
    w_in,
    b_in,
    w_mid,
    b_mid,
    w_out,
    b_out,
    coarse_counts,
    fine_counts,
    fine_anchor,
):
    vm = pltpu.VMEM
    slab = vm((EXT, 8, FL), F32)
    dma = pltpu.SemaphoreType.DMA
    in_vmem = pl.BlockSpec(memory_space=pltpu.VMEM)
    in_smem = pl.BlockSpec(memory_space=pltpu.SMEM)
    in_any = pl.BlockSpec(memory_space=pl.ANY)
    coarse_shape = jax.ShapeDtypeStruct((NF, CR, CL), F32)
    fine_shape = jax.ShapeDtypeStruct((NF, FR, FL), F32)
    whole = (coarse_shape, fine_shape, coarse_shape, fine_shape)
    big = [vm(x.shape, F32) for x in whole]
    *states, packed = pl.pallas_call(
        kernel,
        out_shape=whole + (jax.ShapeDtypeStruct((GROUP, PART, HID), F32),),
        in_specs=[in_smem] * 5 + [in_vmem] * 6 + [in_any] * 4,
        out_specs=(in_any,) * 4 + (in_vmem,),
        scratch_shapes=[
            *big,
            *big,
            vm((HID, 3 * FB_ROWS), BF16),
            vm((HID, HB), BF16),
            vm((16, HID), BF16),
            vm((2 * FB_ROWS, 4 * HID), BF16),
            vm((HID, HID), BF16),
            vm((HID, 16), BF16),
            vm((FL, CL), BF16),
            vm((CL, FL), BF16),
            dma((4,)),
            dma((4,)),
            pltpu.SMEM((DEV,), jnp.int32),
            slab,
            slab,
            slab,
            slab,
            slab,
            vm((EXT, FB_ROWS, FL), BF16),
            vm((EXT, FB_ROWS, FL), BF16),
            vm((UNROLL, HB, FL), BF16),
            vm((UNROLL, HID, FL), BF16),
            vm((UNROLL, HID, FL), F32),
            vm((EXT, HID, FL), BF16),
            vm((UNROLL, HID, FL), BF16),
            vm((UNROLL, 16, FL), BF16),
            slab,
            slab,
            slab,
            slab,
            vm((2, 8, FL), F32),
            vm((3 * FB_ROWS, HID), F32),
            vm((HB, HID), F32),
            vm((16, HID), F32),
            vm((8, FL), F32),
            vm((2, 4, 2, 4, GA_ROWS, CL), F32),
            vm((4, 2, 4, GA_ROWS, CL), F32),
            vm((4, 4, 2, GA_ROWS, 128), F32),
            vm((4, 2, 4, GA_ROWS, 128), F32),
            vm((4, 2, GA_ROWS, 128), F32),
            vm((2, 4, GA_ROWS, 128), F32),
            vm((8, GA_ROWS, 128), F32),
            vm((8, GA_ROWS, 128), F32),
            vm((2, 8, CL), F32),
            vm((2, 8, CL), F32),
            vm((NF, 8, FL), F32),
            vm((NF, 8, FL), F32),
            vm((NF, 8, FL), F32),
            vm((NF, 8, FL), F32),
            vm((16, CL), F32),
            vm((16, CL), F32),
            vm((16, CL), F32),
            vm((16, CL), F32),
            vm((NF, CR, CL), F32),
            vm((NF, CR, CL), F32),
            vm((2, 8, CL), F32),
            vm((DEV, 8, CL), F32),
            vm((8, CL), F32),
            vm((40, CL), F32),
            vm((2, CHIPS, 40, CL), F32),
            vm((16, CL), F32),
            vm((2, 8, CL), F32),
            vm((GROUP, PART, HID), F32),
            vm((GROUP, PART, HID), F32),
            vm((PART, HID), F32),
            vm((4, PART, HID), F32),
            vm((PART, HID), F32),
            vm((4, PART, HID), F32),
            vm((GROUP, PART, HID), F32),
            dma((2,)),
            dma((2, 4)),
            dma((2, 4)),
            dma((2, 8)),
            dma((2, 8)),
            dma((2, 2)),
            dma((2, 4)),
            dma((2,)),
            dma((DEV,)),
            dma((2, CHIPS)),
            dma((2,)),
            dma((2, DEV)),
            dma((2,)),
            dma((16,)),
            dma((16,)),
            dma((4,)),
            dma((4,)),
            dma((4,)),
            dma((4,)),
            dma((16,)),
            dma((16,)),
        ],
        compiler_params=pltpu.CompilerParams(
            collective_id=0, has_side_effects=True, vmem_limit_bytes=56 * 1024 * 1024
        ),
    )(
        fine_counts,
        coarse_counts,
        fine_anchor,
        coarse_diffusion,
        b_out,
        fine_counts.reshape(1, DEV),
        w_in.T,
        b_in.reshape(1, HID),
        w_mid,
        b_mid.reshape(1, HID),
        w_out,
        coarse_state[0],
        fine_state[0],
        coarse_cot[0],
        fine_cot[0],
    )
    *states, g_w_in, g_b_in, g_w_mid, g_b_mid, g_w_out, g_b_out = pl.pallas_call(
        lambda p, i0, i1, i2, i3, o0, o1, o2, o3, *rest: finish(
            p, (i0, i1, i2, i3), (o0, o1, o2, o3), *rest
        ),
        out_shape=whole
        + tuple(
            jax.ShapeDtypeStruct(shape, F32)
            for shape in (
                (27 * NF, HID),
                (1, HID),
                (HID, HID),
                (1, HID),
                (NF, HID),
                (1, NF),
            )
        ),
        in_specs=[in_vmem] * 5,
        out_specs=(in_any,) * 4 + (in_vmem,) * 6,
        scratch_shapes=[dma((4,))],
    )(packed, *states)
    return (
        *(x[None] for x in states),
        g_w_in.T,
        g_b_in[0],
        g_w_mid,
        g_b_mid[0],
        g_w_out,
        g_b_out[0],
    )


def solution(mesh):
    state = P("dp", None, "patch", None)
    return jax.shard_map(
        on_device,
        mesh=mesh,
        in_specs=(state,) * 4 + (P(),) * 10,
        out_specs=(state,) * 4 + (P(),) * 6,
        check_vma=False,
    )
```

```python
import math

import jax
import jax.numpy as jnp
from jax import lax
from jax.experimental import pallas as pl
from jax.experimental.pallas import tpu as pltpu
from jax.sharding import PartitionSpec as P

MESH = pl.DeviceIdType.MESH
F32 = jnp.float32
BF16 = jnp.bfloat16

DEV = 64
CHIPS = 32
CW = 16
FW = 32
CL = CW * CW
FL = FW * FW
CR = 48
FR = 16
NF = 5
CHAIN = 2048
REGION = 384
TAKEN = 4
HALO = TAKEN + 1
EXT = FR + 2 * HALO
UNROLL = 4
FB_ROWS = 80
HID = 128
HB = 144
GROUP = 16
PART = 24
PACKED = GROUP * PART
GA_ROWS = 40


def dot(a, b):
    return jnp.dot(a, b, preferred_element_type=F32)


def dot_nt(a, b):
    return lax.dot_general(a, b, (((1,), (1,)), ((), ())), preferred_element_type=F32)


def dot_tn(a, b):
    return lax.dot_general(a, b, (((0,), (0,)), ((), ())), preferred_element_type=F32)


def grid(shape, dim):
    return lax.broadcasted_iota(jnp.int32, shape, dim)


def bits(mask):
    return mask.astype(F32).astype(BF16)


def pieces(b):
    hi = b.astype(BF16).astype(F32)
    mid = (b - hi).astype(BF16).astype(F32)
    zeros = jnp.zeros((13, b.shape[1]), F32)
    return jnp.concatenate([hi, mid, b - hi - mid, zeros], axis=0).astype(BF16)


def split(x):
    hi = x.astype(BF16)
    return hi, (x - hi.astype(F32)).astype(BF16)


def shift_x(v, step, width):
    lanes = v.shape[1]
    col = grid((v.shape[0], 128), 1) % width
    parts = []
    for i in range(lanes // 128):
        s = v[:, 128 * i : 128 * (i + 1)]
        if step == 1:
            parts.append(
                jnp.where(
                    col == width - 1, pltpu.roll(s, width - 1, 1), pltpu.roll(s, 127, 1)
                )
            )
        else:
            parts.append(
                jnp.where(col == 0, pltpu.roll(s, 129 - width, 1), pltpu.roll(s, 1, 1))
            )
    return jnp.concatenate(parts, axis=1)


def shift_y(v, step, width):
    lanes = v.shape[1]
    return pltpu.roll(v, lanes - width if step == 1 else width, 1)


def neighbours(v, width):
    return (
        shift_y(v, -1, width)
        + shift_y(v, 1, width)
        + shift_x(v, -1, width)
        + shift_x(v, 1, width)
    )


def kernel(
    fc_smem,
    cc_smem,
    anchor_smem,
    cd_smem,
    bo_smem,
    fcv,
    win_ref,
    bin_ref,
    wmid_ref,
    bmid_ref,
    wout_ref,
    cst_hbm,
    fst_hbm,
    cct_hbm,
    fct_hbm,
    coarse_out_hbm,
    fine_out_hbm,
    coarse_adj_hbm,
    fine_adj_hbm,
    p_out,
    cst,
    fst,
    cct,
    fct,
    coarse_out,
    fine_out,
    coarse_adj,
    fine_adj,
    w1,
    w2,
    w3,
    wp,
    w2t,
    w3t,
    pool,
    pool_t,
    sem_in,
    sem_out,
    base_s,
    v0,
    v1,
    v2,
    nb0,
    nb1,
    s0,
    s1,
    a1,
    a2,
    sl1,
    d1,
    d2,
    sbv,
    g2,
    g1,
    araw,
    gout,
    rim,
    p1,
    p2,
    p3,
    gsum,
    sendb,
    pairb,
    ga_a,
    ga_b,
    sum_a,
    sum_b,
    ga_a2,
    ga_b2,
    gh,
    gr,
    hs_dn,
    hs_up,
    hr_lo,
    hr_hi,
    cs_dn,
    cs_up,
    cr_lo,
    cr_hi,
    upd,
    back,
    rim_src,
    rim_got,
    rim_row_ref,
    rs,
    gath,
    rgs,
    rg,
    pk,
    r1,
    r1sum,
    r2,
    r2sum,
    rd,
    pall,
    sem_pair,
    sem_a1,
    sem_b1,
    sem_a2,
    sem_b2,
    sem_edge,
    sem_halo,
    sem_rim_s,
    sem_rim_r,
    sem_rs,
    sem_gp,
    sem_rg_s,
    sem_rg_r,
    sem_r1s,
    sem_r1r,
    sem_r2s,
    sem_r2r,
    sem_rds,
    sem_rdr,
    sem_r3s,
    sem_r3r,
):
    me = lax.axis_index("patch")
    dp = lax.axis_index("dp")
    core = lax.rem(me, 2)
    chip = me // 2
    partner = chip * 2 + (1 - core)
    nxt = lax.rem(me + 1, DEV)
    prv = lax.rem(me + DEV - 1, DEV)

    cx, czy = chip // 8, lax.rem(chip, 8)
    cy, cxz = lax.rem(chip, 4), chip // 4
    w = (lax.rem(cx, 2) * 2 + lax.rem(cxz, 2)) * 4 + lax.rem(cy, 2) * 2 + core
    xg = cx // 2 * 2 + cy // 2

    def member(g, k):
        x = g // 2 * 2 + k // 8
        y = lax.rem(g, 2) * 2 + lax.rem(k // 2, 2)
        return x * GROUP + lax.rem(k // 4, 2) * 8 + y * 2 + lax.rem(k, 2)

    arrivals = [
        pltpu.make_async_copy(src, dst, sem_in.at[i])
        for i, (src, dst) in enumerate(
            ((cst_hbm, cst), (fst_hbm, fst), (cct_hbm, cct), (fct_hbm, fct))
        )
    ]
    for copy in arrivals:
        copy.start()

    barrier = pltpu.get_barrier_semaphore()

    def greet(t, c):
        pl.semaphore_signal(
            barrier, inc=1, device_id={"patch": lax.rem(me + t, DEV)}, device_id_type=MESH
        )
        return c

    lax.fori_loop(1, DEV, greet, 0)

    def greet_dp(t, c):
        pl.semaphore_signal(
            barrier,
            inc=1,
            device_id={"patch": me, "dp": lax.rem(dp + t, 4)},
            device_id_type=MESH,
        )
        return c

    lax.fori_loop(1, 4, greet_dp, 0)

    for copy in arrivals:
        copy.wait()

    anchor = anchor_smem[0]

    def count(d, carry):
        fs, cs = carry
        base_s[d] = fs
        fs = fs + fc_smem[d]
        cs = cs + jnp.where(d < me, cc_smem[d], 0)
        return (fs, cs)

    _, cpatch = lax.fori_loop(0, DEV, count, (jnp.int32(0), jnp.int32(0)))
    cstart = cpatch * CW
    nc = cc_smem[me] * CW
    n = fc_smem[me] * 8
    wide = n == FR
    first = me == 0
    last = me == DEV - 1

    def wrap(x):
        return lax.rem(x + 2 * CHAIN + CHAIN // 2, CHAIN) - CHAIN // 2

    def live_or_none(local):
        return jnp.where((local >= 0) & (local < nc), local, -10000)

    low_local = live_or_none(wrap(anchor - 1 - cstart))
    high_local = live_or_none(wrap(anchor + REGION - cstart))

    row48 = grid((CR, CL), 0)
    live48 = row48 < nc
    off48 = lax.rem(row48 + (cstart - anchor + 2 * CHAIN), CHAIN)
    in_region = (off48 < REGION) & live48

    for f in range(NF):
        hs_dn[f, 0:4, :] = fst[f, 0:4, :]
        hs_dn[f, 4:8, :] = fct[f, 0:4, :]
        hs_up[f, 0:4, :] = jnp.where(wide, fst[f, 12:16, :], fst[f, 4:8, :])
        hs_up[f, 4:8, :] = jnp.where(wide, fct[f, 12:16, :], fct[f, 4:8, :])
    cs_dn[...] = jnp.zeros_like(cs_dn)
    cs_up[...] = jnp.zeros_like(cs_up)
    for f in range(NF):
        kept = jnp.where(in_region, 0.0, cct[f])
        cs_dn[f : f + 1, :] = cst[f, 0:1, :]
        cs_dn[8 + f : 9 + f, :] = kept[0:1]
        cs_up[f : f + 1, :] = jnp.where(
            nc == 48,
            cst[f, 47:48, :],
            jnp.where(nc == 32, cst[f, 31:32, :], cst[f, 15:16, :]),
        )
        cs_up[8 + f : 9 + f, :] = jnp.where(
            nc == 48, kept[47:48], jnp.where(nc == 32, kept[31:32], kept[15:16])
        )

    def neighbour_copies():
        def one(src, dst, k, dev):
            return pltpu.make_async_remote_copy(
                src_ref=src,
                dst_ref=dst,
                send_sem=sem_halo.at[0, k],
                recv_sem=sem_halo.at[1, k],
                device_id={"patch": dev},
                device_id_type=MESH,
            )

        return (
            one(hs_up, hr_lo, 0, nxt),
            one(hs_dn, hr_hi, 1, prv),
            one(cs_up, cr_lo, 2, nxt),
            one(cs_dn, cr_hi, 3, prv),
        )

    cot = jnp.concatenate([jnp.where(live48, cct[f], 0.0) for f in range(NF)], axis=0)
    cot_hi, cot_lo = split(cot)
    cot2 = jnp.concatenate([cot_hi, cot_lo], axis=1)
    srow = grid((GA_ROWS, NF * CR), 0)
    scol = grid((GA_ROWS, NF * CR), 1)
    pick = jnp.where(
        scol // CR == srow % NF, scol % CR - srow // NF, 99999
    )

    def rows_for(c2):
        def one(i, c):
            hot = []
            for k in range(8):
                base = wrap(anchor + 4 * base_s[2 * (8 * i + k) + c2] - cstart)
                hot.append((pick == base).astype(F32))
            both = dot(jnp.concatenate(hot, axis=0).astype(BF16), cot2)
            both = both[:, :CL] + both[:, CL:]
            sendb[c2, i] = both.reshape(2, 4, GA_ROWS, CL)
            return c

        lax.fori_loop(0, CHIPS // 8, one, 0)

    ust = jnp.concatenate([cst[f] for f in range(NF)], axis=0)
    ust_hi, ust_lo = split(ust)
    ust2 = jnp.concatenate([ust_hi, ust_lo], axis=1)
    frow = grid((16, NF * CR), 0)
    fcol = grid((16, NF * CR), 1)
    fpick = jnp.where(fcol // CR == frow, fcol % CR, 99999)
    for e, local in ((0, low_local), (1, high_local)):
        both = dot(bits(fpick == local), ust2)
        rim_src[e] = (both[:, :CL] + both[:, CL:])[0:8]

    pl.semaphore_wait(barrier, DEV - 1 + 3)

    halo_copies = neighbour_copies()
    for copy in halo_copies:
        copy.start()

    def rim_copy(e, sender):
        return pltpu.make_async_remote_copy(
            src_ref=rim_src.at[e],
            dst_ref=rim_got.at[sender],
            send_sem=sem_rim_s.at[e],
            recv_sem=sem_rim_r.at[sender],
            device_id={"patch": (DEV - 1) * e},
            device_id_type=MESH,
        )

    ends = ((0, 0), (1, DEV - 1))
    for e, who in ends:

        @pl.when(me != who)
        def _(e=e):
            rim_copy(e, me).start()

    rows_for(1 - core)
    pair_copy = pltpu.make_async_remote_copy(
        src_ref=sendb.at[1 - core],
        dst_ref=pairb,
        send_sem=sem_pair.at[0],
        recv_sem=sem_pair.at[1],
        device_id={"patch": partner},
        device_id_type=MESH,
    )
    pair_copy.start()
    rows_for(core)

    col = grid((27 * NF, 3 * FB_ROWS), 1)
    row = grid((27 * NF, 3 * FB_ROWS), 0)
    part, field = col % FB_ROWS // 8, col % 8
    place = (col // FB_ROWS * 9 + part) * NF + field
    laid = dot_tn(win_ref[...], bits((row == place) & (part < 9) & (field < NF)))
    brow, bcol = grid((16, 3 * FB_ROWS), 0), grid((16, 3 * FB_ROWS), 1)
    bias = dot_tn(pieces(bin_ref[...]), bits((bcol == FB_ROWS + 72 + brow) & (brow < 3)))
    w1[...] = ((laid + bias) * 0.5).astype(BF16)
    qrow, qcol = grid((FB_ROWS, 27 * NF), 0), grid((FB_ROWS, 27 * NF), 1)
    wp[...] = jnp.zeros_like(wp)
    for a in range(3):
        take = (qcol == (a * 9 + qrow // 8) * NF + qrow % 8) & (qrow < 72) & (qrow % 8 < NF)
        turned = dot(bits(take), win_ref[...]).astype(BF16)
        for j in range(2):
            m = j + 2 - a
            wp[FB_ROWS * j : FB_ROWS * (j + 1), HID * m : HID * (m + 1)] = turned
    eye = bits(grid((HID, HID), 0) == grid((HID, HID), 1))
    eye16 = bits(grid((16, 16), 0) == grid((16, 16), 1))
    w2[:, 0:HID] = (wmid_ref[...].astype(F32) * 0.5).astype(BF16)
    w2[:, HID:HB] = (dot_tn(pieces(bmid_ref[...]), eye16) * 0.5).astype(BF16)
    w2t[...] = (dot_nt(eye, wmid_ref[...]) * 0.5).astype(BF16)
    w3[...] = dot(bits(grid((16, NF), 0) == grid((16, NF), 1)), wout_ref[...]).astype(BF16)
    w3t[...] = (dot_nt(eye, w3[...]) * 0.5).astype(BF16)
    fine_cell, coarse_cell = grid((FL, CL), 0), grid((FL, CL), 1)
    pool[...] = bits(fine_cell // (2 * FW) * CW + fine_cell % FW // 2 == coarse_cell)
    coarse_cell, fine_cell = grid((CL, FL), 0), grid((CL, FL), 1)
    pool_t[...] = bits(fine_cell // (2 * FW) * CW + fine_cell % FW // 2 == coarse_cell)
    field_row = grid((8, FL), 0)
    kf = jnp.zeros((8, FL), F32)
    half_bias = jnp.zeros((8, FL), F32)
    for f in range(NF):
        kf = jnp.where(field_row == f, 2.0 * cd_smem[f], kf)
        half_bias = jnp.where(field_row == f, 0.5 * bo_smem[f], half_bias)

    pair_copy.wait()

    def add_pair(k, c):
        sendb[core, k] = sendb[core, k] + pairb[k]
        return c

    lax.fori_loop(0, 4, add_pair, 0)

    def chip_copy(src, dst, sems, t, to):
        return pltpu.make_async_remote_copy(
            src_ref=src,
            dst_ref=dst,
            send_sem=sems.at[0, t],
            recv_sem=sems.at[1, t],
            device_id={"patch": 2 * to + core},
            device_id_type=MESH,
        )

    def a1_copy(t):
        k = lax.rem(cy + t, 4)
        src = sendb.at[core, :, :, k, :, 0:128]
        return chip_copy(src, ga_a.at[cy], sem_a1, t, cxz * 4 + k)

    def b1_copy(t):
        k = lax.rem(cx + t, 4)
        src = sendb.at[core, k, :, :, :, 128:256]
        return chip_copy(src, ga_b.at[cx], sem_b1, t, k * 8 + czy)

    def a2_copy(t):
        k = lax.rem(cxz + t, 8)
        src = sum_a.at[k // 2, lax.rem(k, 2)]
        return chip_copy(src, ga_a2.at[cxz], sem_a2, t, k * 4 + cy)

    def b2_copy(t):
        k = lax.rem(czy + t, 8)
        src = sum_b.at[k // 4, lax.rem(k, 4)]
        return chip_copy(src, ga_b2.at[czy], sem_b2, t, cx * 8 + k)

    def run(make, what, count=16):
        def one(t, c):
            what(make(t))
            return c

        lax.fori_loop(1, count, one, 0)

    def begin(copy):
        copy.start()

    def end(copy):
        copy.wait()

    run(a1_copy, begin, 4)
    run(b1_copy, begin, 4)

    ones8 = jnp.ones((8, FL), F32)

    def build_features(s_ref, nb_ref, z, v):
        xm = shift_x(v, -1, FW)
        xp = shift_x(v, 1, FW)
        xs = jnp.concatenate([xm, v, xp], axis=0)
        ym = shift_y(xs, -1, FW)
        yp = shift_y(xs, 1, FW)
        s_ref[z] = jnp.concatenate([ym, xs, yp, ones8], axis=0).astype(BF16)
        nb_ref[z] = ym[8:16] + yp[8:16] + xm + xp - 6.0 * v

    for j in range(UNROLL):
        a1[j, HID:HB, :] = jnp.ones((HB - HID, FL), BF16)
    p1[...] = jnp.zeros_like(p1)
    p2[...] = jnp.zeros_like(p2)
    p3[...] = jnp.zeros_like(p3)
    gsum[...] = jnp.zeros_like(gsum)
    v0[...] = jnp.zeros_like(v0)
    g2[...] = jnp.zeros_like(g2)
    for z in (0, EXT - 1):
        s0[z] = jnp.zeros((FB_ROWS, FL), BF16)
        v1[z] = jnp.zeros((8, FL), F32)
    for z in range(EXT - 4, EXT):
        g1[z] = jnp.zeros((8, FL), F32)

    for src, dst in ((fst, v0), (fct, g2)):
        for f in range(NF):
            for i in range(FR):
                line = src[f, i : i + 1, :]
                dst[HALO + i, f : f + 1, :] = line if i < 8 else jnp.where(wide, line, 0.0)

    def features_first(k, c):
        for j in range(UNROLL):
            z = 1 + UNROLL * k + j
            build_features(s0, nb0, z, v0[z])
        return c

    lax.fori_loop(1, 3, features_first, 0)

    halo_copies[0].wait()
    halo_copies[1].wait()
    for at, dst in ((0, v0), (4, g2)):
        for f in range(NF):
            one = slice(f, f + 1)
            for i in range(TAKEN):
                hi = hr_hi[f, at + i : at + i + 1, :]
                dst[1 + i, one, :] = hr_lo[f, at + i : at + i + 1, :]
                dst[HALO + 8 + i, one, :] = jnp.where(wide, dst[HALO + 8 + i, one, :], hi)
                dst[HALO + 16 + i, one, :] = jnp.where(wide, hi, 0.0)

    rim_row_ref[...] = jnp.zeros_like(rim_row_ref)
    for e, who in ends:

        @pl.when(me != who)
        def _(e=e):
            rim_copy(e, me).wait_send()

        @pl.when(me == who)
        def _(e=e, who=who):
            rim_row_ref[...] = rim_src[e]

            def one(t, c):
                s = lax.rem(who + t, DEV)
                rim_copy(e, s).wait_recv()
                rim_row_ref[...] = rim_row_ref[...] + rim_got[s]
                return c

            lax.fori_loop(1, DEV, one, 0)

    rim_hi, rim_lo = split(rim_row_ref[...])
    beside = dot(rim_hi, pool_t[...]) + dot(rim_lo, pool_t[...])
    v0[HALO - 1] = jnp.where(first, beside, v0[HALO - 1])
    v0[HALO + 8] = jnp.where(last & ~wide, beside, v0[HALO + 8])
    v0[HALO + 16] = jnp.where(last & wide, beside, v0[HALO + 16])

    steps_all = (EXT - 2) // UNROLL
    lax.fori_loop(0, 1, features_first, 0)
    lax.fori_loop(3, steps_all, features_first, 0)

    def rim_row(z):
        return (first & (z < HALO)) | (last & (z >= HALO + n))

    def advance(z, v, nb, source):
        lap = v[z - 1] + v[z + 1] + nb[z]
        return v[z] + kf * lap + (0.5 * source[0:8] + half_bias)

    def features_of(s_ref, z):
        return s_ref[pl.ds(z - 1, 3)].reshape(3 * FB_ROWS, FL)

    def forward_rows(k, c):
        rows = [(j, 1 + UNROLL * k + j) for j in range(UNROLL)]
        for _, z in rows:
            before = jnp.maximum(z - UNROLL, 0)
            build_features(s1, nb1, before, v1[before])
        for j, z in rows:
            h = dot(w1[...], features_of(s0, z))
            a1[j, 0:HID, :] = (h + h * jnp.tanh(h)).astype(BF16)
        for j, z in rows:
            h = dot(w2[...], a1[j])
            a2[j] = (h + h * jnp.tanh(h)).astype(BF16)
        for j, z in rows:
            new = advance(z, v0, nb0, dot(w3[...], a2[j]))
            v1[z] = jnp.where(rim_row(z), v0[z], new)
        return c

    lax.fori_loop(0, 3, forward_rows, 0)

    ga_a[cy] = sendb[core, :, :, cy, :, 0:128]
    ga_b[cx] = sendb[core, cx, :, :, :, 128:256]
    run(a1_copy, end, 4)
    run(b1_copy, end, 4)
    sum_a[...] = ga_a[0] + ga_a[1] + ga_a[2] + ga_a[3]
    sum_b[...] = ga_b[0] + ga_b[1] + ga_b[2] + ga_b[3]
    run(a2_copy, begin, 8)
    run(b2_copy, begin, 8)

    lax.fori_loop(3, 5, forward_rows, 0)
    ga_a2[cxz] = sum_a[cxz // 2, lax.rem(cxz, 2)]
    ga_b2[czy] = sum_b[czy // 4, lax.rem(czy, 4)]
    run(a2_copy, end, 8)
    run(b2_copy, end, 8)
    parts = []
    for ref in (ga_a2, ga_b2):
        part = ref[0]
        for k in range(1, 8):
            part = part + ref[k]
        parts.append(part)
    region = jnp.concatenate(parts, axis=1)
    blank = jnp.zeros((3, CL), F32)
    gh[0] = jnp.concatenate([region[0:5], blank], axis=0)
    gh[1] = jnp.concatenate([jnp.where(wide, region[35:40], region[15:20]), blank], axis=0)

    def edge_copy(k, to):
        return pltpu.make_async_remote_copy(
            src_ref=gh.at[k],
            dst_ref=gr.at[k],
            send_sem=sem_edge.at[0, k],
            recv_sem=sem_edge.at[1, k],
            device_id={"patch": to},
            device_id_type=MESH,
        )

    edges = (edge_copy(0, prv), edge_copy(1, nxt))
    for copy in edges:
        copy.start()

    lax.fori_loop(5, steps_all, forward_rows, 0)
    for z in range(EXT - 1 - UNROLL, EXT - 1):
        build_features(s1, nb1, z, v1[z])

    def lift(x):
        hi, lo = split(x)
        return (dot(hi, pool_t[...]) + dot(lo, pool_t[...])) * 0.125

    lifted = lift(region)
    for r in range(8):
        for i in (HALO + 2 * r, HALO + 2 * r + 1):
            g2[i, 0:5, :] = g2[i, 0:5, :] + jnp.where(2 * r < n, lifted[5 * r : 5 * r + 5], 0.0)
    for copy in edges:
        copy.wait()
    lifted = lift(jnp.concatenate([gr[0], gr[1]], axis=0))
    for i in (HALO - 2, HALO - 1):
        g2[i] = g2[i] + lifted[8:16]
    for i in (HALO + 8, HALO + 9):
        g2[i] = g2[i] + jnp.where(wide, 0.0, lifted[0:8])
    for i in (HALO + 16, HALO + 17):
        g2[i] = g2[i] + jnp.where(wide, lifted[0:8], 0.0)

    def level_row(z):
        return ~(rim_row(z)) & (z < HALO + n + 2)

    def mask_g2(z, c):
        g2[z] = jnp.where(level_row(z) & (z >= HALO - 2), g2[z], 0.0)
        return c

    lax.fori_loop(0, EXT, mask_g2, 0)

    def backward_rows(zs, s_ref, g_ref, v_ref, nb_ref, with_source):
        rows = list(enumerate(zs))
        own = [(z >= HALO) & (z < HALO + n) for z in zs]
        for j, z in rows:
            half = 0.5 * g_ref[z]
            gsum[...] = gsum[...] + jnp.where(own[j], half, 0.0)
            sbv[j] = jnp.concatenate([half, jnp.zeros_like(half)], axis=0).astype(BF16)
        for j, z in rows:
            h = dot(w1[...], features_of(s_ref, z))
            t = jnp.tanh(h)
            u = h * t
            a1[j, 0:HID, :] = (h + u).astype(BF16)
            sl1[j] = (1.0 + t) * (1.0 + h - u)
        for j, z in rows:
            h = dot(w2[...], a1[j])
            t = jnp.tanh(h)
            u = h * t
            a2[j] = (h + u).astype(BF16)
            d2[j] = (dot(w3t[...], sbv[j]) * ((1.0 + t) * (1.0 + h - u))).astype(BF16)
        for j, z in rows:
            d1[z] = (dot(w2t[...], d2[j]) * sl1[j]).astype(BF16)
        for j, z in rows:
            p1[...] = p1[...] + jnp.where(own[j], dot_nt(features_of(s_ref, z), d1[z]), 0.0)
            p2[...] = p2[...] + jnp.where(own[j], dot_nt(a1[j], d2[j]), 0.0)
            p3[...] = p3[...] + jnp.where(own[j], dot_nt(sbv[j], a2[j]), 0.0)
            if with_source:
                v2[z] = advance(z, v_ref, nb_ref, dot(w3[...], a2[j]))

    def spread_rows(r0, g_ref, out_ref):
        both = dot(wp[...], d1[pl.ds(r0 - 1, 4)].reshape(4 * HID, FL))
        for j in range(2):
            r = r0 + j
            acc = both[FB_ROWS * j : FB_ROWS * (j + 1)]
            g = g_ref[r]
            kg = kf * g
            lo = jnp.concatenate([acc[0:8], acc[8:16] + kg, acc[16:24]], axis=0)
            mid = jnp.concatenate([acc[24:32] + kg, acc[32:40], acc[40:48] + kg], axis=0)
            hi = jnp.concatenate([acc[48:56], acc[56:64] + kg, acc[64:72]], axis=0)
            xs = shift_y(lo, 1, FW) + mid + shift_y(hi, -1, FW)
            moved = shift_x(xs[0:8], 1, FW) + xs[8:16] + shift_x(xs[16:24], -1, FW)
            a = g + kf * (g_ref[r - 1] + g_ref[r + 1] - 6.0 * g) + moved
            araw[r] = a
            inside = level_row(r) & (r >= HALO - 1) & (r < HALO + n + 1)
            out_ref[r] = jnp.where(inside, a, 0.0)

    start = HALO - 2
    steps = (FR + 4) // UNROLL

    def reverse(first_spread, s_ref, g_ref, out_ref, v_ref, nb_ref, with_source):
        def rows_at(z0):
            zs = [z0 + j for j in range(UNROLL)]
            backward_rows(zs, s_ref, g_ref, v_ref, nb_ref, with_source)

        def step(k, c):
            z0 = start + UNROLL * k
            for j in range(0, UNROLL, 2):
                spread_rows(z0 - UNROLL - 1 + j, g_ref, out_ref)
            rows_at(z0)
            return c

        first_spread()
        rows_at(start)
        lax.fori_loop(1, steps, step, 0)

    def last_spread(g_ref, out_ref):
        for j in range(0, UNROLL, 2):
            spread_rows(start + UNROLL * steps - UNROLL - 1 + j, g_ref, out_ref)

    def second_rest():
        last_spread(g2, g1)
        rim[0] = araw[HALO - 1]
        rim[1] = jnp.where(wide, araw[HALO + 16], araw[HALO + 8])

    reverse(lambda: None, s1, g2, g1, v1, nb1, True)

    pairs = jnp.concatenate(
        [v2[HALO + 2 * k] + v2[HALO + 2 * k + 1] for k in range(8)], axis=0
    )
    pairs_hi, pairs_lo = split(pairs)
    rest = (dot(pairs_hi, pool[...]) + dot(pairs_lo, pool[...])) * 0.125
    for k in range(8):
        for f in range(NF):
            rs[8 * f + k : 8 * f + k + 1, :] = rest[8 * k + f : 8 * k + f + 1]

    def rs_copy(t):
        return pltpu.make_async_remote_copy(
            src_ref=rs,
            dst_ref=gath.at[core, chip],
            send_sem=sem_rs.at[0, t],
            recv_sem=sem_rs.at[1, t],
            device_id={"patch": 2 * lax.rem(chip + t, CHIPS) + core},
            device_id_type=MESH,
        )

    def start_rs(t, c):
        rs_copy(t).start()
        return c

    lax.fori_loop(1, CHIPS, start_rs, 0)
    gath[core, chip] = rs[...]

    def r1_copy(t):
        k = lax.rem(w + t, GROUP)
        return pltpu.make_async_remote_copy(
            src_ref=pk.at[k],
            dst_ref=r1.at[w],
            send_sem=sem_r1s.at[t],
            recv_sem=sem_r1r.at[t],
            device_id={"patch": member(xg, k)},
            device_id_type=MESH,
        )

    def r2_copy(t):
        return pltpu.make_async_remote_copy(
            src_ref=r1sum,
            dst_ref=r2.at[xg],
            send_sem=sem_r2s.at[t],
            recv_sem=sem_r2r.at[t],
            device_id={"patch": member(lax.rem(xg + t, 4), w)},
            device_id_type=MESH,
        )

    def rd_copy(t):
        return pltpu.make_async_remote_copy(
            src_ref=r2sum,
            dst_ref=rd.at[dp],
            send_sem=sem_rds.at[t],
            recv_sem=sem_rdr.at[t],
            device_id={"patch": me, "dp": lax.rem(dp + t, 4)},
            device_id_type=MESH,
        )

    def r3_copy(t):
        k = lax.rem(w + t, GROUP)
        return pltpu.make_async_remote_copy(
            src_ref=pall.at[w],
            dst_ref=pall.at[w],
            send_sem=sem_r3s.at[t],
            recv_sem=sem_r3r.at[t],
            device_id={"patch": member(xg, k)},
            device_id_type=MESH,
        )

    def send_parts():
        total = jnp.sum(gsum[...], axis=1, keepdims=True)
        tiles = [(p1, 8 * i) for i in range(9)]
        tiles += [(p1, FB_ROWS + 8 * i) for i in range(10)]
        tiles += [(p1, 2 * FB_ROWS + 8 * i) for i in range(9)]
        tiles += [(p2, 8 * i) for i in range(17)]
        tiles += [(p3, 0)]
        for i, (ref, at) in enumerate(tiles):
            pk[i // 3, 8 * (i % 3) : 8 * (i % 3) + 8, :] = ref[at : at + 8, :]
        pk[15, 8:16, :] = jnp.broadcast_to(total, (8, HID))
        pk[15, 16:24, :] = jnp.zeros((8, HID), F32)
        run(r1_copy, begin)

    reverse(second_rest, s0, g1, gout, v0, nb0, False)
    send_parts()
    last_spread(g1, gout)

    rim[0] = rim[0] + araw[HALO - 1]
    rim[1] = rim[1] + jnp.where(wide, araw[HALO + 16], araw[HALO + 8])
    rims = jnp.concatenate([rim[0], rim[1]], axis=0)
    rims_hi, rims_lo = split(rims)
    rims = dot(rims_hi, pool[...]) + dot(rims_lo, pool[...])
    rgs[...] = rims

    def rg_copy(e, dev, t):
        return pltpu.make_async_remote_copy(
            src_ref=rgs.at[pl.ds(8 * e, 8)],
            dst_ref=rg.at[e],
            send_sem=sem_rg_s.at[e, t],
            recv_sem=sem_rg_r.at[e],
            device_id={"patch": dev},
            device_id_type=MESH,
        )

    for e, who in ends:

        @pl.when(me == who)
        def _(e=e, who=who):
            def one(t, c):
                rg_copy(e, lax.rem(who + t, DEV), t).start()
                return c

            lax.fori_loop(1, DEV, one, 0)
            rg[e] = rgs[8 * e : 8 * e + 8, :]

    halo_copies[2].wait()
    halo_copies[3].wait()
    for f in range(NF):
        kappa = cd_smem[f]
        for src, lo, hi, dst in (
            (jnp.where(live48, cst[f], 0.0), cr_lo[f : f + 1], cr_hi[f : f + 1], upd),
            (
                jnp.where(in_region | ~live48, 0.0, cct[f]),
                cr_lo[8 + f : 9 + f],
                cr_hi[8 + f : 9 + f],
                back,
            ),
        ):
            below = jnp.where(row48 == 0, lo, pltpu.roll(src, 1, 0))
            above = jnp.where(row48 == nc - 1, hi, pltpu.roll(src, CR - 1, 0))
            new = src + kappa * (below + above + neighbours(src, CW) - 6.0 * src)
            dst[f] = jnp.where(live48, new, 0.0)

    r1[w] = pk[w]
    run(r1_copy, end)

    def add_up(ref, count):
        out = ref[0]
        for k in range(1, count):
            out = out + ref[k]
        return out

    r1sum[...] = add_up(r1, GROUP)
    run(r2_copy, begin, 4)

    def wait_rs(t, c):
        rs_copy(t).wait()
        return c

    lax.fori_loop(1, CHIPS, wait_rs, 0)
    gp_copy = pltpu.make_async_remote_copy(
        src_ref=gath.at[core],
        dst_ref=gath.at[core],
        send_sem=sem_gp.at[0],
        recv_sem=sem_gp.at[1],
        device_id={"patch": partner},
        device_id_type=MESH,
    )
    gp_copy.start()

    r2[xg] = r1sum[...]
    run(r2_copy, end, 4)
    r2sum[...] = add_up(r2, 4)
    run(rd_copy, begin, 4)

    for i in range(FR):
        keep = (i < n)
        a = jnp.where(keep, v2[HALO + i], 0.0)
        b = jnp.where(keep, gout[HALO + i], 0.0)
        for f in range(NF):
            fine_out[f, i : i + 1, :] = a[f : f + 1]
            fine_adj[f, i : i + 1, :] = b[f : f + 1]
    departures = [
        pltpu.make_async_copy(src, dst, sem_out.at[i])
        for i, (src, dst) in enumerate(
            (
                (fine_out, fine_out_hbm),
                (fine_adj, fine_adj_hbm),
                (coarse_out, coarse_out_hbm),
                (coarse_adj, coarse_adj_hbm),
            )
        )
    ]
    departures[0].start()
    departures[1].start()

    rd[dp] = r2sum[...]
    run(rd_copy, end, 4)
    pall[w] = add_up(rd, 4)
    run(r3_copy, begin)

    qi = grid((DEV, 512), 0)
    qc = grid((DEV, 512), 1)
    qd = 2 * ((qc % 256) // 8) + qc // 256
    counts = jnp.broadcast_to(fcv[...].astype(F32), (16, DEV)).astype(BF16)
    starts = dot(counts, (qi < qd).astype(F32).astype(BF16))
    sizes = dot(counts, (qi == qd).astype(F32).astype(BF16))
    qr = (grid((16, 512), 1) % 8).astype(F32)
    place = jnp.where(qr < 4.0 * sizes, 4.0 * starts + qr, -1.0)[0:1]
    off = off48[:, 0:1].astype(F32)
    onehot = (off == place).astype(F32).astype(BF16)

    gp_copy.wait()
    for f in range(NF):
        rows = gath[:, :, 8 * f : 8 * f + 8, :].reshape(512, CL)
        rows_hi, rows_lo = split(rows)
        pulled = dot(onehot, rows_hi) + dot(onehot, rows_lo)
        coarse_out[f] = jnp.where(in_region, pulled, upd[f])
    departures[2].start()

    for e, who in ends:

        @pl.when(me != who)
        def _(e=e):
            rg_copy(e, partner, 0).wait_recv()

        @pl.when(me == who)
        def _(e=e, who=who):
            def one(t, c):
                rg_copy(e, lax.rem(who + t, DEV), t).wait_send()
                return c

            lax.fori_loop(1, DEV, one, 0)

    for f in range(NF):
        coarse_adj[f] = (
            back[f]
            + jnp.where(row48 == low_local, rg[0, f : f + 1, :], 0.0)
            + jnp.where(row48 == high_local, rg[1, f : f + 1, :], 0.0)
        )

    departures[3].start()

    run(r3_copy, end)
    p_out[...] = pall[...]
    for copy in departures:
        copy.wait()


def finish(packed, ins, outs, w_in, b_in, w_mid, b_mid, w_out, b_out, sems):
    copies = [
        pltpu.make_async_copy(src, dst, sems.at[i])
        for i, (src, dst) in enumerate(zip(ins, outs))
    ]
    for copy in copies:
        copy.start()
    x = packed[...].reshape(PACKED, HID) * (1.0 / math.sqrt(4 * 96 * 8 * FL))
    hi = x.astype(BF16)
    rest = x - hi.astype(F32)
    mid = rest.astype(BF16)
    lo = (rest - mid.astype(F32)).astype(BF16)
    j = grid((27 * NF, 224), 0)
    at = j // NF * 8 + j % NF + jnp.where(j >= 18 * NF, 8, 0)
    take = bits(grid((27 * NF, 224), 1) == at)
    eye = bits(grid((HID, HID), 0) == grid((HID, HID), 1))

    def pull(product, a, b):
        return product(hi[a:b]) + product(mid[a:b]) + product(lo[a:b])

    w_in[...] = pull(lambda y: dot(take, y), 0, 224)
    w_mid[...] = pull(lambda y: dot_tn(y, eye), 224, 224 + HID)
    b_in[...] = x[144:145]
    b_mid[...] = x[352:353]
    w_out[...] = x[360:365]
    on = grid((8, HID), 0) == grid((8, HID), 1)
    b_out[...] = jnp.sum(jnp.where(on, x[368:376], 0.0), axis=0, keepdims=True)[:, 0:NF]
    for copy in copies:
        copy.wait()


def on_device(
    coarse_state,
    fine_state,
    coarse_cot,
    fine_cot,
    coarse_diffusion,
    w_in,
    b_in,
    w_mid,
    b_mid,
    w_out,
    b_out,
    coarse_counts,
    fine_counts,
    fine_anchor,
):
    vm = pltpu.VMEM
    slab = vm((EXT, 8, FL), F32)
    dma = pltpu.SemaphoreType.DMA
    in_vmem = pl.BlockSpec(memory_space=pltpu.VMEM)
    in_smem = pl.BlockSpec(memory_space=pltpu.SMEM)
    in_any = pl.BlockSpec(memory_space=pl.ANY)
    coarse_shape = jax.ShapeDtypeStruct((NF, CR, CL), F32)
    fine_shape = jax.ShapeDtypeStruct((NF, FR, FL), F32)
    whole = (coarse_shape, fine_shape, coarse_shape, fine_shape)
    big = [vm(x.shape, F32) for x in whole]
    *states, packed = pl.pallas_call(
        kernel,
        out_shape=whole + (jax.ShapeDtypeStruct((GROUP, PART, HID), F32),),
        in_specs=[in_smem] * 5 + [in_vmem] * 6 + [in_any] * 4,
        out_specs=(in_any,) * 4 + (in_vmem,),
        scratch_shapes=[
            *big,
            *big,
            vm((HID, 3 * FB_ROWS), BF16),
            vm((HID, HB), BF16),
            vm((16, HID), BF16),
            vm((2 * FB_ROWS, 4 * HID), BF16),
            vm((HID, HID), BF16),
            vm((HID, 16), BF16),
            vm((FL, CL), BF16),
            vm((CL, FL), BF16),
            dma((4,)),
            dma((4,)),
            pltpu.SMEM((DEV,), jnp.int32),
            slab,
            slab,
            slab,
            slab,
            slab,
            vm((EXT, FB_ROWS, FL), BF16),
            vm((EXT, FB_ROWS, FL), BF16),
            vm((UNROLL, HB, FL), BF16),
            vm((UNROLL, HID, FL), BF16),
            vm((UNROLL, HID, FL), F32),
            vm((EXT, HID, FL), BF16),
            vm((UNROLL, HID, FL), BF16),
            vm((UNROLL, 16, FL), BF16),
            slab,
            slab,
            slab,
            slab,
            vm((2, 8, FL), F32),
            vm((3 * FB_ROWS, HID), F32),
            vm((HB, HID), F32),
            vm((16, HID), F32),
            vm((8, FL), F32),
            vm((2, 4, 2, 4, GA_ROWS, CL), F32),
            vm((4, 2, 4, GA_ROWS, CL), F32),
            vm((4, 4, 2, GA_ROWS, 128), F32),
            vm((4, 2, 4, GA_ROWS, 128), F32),
            vm((4, 2, GA_ROWS, 128), F32),
            vm((2, 4, GA_ROWS, 128), F32),
            vm((8, GA_ROWS, 128), F32),
            vm((8, GA_ROWS, 128), F32),
            vm((2, 8, CL), F32),
            vm((2, 8, CL), F32),
            vm((NF, 8, FL), F32),
            vm((NF, 8, FL), F32),
            vm((NF, 8, FL), F32),
            vm((NF, 8, FL), F32),
            vm((16, CL), F32),
            vm((16, CL), F32),
            vm((16, CL), F32),
            vm((16, CL), F32),
            vm((NF, CR, CL), F32),
            vm((NF, CR, CL), F32),
            vm((2, 8, CL), F32),
            vm((DEV, 8, CL), F32),
            vm((8, CL), F32),
            vm((40, CL), F32),
            vm((2, CHIPS, 40, CL), F32),
            vm((16, CL), F32),
            vm((2, 8, CL), F32),
            vm((GROUP, PART, HID), F32),
            vm((GROUP, PART, HID), F32),
            vm((PART, HID), F32),
            vm((4, PART, HID), F32),
            vm((PART, HID), F32),
            vm((4, PART, HID), F32),
            vm((GROUP, PART, HID), F32),
            dma((2,)),
            dma((2, 4)),
            dma((2, 4)),
            dma((2, 8)),
            dma((2, 8)),
            dma((2, 2)),
            dma((2, 4)),
            dma((2,)),
            dma((DEV,)),
            dma((2, CHIPS)),
            dma((2,)),
            dma((2, DEV)),
            dma((2,)),
            dma((16,)),
            dma((16,)),
            dma((4,)),
            dma((4,)),
            dma((4,)),
            dma((4,)),
            dma((16,)),
            dma((16,)),
        ],
        compiler_params=pltpu.CompilerParams(
            collective_id=0, has_side_effects=True, vmem_limit_bytes=56 * 1024 * 1024
        ),
    )(
        fine_counts,
        coarse_counts,
        fine_anchor,
        coarse_diffusion,
        b_out,
        fine_counts.reshape(1, DEV),
        w_in.T,
        b_in.reshape(1, HID),
        w_mid,
        b_mid.reshape(1, HID),
        w_out,
        coarse_state[0],
        fine_state[0],
        coarse_cot[0],
        fine_cot[0],
    )
    *states, g_w_in, g_b_in, g_w_mid, g_b_mid, g_w_out, g_b_out = pl.pallas_call(
        lambda p, i0, i1, i2, i3, o0, o1, o2, o3, *rest: finish(
            p, (i0, i1, i2, i3), (o0, o1, o2, o3), *rest
        ),
        out_shape=whole
        + tuple(
            jax.ShapeDtypeStruct(shape, F32)
            for shape in (
                (27 * NF, HID),
                (1, HID),
                (HID, HID),
                (1, HID),
                (NF, HID),
                (1, NF),
            )
        ),
        in_specs=[in_vmem] * 5,
        out_specs=(in_any,) * 4 + (in_vmem,) * 6,
        scratch_shapes=[dma((4,))],
    )(packed, *states)
    return (
        *(x[None] for x in states),
        g_w_in.T,
        g_b_in[0],
        g_w_mid,
        g_b_mid[0],
        g_w_out,
        g_b_out[0],
    )


def solution(mesh):
    state = P("dp", None, "patch", None)
    return jax.shard_map(
        on_device,
        mesh=mesh,
        in_specs=(state,) * 4 + (P(),) * 10,
        out_specs=(state,) * 4 + (P(),) * 6,
        check_vma=False,
    )
```

```python
import math

import jax
import jax.numpy as jnp
from jax import lax
from jax.experimental import pallas as pl
from jax.experimental.pallas import tpu as pltpu
from jax.sharding import PartitionSpec as P

MESH = pl.DeviceIdType.MESH
F32 = jnp.float32
BF16 = jnp.bfloat16

DEV = 64
CHIPS = 32
CW = 16
FW = 32
CL = CW * CW
FL = FW * FW
CR = 48
FR = 16
NF = 5
CHAIN = 2048
REGION = 384
TAKEN = 4
HALO = TAKEN + 1
EXT = FR + 2 * HALO
UNROLL = 4
FB_ROWS = 80
HID = 128
HB = 144
GROUP = 16
PART = 24
PACKED = GROUP * PART
GA_ROWS = 40


def dot(a, b):
    return jnp.dot(a, b, preferred_element_type=F32)


def dot_nt(a, b):
    return lax.dot_general(a, b, (((1,), (1,)), ((), ())), preferred_element_type=F32)


def dot_tn(a, b):
    return lax.dot_general(a, b, (((0,), (0,)), ((), ())), preferred_element_type=F32)


def grid(shape, dim):
    return lax.broadcasted_iota(jnp.int32, shape, dim)


def bits(mask):
    return mask.astype(F32).astype(BF16)


def pieces(b):
    hi = b.astype(BF16).astype(F32)
    mid = (b - hi).astype(BF16).astype(F32)
    zeros = jnp.zeros((13, b.shape[1]), F32)
    return jnp.concatenate([hi, mid, b - hi - mid, zeros], axis=0).astype(BF16)


def split(x):
    hi = x.astype(BF16)
    return hi, (x - hi.astype(F32)).astype(BF16)


def shift_x(v, step, width):
    lanes = v.shape[1]
    col = grid((v.shape[0], 128), 1) % width
    parts = []
    for i in range(lanes // 128):
        s = v[:, 128 * i : 128 * (i + 1)]
        if step == 1:
            parts.append(
                jnp.where(
                    col == width - 1, pltpu.roll(s, width - 1, 1), pltpu.roll(s, 127, 1)
                )
            )
        else:
            parts.append(
                jnp.where(col == 0, pltpu.roll(s, 129 - width, 1), pltpu.roll(s, 1, 1))
            )
    return jnp.concatenate(parts, axis=1)


def shift_y(v, step, width):
    lanes = v.shape[1]
    return pltpu.roll(v, lanes - width if step == 1 else width, 1)


def neighbours(v, width):
    return (
        shift_y(v, -1, width)
        + shift_y(v, 1, width)
        + shift_x(v, -1, width)
        + shift_x(v, 1, width)
    )


def kernel(
    fc_smem,
    cc_smem,
    anchor_smem,
    cd_smem,
    bo_smem,
    fcv,
    win_ref,
    bin_ref,
    wmid_ref,
    bmid_ref,
    wout_ref,
    cst_hbm,
    fst_hbm,
    cct_hbm,
    fct_hbm,
    coarse_out_hbm,
    fine_out_hbm,
    coarse_adj_hbm,
    fine_adj_hbm,
    p_out,
    cst,
    fst,
    cct,
    fct,
    coarse_out,
    fine_out,
    coarse_adj,
    fine_adj,
    w1,
    w2,
    w3,
    wp,
    w2t,
    w3t,
    pool,
    pool_t,
    sem_in,
    sem_out,
    base_s,
    v0,
    v1,
    v2,
    nb0,
    nb1,
    s0,
    s1,
    a1,
    a2,
    sl1,
    d1,
    d2,
    sbv,
    g2,
    g1,
    araw,
    gout,
    rim,
    p1,
    p2,
    p3,
    gsum,
    sendb,
    pairb,
    ga_a,
    ga_b,
    sum_a,
    sum_b,
    ga_a2,
    ga_b2,
    gh,
    gr,
    hs_dn,
    hs_up,
    hr_lo,
    hr_hi,
    cs_dn,
    cs_up,
    cr_lo,
    cr_hi,
    upd,
    back,
    rim_src,
    rim_got,
    rim_row_ref,
    rs,
    gath,
    rgs,
    rg,
    pk,
    r1,
    r1sum,
    r2,
    r2sum,
    rd,
    pall,
    sem_pair,
    sem_a1,
    sem_b1,
    sem_a2,
    sem_b2,
    sem_edge,
    sem_halo,
    sem_rim_s,
    sem_rim_r,
    sem_rs,
    sem_gp,
    sem_rg_s,
    sem_rg_r,
    sem_r1s,
    sem_r1r,
    sem_r2s,
    sem_r2r,
    sem_rds,
    sem_rdr,
    sem_r3s,
    sem_r3r,
):
    me = lax.axis_index("patch")
    dp = lax.axis_index("dp")
    core = lax.rem(me, 2)
    chip = me // 2
    partner = chip * 2 + (1 - core)
    nxt = lax.rem(me + 1, DEV)
    prv = lax.rem(me + DEV - 1, DEV)

    cx, czy = chip // 8, lax.rem(chip, 8)
    cy, cxz = lax.rem(chip, 4), chip // 4
    w = (lax.rem(cx, 2) * 2 + lax.rem(cxz, 2)) * 4 + lax.rem(cy, 2) * 2 + core
    xg = cx // 2 * 2 + cy // 2

    def member(g, k):
        x = g // 2 * 2 + k // 8
        y = lax.rem(g, 2) * 2 + lax.rem(k // 2, 2)
        return x * GROUP + lax.rem(k // 4, 2) * 8 + y * 2 + lax.rem(k, 2)

    arrivals = [
        pltpu.make_async_copy(src, dst, sem_in.at[i])
        for i, (src, dst) in enumerate(
            ((cst_hbm, cst), (fst_hbm, fst), (cct_hbm, cct), (fct_hbm, fct))
        )
    ]
    for copy in arrivals:
        copy.start()

    barrier = pltpu.get_barrier_semaphore()

    def greet(t, c):
        pl.semaphore_signal(
            barrier, inc=1, device_id={"patch": lax.rem(me + t, DEV)}, device_id_type=MESH
        )
        return c

    lax.fori_loop(1, DEV, greet, 0)

    def greet_dp(t, c):
        pl.semaphore_signal(
            barrier,
            inc=1,
            device_id={"patch": me, "dp": lax.rem(dp + t, 4)},
            device_id_type=MESH,
        )
        return c

    lax.fori_loop(1, 4, greet_dp, 0)

    col = grid((27 * NF, 3 * FB_ROWS), 1)
    row = grid((27 * NF, 3 * FB_ROWS), 0)
    part, field = col % FB_ROWS // 8, col % 8
    place = (col // FB_ROWS * 9 + part) * NF + field
    laid = dot_tn(win_ref[...], bits((row == place) & (part < 9) & (field < NF)))
    brow, bcol = grid((16, 3 * FB_ROWS), 0), grid((16, 3 * FB_ROWS), 1)
    bias = dot_tn(pieces(bin_ref[...]), bits((bcol == FB_ROWS + 72 + brow) & (brow < 3)))
    w1[...] = ((laid + bias) * 0.5).astype(BF16)
    qrow, qcol = grid((FB_ROWS, 27 * NF), 0), grid((FB_ROWS, 27 * NF), 1)
    wp[...] = jnp.zeros_like(wp)
    for a in range(3):
        take = (qcol == (a * 9 + qrow // 8) * NF + qrow % 8) & (qrow < 72) & (qrow % 8 < NF)
        turned = dot(bits(take), win_ref[...]).astype(BF16)
        for j in range(2):
            m = j + 2 - a
            wp[FB_ROWS * j : FB_ROWS * (j + 1), HID * m : HID * (m + 1)] = turned
    eye = bits(grid((HID, HID), 0) == grid((HID, HID), 1))
    eye16 = bits(grid((16, 16), 0) == grid((16, 16), 1))
    w2[:, 0:HID] = (wmid_ref[...].astype(F32) * 0.5).astype(BF16)
    w2[:, HID:HB] = (dot_tn(pieces(bmid_ref[...]), eye16) * 0.5).astype(BF16)
    w2t[...] = (dot_nt(eye, wmid_ref[...]) * 0.5).astype(BF16)
    w3[...] = dot(bits(grid((16, NF), 0) == grid((16, NF), 1)), wout_ref[...]).astype(BF16)
    w3t[...] = (dot_nt(eye, w3[...]) * 0.5).astype(BF16)
    fine_cell, coarse_cell = grid((FL, CL), 0), grid((FL, CL), 1)
    pool[...] = bits(fine_cell // (2 * FW) * CW + fine_cell % FW // 2 == coarse_cell)
    coarse_cell, fine_cell = grid((CL, FL), 0), grid((CL, FL), 1)
    pool_t[...] = bits(fine_cell // (2 * FW) * CW + fine_cell % FW // 2 == coarse_cell)
    field_row = grid((8, FL), 0)
    kf = jnp.zeros((8, FL), F32)
    half_bias = jnp.zeros((8, FL), F32)
    for f in range(NF):
        kf = jnp.where(field_row == f, 2.0 * cd_smem[f], kf)
        half_bias = jnp.where(field_row == f, 0.5 * bo_smem[f], half_bias)
    for copy in arrivals:
        copy.wait()

    anchor = anchor_smem[0]

    def count(d, carry):
        fs, cs = carry
        base_s[d] = fs
        fs = fs + fc_smem[d]
        cs = cs + jnp.where(d < me, cc_smem[d], 0)
        return (fs, cs)

    _, cpatch = lax.fori_loop(0, DEV, count, (jnp.int32(0), jnp.int32(0)))
    cstart = cpatch * CW
    nc = cc_smem[me] * CW
    n = fc_smem[me] * 8
    wide = n == FR
    first = me == 0
    last = me == DEV - 1

    def wrap(x):
        return lax.rem(x + 2 * CHAIN + CHAIN // 2, CHAIN) - CHAIN // 2

    def live_or_none(local):
        return jnp.where((local >= 0) & (local < nc), local, -10000)

    low_local = live_or_none(wrap(anchor - 1 - cstart))
    high_local = live_or_none(wrap(anchor + REGION - cstart))

    row48 = grid((CR, CL), 0)
    live48 = row48 < nc
    off48 = lax.rem(row48 + (cstart - anchor + 2 * CHAIN), CHAIN)
    in_region = (off48 < REGION) & live48

    for f in range(NF):
        hs_dn[f, 0:4, :] = fst[f, 0:4, :]
        hs_dn[f, 4:8, :] = fct[f, 0:4, :]
        hs_up[f, 0:4, :] = jnp.where(wide, fst[f, 12:16, :], fst[f, 4:8, :])
        hs_up[f, 4:8, :] = jnp.where(wide, fct[f, 12:16, :], fct[f, 4:8, :])
    cs_dn[...] = jnp.zeros_like(cs_dn)
    cs_up[...] = jnp.zeros_like(cs_up)
    for f in range(NF):
        kept = jnp.where(in_region, 0.0, cct[f])
        cs_dn[f : f + 1, :] = cst[f, 0:1, :]
        cs_dn[8 + f : 9 + f, :] = kept[0:1]
        cs_up[f : f + 1, :] = jnp.where(
            nc == 48,
            cst[f, 47:48, :],
            jnp.where(nc == 32, cst[f, 31:32, :], cst[f, 15:16, :]),
        )
        cs_up[8 + f : 9 + f, :] = jnp.where(
            nc == 48, kept[47:48], jnp.where(nc == 32, kept[31:32], kept[15:16])
        )

    def neighbour_copies():
        def one(src, dst, k, dev):
            return pltpu.make_async_remote_copy(
                src_ref=src,
                dst_ref=dst,
                send_sem=sem_halo.at[0, k],
                recv_sem=sem_halo.at[1, k],
                device_id={"patch": dev},
                device_id_type=MESH,
            )

        return (
            one(hs_up, hr_lo, 0, nxt),
            one(hs_dn, hr_hi, 1, prv),
            one(cs_up, cr_lo, 2, nxt),
            one(cs_dn, cr_hi, 3, prv),
        )

    cot = jnp.concatenate([jnp.where(live48, cct[f], 0.0) for f in range(NF)], axis=0)
    cot_hi, cot_lo = split(cot)
    cot2 = jnp.concatenate([cot_hi, cot_lo], axis=1)
    srow = grid((GA_ROWS, NF * CR), 0)
    scol = grid((GA_ROWS, NF * CR), 1)
    pick = jnp.where(
        scol // CR == srow % NF, scol % CR - srow // NF, 99999
    )

    def rows_for(c2):
        def one(i, c):
            hot = []
            for k in range(8):
                base = wrap(anchor + 4 * base_s[2 * (8 * i + k) + c2] - cstart)
                hot.append((pick == base).astype(F32))
            both = dot(jnp.concatenate(hot, axis=0).astype(BF16), cot2)
            both = both[:, :CL] + both[:, CL:]
            sendb[c2, i] = both.reshape(2, 4, GA_ROWS, CL)
            return c

        lax.fori_loop(0, CHIPS // 8, one, 0)

    ust = jnp.concatenate([cst[f] for f in range(NF)], axis=0)
    ust_hi, ust_lo = split(ust)
    ust2 = jnp.concatenate([ust_hi, ust_lo], axis=1)
    frow = grid((16, NF * CR), 0)
    fcol = grid((16, NF * CR), 1)
    fpick = jnp.where(fcol // CR == frow, fcol % CR, 99999)
    for e, local in ((0, low_local), (1, high_local)):
        both = dot(bits(fpick == local), ust2)
        rim_src[e] = (both[:, :CL] + both[:, CL:])[0:8]

    ones8 = jnp.ones((8, FL), F32)

    def build_features(s_ref, nb_ref, z, v):
        xm = shift_x(v, -1, FW)
        xp = shift_x(v, 1, FW)
        xs = jnp.concatenate([xm, v, xp], axis=0)
        ym = shift_y(xs, -1, FW)
        yp = shift_y(xs, 1, FW)
        s_ref[z] = jnp.concatenate([ym, xs, yp, ones8], axis=0).astype(BF16)
        nb_ref[z] = ym[8:16] + yp[8:16] + xm + xp - 6.0 * v

    for j in range(UNROLL):
        a1[j, HID:HB, :] = jnp.ones((HB - HID, FL), BF16)
    p1[...] = jnp.zeros_like(p1)
    p2[...] = jnp.zeros_like(p2)
    p3[...] = jnp.zeros_like(p3)
    gsum[...] = jnp.zeros_like(gsum)
    v0[...] = jnp.zeros_like(v0)
    g2[...] = jnp.zeros_like(g2)
    for z in (0, EXT - 1):
        s0[z] = jnp.zeros((FB_ROWS, FL), BF16)
        v1[z] = jnp.zeros((8, FL), F32)
    for z in range(EXT - 4, EXT):
        g1[z] = jnp.zeros((8, FL), F32)

    for src, dst in ((fst, v0), (fct, g2)):
        for f in range(NF):
            for i in range(FR):
                line = src[f, i : i + 1, :]
                dst[HALO + i, f : f + 1, :] = line if i < 8 else jnp.where(wide, line, 0.0)

    def features_first(k, c):
        for j in range(UNROLL):
            z = 1 + UNROLL * k + j
            build_features(s0, nb0, z, v0[z])
        return c

    rows_for(1 - core)

    pl.semaphore_wait(barrier, DEV - 1 + 3)

    halo_copies = neighbour_copies()
    for copy in halo_copies:
        copy.start()

    def rim_copy(e, sender):
        return pltpu.make_async_remote_copy(
            src_ref=rim_src.at[e],
            dst_ref=rim_got.at[sender],
            send_sem=sem_rim_s.at[e],
            recv_sem=sem_rim_r.at[sender],
            device_id={"patch": (DEV - 1) * e},
            device_id_type=MESH,
        )

    ends = ((0, 0), (1, DEV - 1))
    for e, who in ends:

        @pl.when(me != who)
        def _(e=e):
            rim_copy(e, me).start()

    pair_copy = pltpu.make_async_remote_copy(
        src_ref=sendb.at[1 - core],
        dst_ref=pairb,
        send_sem=sem_pair.at[0],
        recv_sem=sem_pair.at[1],
        device_id={"patch": partner},
        device_id_type=MESH,
    )
    pair_copy.start()
    rows_for(core)
    lax.fori_loop(1, 3, features_first, 0)

    pair_copy.wait()

    def add_pair(k, c):
        sendb[core, k] = sendb[core, k] + pairb[k]
        return c

    lax.fori_loop(0, 4, add_pair, 0)

    def chip_copy(src, dst, sems, t, to):
        return pltpu.make_async_remote_copy(
            src_ref=src,
            dst_ref=dst,
            send_sem=sems.at[0, t],
            recv_sem=sems.at[1, t],
            device_id={"patch": 2 * to + core},
            device_id_type=MESH,
        )

    def a1_copy(t):
        k = lax.rem(cy + t, 4)
        src = sendb.at[core, :, :, k, :, 0:128]
        return chip_copy(src, ga_a.at[cy], sem_a1, t, cxz * 4 + k)

    def b1_copy(t):
        k = lax.rem(cx + t, 4)
        src = sendb.at[core, k, :, :, :, 128:256]
        return chip_copy(src, ga_b.at[cx], sem_b1, t, k * 8 + czy)

    def a2_copy(t):
        k = lax.rem(cxz + t, 8)
        src = sum_a.at[k // 2, lax.rem(k, 2)]
        return chip_copy(src, ga_a2.at[cxz], sem_a2, t, k * 4 + cy)

    def b2_copy(t):
        k = lax.rem(czy + t, 8)
        src = sum_b.at[k // 4, lax.rem(k, 4)]
        return chip_copy(src, ga_b2.at[czy], sem_b2, t, cx * 8 + k)

    def run(make, what, count=16):
        def one(t, c):
            what(make(t))
            return c

        lax.fori_loop(1, count, one, 0)

    def begin(copy):
        copy.start()

    def end(copy):
        copy.wait()

    run(a1_copy, begin, 4)
    run(b1_copy, begin, 4)

    halo_copies[0].wait()
    halo_copies[1].wait()
    for at, dst in ((0, v0), (4, g2)):
        for f in range(NF):
            one = slice(f, f + 1)
            for i in range(TAKEN):
                hi = hr_hi[f, at + i : at + i + 1, :]
                dst[1 + i, one, :] = hr_lo[f, at + i : at + i + 1, :]
                dst[HALO + 8 + i, one, :] = jnp.where(wide, dst[HALO + 8 + i, one, :], hi)
                dst[HALO + 16 + i, one, :] = jnp.where(wide, hi, 0.0)

    rim_row_ref[...] = jnp.zeros_like(rim_row_ref)
    for e, who in ends:

        @pl.when(me != who)
        def _(e=e):
            rim_copy(e, me).wait_send()

        @pl.when(me == who)
        def _(e=e, who=who):
            rim_row_ref[...] = rim_src[e]

            def one(t, c):
                s = lax.rem(who + t, DEV)
                rim_copy(e, s).wait_recv()
                rim_row_ref[...] = rim_row_ref[...] + rim_got[s]
                return c

            lax.fori_loop(1, DEV, one, 0)

    rim_hi, rim_lo = split(rim_row_ref[...])
    beside = dot(rim_hi, pool_t[...]) + dot(rim_lo, pool_t[...])
    v0[HALO - 1] = jnp.where(first, beside, v0[HALO - 1])
    v0[HALO + 8] = jnp.where(last & ~wide, beside, v0[HALO + 8])
    v0[HALO + 16] = jnp.where(last & wide, beside, v0[HALO + 16])

    steps_all = (EXT - 2) // UNROLL
    lax.fori_loop(0, 1, features_first, 0)
    lax.fori_loop(3, steps_all, features_first, 0)

    def rim_row(z):
        return (first & (z < HALO)) | (last & (z >= HALO + n))

    def advance(z, v, nb, source):
        lap = v[z - 1] + v[z + 1] + nb[z]
        return v[z] + kf * lap + (0.5 * source[0:8] + half_bias)

    def features_of(s_ref, z):
        return s_ref[pl.ds(z - 1, 3)].reshape(3 * FB_ROWS, FL)

    def forward_rows(k, c):
        rows = [(j, 1 + UNROLL * k + j) for j in range(UNROLL)]
        for _, z in rows:
            before = jnp.maximum(z - UNROLL, 0)
            build_features(s1, nb1, before, v1[before])
        for j, z in rows:
            h = dot(w1[...], features_of(s0, z))
            a1[j, 0:HID, :] = (h + h * jnp.tanh(h)).astype(BF16)
        for j, z in rows:
            h = dot(w2[...], a1[j])
            a2[j] = (h + h * jnp.tanh(h)).astype(BF16)
        for j, z in rows:
            new = advance(z, v0, nb0, dot(w3[...], a2[j]))
            v1[z] = jnp.where(rim_row(z), v0[z], new)
        return c

    lax.fori_loop(0, 3, forward_rows, 0)

    ga_a[cy] = sendb[core, :, :, cy, :, 0:128]
    ga_b[cx] = sendb[core, cx, :, :, :, 128:256]
    run(a1_copy, end, 4)
    run(b1_copy, end, 4)
    sum_a[...] = ga_a[0] + ga_a[1] + ga_a[2] + ga_a[3]
    sum_b[...] = ga_b[0] + ga_b[1] + ga_b[2] + ga_b[3]
    run(a2_copy, begin, 8)
    run(b2_copy, begin, 8)

    lax.fori_loop(3, 5, forward_rows, 0)
    ga_a2[cxz] = sum_a[cxz // 2, lax.rem(cxz, 2)]
    ga_b2[czy] = sum_b[czy // 4, lax.rem(czy, 4)]
    run(a2_copy, end, 8)
    run(b2_copy, end, 8)
    parts = []
    for ref in (ga_a2, ga_b2):
        part = ref[0]
        for k in range(1, 8):
            part = part + ref[k]
        parts.append(part)
    region = jnp.concatenate(parts, axis=1)
    blank = jnp.zeros((3, CL), F32)
    gh[0] = jnp.concatenate([region[0:5], blank], axis=0)
    gh[1] = jnp.concatenate([jnp.where(wide, region[35:40], region[15:20]), blank], axis=0)

    def edge_copy(k, to):
        return pltpu.make_async_remote_copy(
            src_ref=gh.at[k],
            dst_ref=gr.at[k],
            send_sem=sem_edge.at[0, k],
            recv_sem=sem_edge.at[1, k],
            device_id={"patch": to},
            device_id_type=MESH,
        )

    edges = (edge_copy(0, prv), edge_copy(1, nxt))
    for copy in edges:
        copy.start()

    lax.fori_loop(5, steps_all, forward_rows, 0)
    for z in range(EXT - 1 - UNROLL, EXT - 1):
        build_features(s1, nb1, z, v1[z])

    def lift(x):
        hi, lo = split(x)
        return (dot(hi, pool_t[...]) + dot(lo, pool_t[...])) * 0.125

    lifted = lift(region)
    for r in range(8):
        for i in (HALO + 2 * r, HALO + 2 * r + 1):
            g2[i, 0:5, :] = g2[i, 0:5, :] + jnp.where(2 * r < n, lifted[5 * r : 5 * r + 5], 0.0)
    for copy in edges:
        copy.wait()
    lifted = lift(jnp.concatenate([gr[0], gr[1]], axis=0))
    for i in (HALO - 2, HALO - 1):
        g2[i] = g2[i] + lifted[8:16]
    for i in (HALO + 8, HALO + 9):
        g2[i] = g2[i] + jnp.where(wide, 0.0, lifted[0:8])
    for i in (HALO + 16, HALO + 17):
        g2[i] = g2[i] + jnp.where(wide, lifted[0:8], 0.0)

    def level_row(z):
        return ~(rim_row(z)) & (z < HALO + n + 2)

    def mask_g2(z, c):
        g2[z] = jnp.where(level_row(z) & (z >= HALO - 2), g2[z], 0.0)
        return c

    lax.fori_loop(0, EXT, mask_g2, 0)

    def backward_rows(zs, s_ref, g_ref, v_ref, nb_ref, with_source):
        rows = list(enumerate(zs))
        own = [(z >= HALO) & (z < HALO + n) for z in zs]
        for j, z in rows:
            half = 0.5 * g_ref[z]
            gsum[...] = gsum[...] + jnp.where(own[j], half, 0.0)
            sbv[j] = jnp.concatenate([half, jnp.zeros_like(half)], axis=0).astype(BF16)
        for j, z in rows:
            h = dot(w1[...], features_of(s_ref, z))
            t = jnp.tanh(h)
            u = h * t
            a1[j, 0:HID, :] = (h + u).astype(BF16)
            sl1[j] = (1.0 + t) * (1.0 + h - u)
        for j, z in rows:
            h = dot(w2[...], a1[j])
            t = jnp.tanh(h)
            u = h * t
            a2[j] = (h + u).astype(BF16)
            d2[j] = (dot(w3t[...], sbv[j]) * ((1.0 + t) * (1.0 + h - u))).astype(BF16)
        for j, z in rows:
            d1[z] = (dot(w2t[...], d2[j]) * sl1[j]).astype(BF16)
        for j, z in rows:
            p1[...] = p1[...] + jnp.where(own[j], dot_nt(features_of(s_ref, z), d1[z]), 0.0)
            p2[...] = p2[...] + jnp.where(own[j], dot_nt(a1[j], d2[j]), 0.0)
            p3[...] = p3[...] + jnp.where(own[j], dot_nt(sbv[j], a2[j]), 0.0)
            if with_source:
                v2[z] = advance(z, v_ref, nb_ref, dot(w3[...], a2[j]))

    def spread_rows(r0, g_ref, out_ref):
        both = dot(wp[...], d1[pl.ds(r0 - 1, 4)].reshape(4 * HID, FL))
        for j in range(2):
            r = r0 + j
            acc = both[FB_ROWS * j : FB_ROWS * (j + 1)]
            g = g_ref[r]
            kg = kf * g
            lo = jnp.concatenate([acc[0:8], acc[8:16] + kg, acc[16:24]], axis=0)
            mid = jnp.concatenate([acc[24:32] + kg, acc[32:40], acc[40:48] + kg], axis=0)
            hi = jnp.concatenate([acc[48:56], acc[56:64] + kg, acc[64:72]], axis=0)
            xs = shift_y(lo, 1, FW) + mid + shift_y(hi, -1, FW)
            moved = shift_x(xs[0:8], 1, FW) + xs[8:16] + shift_x(xs[16:24], -1, FW)
            a = g + kf * (g_ref[r - 1] + g_ref[r + 1] - 6.0 * g) + moved
            araw[r] = a
            inside = level_row(r) & (r >= HALO - 1) & (r < HALO + n + 1)
            out_ref[r] = jnp.where(inside, a, 0.0)

    start = HALO - 2
    steps = (FR + 4) // UNROLL

    def reverse(first_spread, s_ref, g_ref, out_ref, v_ref, nb_ref, with_source):
        def rows_at(z0):
            zs = [z0 + j for j in range(UNROLL)]
            backward_rows(zs, s_ref, g_ref, v_ref, nb_ref, with_source)

        def step(k, c):
            z0 = start + UNROLL * k
            for j in range(0, UNROLL, 2):
                spread_rows(z0 - UNROLL - 1 + j, g_ref, out_ref)
            rows_at(z0)
            return c

        first_spread()
        rows_at(start)
        lax.fori_loop(1, steps, step, 0)

    def last_spread(g_ref, out_ref):
        for j in range(0, UNROLL, 2):
            spread_rows(start + UNROLL * steps - UNROLL - 1 + j, g_ref, out_ref)

    def second_rest():
        last_spread(g2, g1)
        rim[0] = araw[HALO - 1]
        rim[1] = jnp.where(wide, araw[HALO + 16], araw[HALO + 8])

    reverse(lambda: None, s1, g2, g1, v1, nb1, True)

    pairs = jnp.concatenate(
        [v2[HALO + 2 * k] + v2[HALO + 2 * k + 1] for k in range(8)], axis=0
    )
    pairs_hi, pairs_lo = split(pairs)
    rest = (dot(pairs_hi, pool[...]) + dot(pairs_lo, pool[...])) * 0.125
    for k in range(8):
        for f in range(NF):
            rs[8 * f + k : 8 * f + k + 1, :] = rest[8 * k + f : 8 * k + f + 1]

    def rs_copy(t):
        return pltpu.make_async_remote_copy(
            src_ref=rs,
            dst_ref=gath.at[core, chip],
            send_sem=sem_rs.at[0, t],
            recv_sem=sem_rs.at[1, t],
            device_id={"patch": 2 * lax.rem(chip + t, CHIPS) + core},
            device_id_type=MESH,
        )

    def start_rs(t, c):
        rs_copy(t).start()
        return c

    lax.fori_loop(1, CHIPS, start_rs, 0)
    gath[core, chip] = rs[...]

    def r1_copy(t):
        k = lax.rem(w + t, GROUP)
        return pltpu.make_async_remote_copy(
            src_ref=pk.at[k],
            dst_ref=r1.at[w],
            send_sem=sem_r1s.at[t],
            recv_sem=sem_r1r.at[t],
            device_id={"patch": member(xg, k)},
            device_id_type=MESH,
        )

    def r2_copy(t):
        return pltpu.make_async_remote_copy(
            src_ref=r1sum,
            dst_ref=r2.at[xg],
            send_sem=sem_r2s.at[t],
            recv_sem=sem_r2r.at[t],
            device_id={"patch": member(lax.rem(xg + t, 4), w)},
            device_id_type=MESH,
        )

    def rd_copy(t):
        return pltpu.make_async_remote_copy(
            src_ref=r2sum,
            dst_ref=rd.at[dp],
            send_sem=sem_rds.at[t],
            recv_sem=sem_rdr.at[t],
            device_id={"patch": me, "dp": lax.rem(dp + t, 4)},
            device_id_type=MESH,
        )

    def r3_copy(t):
        k = lax.rem(w + t, GROUP)
        return pltpu.make_async_remote_copy(
            src_ref=pall.at[w],
            dst_ref=pall.at[w],
            send_sem=sem_r3s.at[t],
            recv_sem=sem_r3r.at[t],
            device_id={"patch": member(xg, k)},
            device_id_type=MESH,
        )

    def send_parts():
        total = jnp.sum(gsum[...], axis=1, keepdims=True)
        tiles = [(p1, 8 * i) for i in range(9)]
        tiles += [(p1, FB_ROWS + 8 * i) for i in range(10)]
        tiles += [(p1, 2 * FB_ROWS + 8 * i) for i in range(9)]
        tiles += [(p2, 8 * i) for i in range(17)]
        tiles += [(p3, 0)]
        for i, (ref, at) in enumerate(tiles):
            pk[i // 3, 8 * (i % 3) : 8 * (i % 3) + 8, :] = ref[at : at + 8, :]
        pk[15, 8:16, :] = jnp.broadcast_to(total, (8, HID))
        pk[15, 16:24, :] = jnp.zeros((8, HID), F32)
        run(r1_copy, begin)

    reverse(second_rest, s0, g1, gout, v0, nb0, False)
    send_parts()
    last_spread(g1, gout)

    rim[0] = rim[0] + araw[HALO - 1]
    rim[1] = rim[1] + jnp.where(wide, araw[HALO + 16], araw[HALO + 8])
    rims = jnp.concatenate([rim[0], rim[1]], axis=0)
    rims_hi, rims_lo = split(rims)
    rims = dot(rims_hi, pool[...]) + dot(rims_lo, pool[...])
    rgs[...] = rims

    def rg_copy(e, dev, t):
        return pltpu.make_async_remote_copy(
            src_ref=rgs.at[pl.ds(8 * e, 8)],
            dst_ref=rg.at[e],
            send_sem=sem_rg_s.at[e, t],
            recv_sem=sem_rg_r.at[e],
            device_id={"patch": dev},
            device_id_type=MESH,
        )

    for e, who in ends:

        @pl.when(me == who)
        def _(e=e, who=who):
            def one(t, c):
                rg_copy(e, lax.rem(who + t, DEV), t).start()
                return c

            lax.fori_loop(1, DEV, one, 0)
            rg[e] = rgs[8 * e : 8 * e + 8, :]

    halo_copies[2].wait()
    halo_copies[3].wait()
    for f in range(NF):
        kappa = cd_smem[f]
        for src, lo, hi, dst in (
            (jnp.where(live48, cst[f], 0.0), cr_lo[f : f + 1], cr_hi[f : f + 1], upd),
            (
                jnp.where(in_region | ~live48, 0.0, cct[f]),
                cr_lo[8 + f : 9 + f],
                cr_hi[8 + f : 9 + f],
                back,
            ),
        ):
            below = jnp.where(row48 == 0, lo, pltpu.roll(src, 1, 0))
            above = jnp.where(row48 == nc - 1, hi, pltpu.roll(src, CR - 1, 0))
            new = src + kappa * (below + above + neighbours(src, CW) - 6.0 * src)
            dst[f] = jnp.where(live48, new, 0.0)

    r1[w] = pk[w]
    run(r1_copy, end)

    def add_up(ref, count):
        out = ref[0]
        for k in range(1, count):
            out = out + ref[k]
        return out

    r1sum[...] = add_up(r1, GROUP)
    run(r2_copy, begin, 4)

    def wait_rs(t, c):
        rs_copy(t).wait()
        return c

    lax.fori_loop(1, CHIPS, wait_rs, 0)
    gp_copy = pltpu.make_async_remote_copy(
        src_ref=gath.at[core],
        dst_ref=gath.at[core],
        send_sem=sem_gp.at[0],
        recv_sem=sem_gp.at[1],
        device_id={"patch": partner},
        device_id_type=MESH,
    )
    gp_copy.start()

    r2[xg] = r1sum[...]
    run(r2_copy, end, 4)
    r2sum[...] = add_up(r2, 4)
    run(rd_copy, begin, 4)

    for i in range(FR):
        keep = (i < n)
        a = jnp.where(keep, v2[HALO + i], 0.0)
        b = jnp.where(keep, gout[HALO + i], 0.0)
        for f in range(NF):
            fine_out[f, i : i + 1, :] = a[f : f + 1]
            fine_adj[f, i : i + 1, :] = b[f : f + 1]
    departures = [
        pltpu.make_async_copy(src, dst, sem_out.at[i])
        for i, (src, dst) in enumerate(
            (
                (fine_out, fine_out_hbm),
                (fine_adj, fine_adj_hbm),
                (coarse_out, coarse_out_hbm),
                (coarse_adj, coarse_adj_hbm),
            )
        )
    ]
    departures[0].start()
    departures[1].start()

    rd[dp] = r2sum[...]
    run(rd_copy, end, 4)
    pall[w] = add_up(rd, 4)
    run(r3_copy, begin)

    qi = grid((DEV, 512), 0)
    qc = grid((DEV, 512), 1)
    qd = 2 * ((qc % 256) // 8) + qc // 256
    counts = jnp.broadcast_to(fcv[...].astype(F32), (16, DEV)).astype(BF16)
    starts = dot(counts, (qi < qd).astype(F32).astype(BF16))
    sizes = dot(counts, (qi == qd).astype(F32).astype(BF16))
    qr = (grid((16, 512), 1) % 8).astype(F32)
    place = jnp.where(qr < 4.0 * sizes, 4.0 * starts + qr, -1.0)[0:1]
    off = off48[:, 0:1].astype(F32)
    onehot = (off == place).astype(F32).astype(BF16)

    gp_copy.wait()
    for f in range(NF):
        rows = gath[:, :, 8 * f : 8 * f + 8, :].reshape(512, CL)
        rows_hi, rows_lo = split(rows)
        pulled = dot(onehot, rows_hi) + dot(onehot, rows_lo)
        coarse_out[f] = jnp.where(in_region, pulled, upd[f])
    departures[2].start()

    for e, who in ends:

        @pl.when(me != who)
        def _(e=e):
            rg_copy(e, partner, 0).wait_recv()

        @pl.when(me == who)
        def _(e=e, who=who):
            def one(t, c):
                rg_copy(e, lax.rem(who + t, DEV), t).wait_send()
                return c

            lax.fori_loop(1, DEV, one, 0)

    for f in range(NF):
        coarse_adj[f] = (
            back[f]
            + jnp.where(row48 == low_local, rg[0, f : f + 1, :], 0.0)
            + jnp.where(row48 == high_local, rg[1, f : f + 1, :], 0.0)
        )

    departures[3].start()

    run(r3_copy, end)
    p_out[...] = pall[...]
    for copy in departures:
        copy.wait()


def finish(packed, ins, outs, w_in, b_in, w_mid, b_mid, w_out, b_out, sems):
    copies = [
        pltpu.make_async_copy(src, dst, sems.at[i])
        for i, (src, dst) in enumerate(zip(ins, outs))
    ]
    for copy in copies:
        copy.start()
    x = packed[...].reshape(PACKED, HID) * (1.0 / math.sqrt(4 * 96 * 8 * FL))
    hi = x.astype(BF16)
    rest = x - hi.astype(F32)
    mid = rest.astype(BF16)
    lo = (rest - mid.astype(F32)).astype(BF16)
    j = grid((27 * NF, 224), 0)
    at = j // NF * 8 + j % NF + jnp.where(j >= 18 * NF, 8, 0)
    take = bits(grid((27 * NF, 224), 1) == at)
    eye = bits(grid((HID, HID), 0) == grid((HID, HID), 1))

    def pull(product, a, b):
        return product(hi[a:b]) + product(mid[a:b]) + product(lo[a:b])

    w_in[...] = pull(lambda y: dot(take, y), 0, 224)
    w_mid[...] = pull(lambda y: dot_tn(y, eye), 224, 224 + HID)
    b_in[...] = x[144:145]
    b_mid[...] = x[352:353]
    w_out[...] = x[360:365]
    on = grid((8, HID), 0) == grid((8, HID), 1)
    b_out[...] = jnp.sum(jnp.where(on, x[368:376], 0.0), axis=0, keepdims=True)[:, 0:NF]
    for copy in copies:
        copy.wait()


def on_device(
    coarse_state,
    fine_state,
    coarse_cot,
    fine_cot,
    coarse_diffusion,
    w_in,
    b_in,
    w_mid,
    b_mid,
    w_out,
    b_out,
    coarse_counts,
    fine_counts,
    fine_anchor,
):
    vm = pltpu.VMEM
    slab = vm((EXT, 8, FL), F32)
    dma = pltpu.SemaphoreType.DMA
    in_vmem = pl.BlockSpec(memory_space=pltpu.VMEM)
    in_smem = pl.BlockSpec(memory_space=pltpu.SMEM)
    in_any = pl.BlockSpec(memory_space=pl.ANY)
    coarse_shape = jax.ShapeDtypeStruct((NF, CR, CL), F32)
    fine_shape = jax.ShapeDtypeStruct((NF, FR, FL), F32)
    whole = (coarse_shape, fine_shape, coarse_shape, fine_shape)
    big = [vm(x.shape, F32) for x in whole]
    *states, packed = pl.pallas_call(
        kernel,
        out_shape=whole + (jax.ShapeDtypeStruct((GROUP, PART, HID), F32),),
        in_specs=[in_smem] * 5 + [in_vmem] * 6 + [in_any] * 4,
        out_specs=(in_any,) * 4 + (in_vmem,),
        scratch_shapes=[
            *big,
            *big,
            vm((HID, 3 * FB_ROWS), BF16),
            vm((HID, HB), BF16),
            vm((16, HID), BF16),
            vm((2 * FB_ROWS, 4 * HID), BF16),
            vm((HID, HID), BF16),
            vm((HID, 16), BF16),
            vm((FL, CL), BF16),
            vm((CL, FL), BF16),
            dma((4,)),
            dma((4,)),
            pltpu.SMEM((DEV,), jnp.int32),
            slab,
            slab,
            slab,
            slab,
            slab,
            vm((EXT, FB_ROWS, FL), BF16),
            vm((EXT, FB_ROWS, FL), BF16),
            vm((UNROLL, HB, FL), BF16),
            vm((UNROLL, HID, FL), BF16),
            vm((UNROLL, HID, FL), F32),
            vm((EXT, HID, FL), BF16),
            vm((UNROLL, HID, FL), BF16),
            vm((UNROLL, 16, FL), BF16),
            slab,
            slab,
            slab,
            slab,
            vm((2, 8, FL), F32),
            vm((3 * FB_ROWS, HID), F32),
            vm((HB, HID), F32),
            vm((16, HID), F32),
            vm((8, FL), F32),
            vm((2, 4, 2, 4, GA_ROWS, CL), F32),
            vm((4, 2, 4, GA_ROWS, CL), F32),
            vm((4, 4, 2, GA_ROWS, 128), F32),
            vm((4, 2, 4, GA_ROWS, 128), F32),
            vm((4, 2, GA_ROWS, 128), F32),
            vm((2, 4, GA_ROWS, 128), F32),
            vm((8, GA_ROWS, 128), F32),
            vm((8, GA_ROWS, 128), F32),
            vm((2, 8, CL), F32),
            vm((2, 8, CL), F32),
            vm((NF, 8, FL), F32),
            vm((NF, 8, FL), F32),
            vm((NF, 8, FL), F32),
            vm((NF, 8, FL), F32),
            vm((16, CL), F32),
            vm((16, CL), F32),
            vm((16, CL), F32),
            vm((16, CL), F32),
            vm((NF, CR, CL), F32),
            vm((NF, CR, CL), F32),
            vm((2, 8, CL), F32),
            vm((DEV, 8, CL), F32),
            vm((8, CL), F32),
            vm((40, CL), F32),
            vm((2, CHIPS, 40, CL), F32),
            vm((16, CL), F32),
            vm((2, 8, CL), F32),
            vm((GROUP, PART, HID), F32),
            vm((GROUP, PART, HID), F32),
            vm((PART, HID), F32),
            vm((4, PART, HID), F32),
            vm((PART, HID), F32),
            vm((4, PART, HID), F32),
            vm((GROUP, PART, HID), F32),
            dma((2,)),
            dma((2, 4)),
            dma((2, 4)),
            dma((2, 8)),
            dma((2, 8)),
            dma((2, 2)),
            dma((2, 4)),
            dma((2,)),
            dma((DEV,)),
            dma((2, CHIPS)),
            dma((2,)),
            dma((2, DEV)),
            dma((2,)),
            dma((16,)),
            dma((16,)),
            dma((4,)),
            dma((4,)),
            dma((4,)),
            dma((4,)),
            dma((16,)),
            dma((16,)),
        ],
        compiler_params=pltpu.CompilerParams(
            collective_id=0, has_side_effects=True, vmem_limit_bytes=56 * 1024 * 1024
        ),
    )(
        fine_counts,
        coarse_counts,
        fine_anchor,
        coarse_diffusion,
        b_out,
        fine_counts.reshape(1, DEV),
        w_in.T,
        b_in.reshape(1, HID),
        w_mid,
        b_mid.reshape(1, HID),
        w_out,
        coarse_state[0],
        fine_state[0],
        coarse_cot[0],
        fine_cot[0],
    )
    *states, g_w_in, g_b_in, g_w_mid, g_b_mid, g_w_out, g_b_out = pl.pallas_call(
        lambda p, i0, i1, i2, i3, o0, o1, o2, o3, *rest: finish(
            p, (i0, i1, i2, i3), (o0, o1, o2, o3), *rest
        ),
        out_shape=whole
        + tuple(
            jax.ShapeDtypeStruct(shape, F32)
            for shape in (
                (27 * NF, HID),
                (1, HID),
                (HID, HID),
                (1, HID),
                (NF, HID),
                (1, NF),
            )
        ),
        in_specs=[in_vmem] * 5,
        out_specs=(in_any,) * 4 + (in_vmem,) * 6,
        scratch_shapes=[dma((4,))],
    )(packed, *states)
    return (
        *(x[None] for x in states),
        g_w_in.T,
        g_b_in[0],
        g_w_mid,
        g_b_mid[0],
        g_w_out,
        g_b_out[0],
    )


def solution(mesh):
    state = P("dp", None, "patch", None)
    return jax.shard_map(
        on_device,
        mesh=mesh,
        in_specs=(state,) * 4 + (P(),) * 10,
        out_specs=(state,) * 4 + (P(),) * 6,
        check_vma=False,
    )
```
